32 devices in a mesh: orb: 4 (over x, core), sx: 2 (over y), sy: 4 (over z).
Axes of the slice: x: 2, y: 2, z: 4, core: 2. Of those that a mesh axis runs over, the one named last changes fastest.
Arguments:
- orbitals: bfloat16 [16, 32, 8192], P('sx', 'sy', 'orb'), may hold values from -6 to 6
- src_owner: int32 [2, 2], replicated, may hold values from 0 to 3
- src_slot: int32 [2, 2], replicated, may hold values from 0 to 63
Outputs:
- exchange_field: float32 [16, 32, 8192], P('sx', 'sy', 'orb')
The draws below stay inside these ranges and needn't reach their ends.
All inputs are finite; a program needn't handle non-finite values.
Results may differ from the reference program's by a relative error of at most 0.0003.
Values may be sent and summed in bfloat16 or wider, within the bound.
No kernel may reach another device: no remote copies, remote signals or barrier semaphores. Data moves between devices by JAX's collectives and lax.ppermute only.
A program may use at most 128 MiB of HBM per device.

```python
import jax
import jax.numpy as jnp
from jax import lax

NZ = 32
TGT = 64
SRC = 2
ROUNDS = 2
DEGREE = 4
NX = 16
NY = 32
NORB = 256
N_ORB = 4


def draw_orbitals(key, part):
    key_base = jax.random.fold_in(key, 0)
    array_shape = (NX, NY, NORB * NZ)
    values = jnp.clip(jax.random.normal(key_base, array_shape, jnp.float32), -6.0, 6.0)
    return values.astype(jnp.bfloat16)


def place_ends(result, rng, low, top_value):
    place = [jax.random.randint(jax.random.fold_in(rng, axis), (), 0, length) for axis, length in enumerate(result.shape)]
    main_axis = result.shape.index(max(result.shape))
    beside = place[:main_axis] + [(place[main_axis] + 1) % result.shape[main_axis]] + place[main_axis + 1:]
    return result.at[tuple(place)].set(low).at[tuple(beside)].set(top_value)


def setup_inputs(seed: int = 0) -> dict:
    keys = jax.random.split(jax.random.key(seed), 4)
    return {
        "orbitals": draw_orbitals(jax.random.fold_in(keys[3], 71), 0),
        "src_owner": place_ends(jax.random.randint(keys[1], (ROUNDS, SRC), 0, N_ORB), jax.random.fold_in(keys[1], 1), 0, N_ORB - 1).astype(jnp.int32),
        "src_slot": place_ends(jax.random.randint(keys[2], (ROUNDS, SRC), 0, TGT), jax.random.fold_in(keys[2], 1), 0, TGT - 1).astype(jnp.int32),
    }


cheb_coeffs = (1.021021021021021, -1.7357357357357357, 1.4753753753753754, -1.2540690690690691, 1.0659587087087087)


def screened(field):
    side = jnp.roll(field, -1, 1) + jnp.roll(field, 1, 1)
    side = side + jnp.roll(field, -1, 2) + jnp.roll(field, 1, 2)
    padded = jnp.pad(field, ((0, 0), (0, 0), (0, 0), (1, 1)))
    side = side + padded[..., 2:] + padded[..., :-2]
    return -side / 6.0


def potential(density):
    t_prev = density
    t_cur = screened(density)
    total = cheb_coeffs[0] * t_prev + cheb_coeffs[1] * t_cur
    for order in range(2, DEGREE + 1):
        t_next = 2.0 * screened(t_cur) - t_prev
        total = total + cheb_coeffs[order] * t_next
        t_prev, t_cur = t_cur, t_next
    return total


def reference(orbitals, src_owner, src_slot):
    grid = orbitals.astype(jnp.float32).reshape(NX, NY, NORB, NZ).transpose(2, 0, 1, 3)
    picked = (src_owner * TGT + src_slot).reshape(-1).astype(jnp.int32)
    sources = grid[picked]

    def one_target(target):
        density = sources * target[None]
        return -jnp.sum(potential(density) * sources, axis=0)

    fields = lax.map(one_target, grid)
    return fields.transpose(1, 2, 0, 3).reshape(NX, NY, NORB * NZ)
```

```python
import functools

import jax
import jax.numpy as jnp
from jax import lax
from jax.experimental import pallas as pl
from jax.experimental.pallas import tpu as pltpu
from jax.sharding import PartitionSpec as P

NZ = 32
LANES = 128
SUB = 8
DEGREE = 4
HALO = DEGREE
EDGE = 8

CHEB = (
    1.021021021021021,
    -1.7357357357357357,
    1.4753753753753753,
    -1.254069069069069,
    1.0659587087087088,
)


def power_coeffs():
    c0, c1, c2, c3, c4 = CHEB
    return (
        c0 - c2 + c4,
        -(c1 - 3.0 * c3) / 6.0,
        (2.0 * c2 - 8.0 * c4) / 36.0,
        -4.0 * c3 / 216.0,
        8.0 * c4 / 1296.0,
    )


CORNER_LOW = ((0, 5, 3), (1, 6, 2), (2, 7, 1), (5, 7, 1), (6, 6, 2), (7, 5, 3))
CORNER_HIGH = tuple((row, 0, count) for row, _, count in CORNER_LOW)


def ring(axis, step):
    count = lax.axis_size(axis)
    return [(i, (i + step) % count) for i in range(count)]


def diagonal(step_x, step_y):
    count_x, count_y = lax.axis_size("sx"), lax.axis_size("sy")
    return [
        (i * count_y + j, (i + step_x) % count_x * count_y + (j + step_y) % count_y)
        for i in range(count_x)
        for j in range(count_y)
    ]


def pack(block, corners):
    return jnp.concatenate(
        [block[row, first : first + count] for row, first, count in corners], axis=0
    )


def halos(block):
    last, first = block[:, EDGE - HALO :], block[:, :HALO]
    if lax.axis_size("sx") == 2:
        across = lax.ppermute(block, "sx", ring("sx", 1))
    else:
        across = jnp.concatenate(
            [
                lax.ppermute(block[:HALO], "sx", ring("sx", -1)),
                lax.ppermute(block[EDGE - HALO :], "sx", ring("sx", 1)),
            ],
            axis=0,
        )
    below = lax.ppermute(last, "sy", ring("sy", 1))
    above = lax.ppermute(first, "sy", ring("sy", -1))
    both = ("sx", "sy")
    corners = []
    for cells, step_y in ((CORNER_LOW, 1), (CORNER_HIGH, -1)):
        if lax.axis_size("sx") == 2:
            corners.append(lax.ppermute(pack(block, cells), both, diagonal(1, step_y)))
        else:
            corners.append(
                jnp.concatenate(
                    [
                        lax.ppermute(pack(block, cells[:3]), both, diagonal(-1, step_y)),
                        lax.ppermute(pack(block, cells[3:]), both, diagonal(1, step_y)),
                    ],
                    axis=0,
                )
            )
    return block, across, below, above, corners[0], corners[1]


def candidates(orbitals, src_slot):
    slots = src_slot.reshape(-1)
    return jnp.concatenate(
        [lax.dynamic_slice_in_dim(orbitals, slots[i] * NZ, NZ, 2) for i in range(slots.shape[0])],
        axis=2,
    )


def pick_sources(mine, src_owner):
    count = lax.axis_size("orb")
    owner = jnp.repeat(src_owner.reshape(-1), NZ)
    me = lax.axis_index("orb")
    picked = mine
    for step in range(1, count):
        theirs = lax.ppermute(mine, "orb", ring("orb", step))
        picked = jnp.where(owner == (me + count - step) % count, theirs, picked)
    return picked


def fill(dst, own, across, below, above, corner_low, corner_high, groups):
    size = 2 * HALO + EDGE

    def put(x, y, rows, group, values):
        start = y * groups + group
        if groups == 1:
            dst[x, pl.ds(start, rows), :] = values
        else:
            dst[x, pl.ds(start, rows, stride=groups), :] = values

    def one(group):
        lanes = pl.ds(group * LANES, LANES)
        for row in range(EDGE):
            put(HALO + row, HALO, EDGE, group, own[row, :, lanes].astype(jnp.float32))
            outer = row - EDGE if row >= HALO else row + EDGE
            put(HALO + outer, HALO, EDGE, group, across[row, :, lanes].astype(jnp.float32))
            put(HALO + row, 0, HALO, group, below[row, :, lanes].astype(jnp.float32))
            put(HALO + row, HALO + EDGE, HALO, group, above[row, :, lanes].astype(jnp.float32))
        for ref, cells, shift in (
            (corner_low, CORNER_LOW, HALO - EDGE),
            (corner_high, CORNER_HIGH, HALO + EDGE),
        ):
            values = ref[:, lanes].astype(jnp.float32)
            at = 0
            for row, first, count in cells:
                outer = row - EDGE if row >= HALO else row + EDGE
                put(HALO + outer, first + shift, count, group, values[at : at + count])
                at += count

    for group in range(groups):
        one(group)


def reach(x, y):
    out_x = max(HALO - x, x - (HALO + EDGE - 1), 0)
    out_y = max(HALO - y, y - (HALO + EDGE - 1), 0)
    return out_x + out_y


def kernel(count, *refs):
    block, source = refs[0:6], refs[6:12]
    out, cells, src_rows, src, dens, work_a, work_b, acc = refs[12:]
    groups = block[0].shape[2] // LANES
    size = 2 * HALO + EDGE
    p0, p1, p2, p3, p4 = power_coeffs()
    tail = (p3 / p4, p2 / p4, p1 / p4, p0 / p4)

    fill(src_rows, *source, 1)
    lane = lax.broadcasted_iota(jnp.int32, (SUB, LANES), 1)
    for x in range(size):
        for y in range(0, size, SUB):
            rows = src_rows[x, pl.ds(y, SUB), :]
            for place in range(count):
                one = jnp.where(lane // NZ == place, rows, 0.0)
                one = one + pltpu.roll(one, NZ, 1)
                src[place, x, pl.ds(y, SUB), :] = one + pltpu.roll(one, 2 * NZ, 1)
    fill(cells, *block, groups)

    inner = lane % NZ
    not_first, not_last = inner != 0, inner != NZ - 1

    def z_sum(v):
        lower = jnp.where(not_first, pltpu.roll(v, 1, 1), 0.0)
        upper = jnp.where(not_last, pltpu.roll(v, LANES - 1, 1), 0.0)
        return lower + upper

    spots = [
        [(x, y) for x in range(size) for y in range(size) if reach(x, y) <= radius]
        for radius in range(HALO + 1)
    ]

    def one_pass(index, carry):
        place, half = index // (groups // SUB), index % (groups // SUB)
        base = half * SUB

        def spread(x, y):
            row = src[place, x, pl.ds(y, 1), :]
            return jnp.broadcast_to(row, (SUB, LANES))

        for x, y in spots[HALO]:
            value = cells[x, pl.ds(pl.multiple_of(y * groups + base, SUB), SUB), :]
            dens[x, y] = value * spread(x, y)
        old = dens
        for step in range(DEGREE):
            new = (work_a, work_b, work_a, None)[step]
            radius = HALO - 1 - step
            targets = set(spots[radius])
            pair_prev = {}
            for x in range(size):
                pair = {}
                for y in range(size):
                    if (x, y) in targets or (x + 1, y + 1) in targets:
                        pair[y] = old[x + 1, y] + old[x, y + 1]
                for y in range(size):
                    if (x, y) not in targets:
                        continue
                    total = pair[y] + pair_prev[y - 1]
                    total = total + z_sum(old[x, y])
                    total = total + tail[step] * dens[x, y]
                    if new is not None:
                        new[x, y] = total
                    else:
                        total = total * spread(x, y)
                        at = pl.multiple_of((y - HALO) * groups + base, SUB)
                        row = acc.at[x - HALO, pl.ds(at, SUB), :]
                        row[...] = row[...] + total
                pair_prev = pair
            old = new
        return carry

    acc[...] = jnp.zeros(acc.shape, jnp.float32)
    lax.fori_loop(0, count * (groups // SUB), one_pass, 0)
    for x in range(EDGE):
        for group in range(groups):
            tile = acc[x, pl.ds(group, EDGE, stride=groups), :]
            out[x, :, pl.ds(group * LANES, LANES)] = tile * (-p4)


def fields(block, source, count):
    rows_x, rows_y, width = block[0].shape
    groups = width // LANES
    size = 2 * HALO + EDGE
    vmem = pl.BlockSpec(memory_space=pltpu.VMEM)
    plane = pltpu.VMEM((size, size, SUB, LANES), jnp.float32)
    return pl.pallas_call(
        functools.partial(kernel, count),
        out_shape=jax.ShapeDtypeStruct((rows_x, rows_y, width), jnp.float32),
        in_specs=[vmem] * 12,
        out_specs=vmem,
        scratch_shapes=[
            pltpu.VMEM((size, size * groups, LANES), jnp.float32),
            pltpu.VMEM((size, size, LANES), jnp.float32),
            pltpu.VMEM((count, size, size, LANES), jnp.float32),
            plane,
            plane,
            plane,
            pltpu.VMEM((rows_x, rows_y * groups, LANES), jnp.float32),
        ],
        compiler_params=pltpu.CompilerParams(vmem_limit_bytes=40 * 2**20),
        name="fields",
    )(*block, *source)


def body(orbitals, src_owner, src_slot):
    mine = candidates(orbitals, src_slot)
    block = halos(orbitals)
    source = halos(pick_sources(mine, src_owner))
    return fields(block, source, src_slot.size)


def solution(mesh):
    in_specs = (P("sx", "sy", "orb"), P(), P())
    out_specs = P("sx", "sy", "orb")
    return jax.shard_map(body, mesh=mesh, in_specs=in_specs, out_specs=out_specs, check_vma=False)
```

```python
import functools

import jax
import jax.numpy as jnp
from jax import lax
from jax.experimental import pallas as pl
from jax.experimental.pallas import tpu as pltpu
from jax.sharding import PartitionSpec as P

NZ = 32
LANES = 128
SUB = 8
DEGREE = 4
HALO = DEGREE
EDGE = 8

CHEB = (
    1.021021021021021,
    -1.7357357357357357,
    1.4753753753753753,
    -1.254069069069069,
    1.0659587087087088,
)


def power_coeffs():
    c0, c1, c2, c3, c4 = CHEB
    return (
        c0 - c2 + c4,
        -(c1 - 3.0 * c3) / 6.0,
        (2.0 * c2 - 8.0 * c4) / 36.0,
        -4.0 * c3 / 216.0,
        8.0 * c4 / 1296.0,
    )


CORNER_LOW = ((0, 5, 3), (1, 6, 2), (2, 7, 1), (5, 7, 1), (6, 6, 2), (7, 5, 3))
CORNER_HIGH = tuple((row, 0, count) for row, _, count in CORNER_LOW)


def ring(axis, step):
    count = lax.axis_size(axis)
    return [(i, (i + step) % count) for i in range(count)]


def diagonal(step_x, step_y):
    count_x, count_y = lax.axis_size("sx"), lax.axis_size("sy")
    return [
        (i * count_y + j, (i + step_x) % count_x * count_y + (j + step_y) % count_y)
        for i in range(count_x)
        for j in range(count_y)
    ]


def candidates_kernel(slots, orbitals, out):
    lane = lax.broadcasted_iota(jnp.int32, (EDGE, LANES), 1)
    per_tile = LANES // NZ
    rounds, places = slots.shape
    for row in range(EDGE):
        packed = jnp.zeros((EDGE, LANES), jnp.float32)
        for index in range(rounds * places):
            slot = slots[index // places, index % places]
            first = pl.multiple_of(slot // per_tile * LANES, LANES)
            tile = orbitals[row, :, pl.ds(first, LANES)].astype(jnp.float32)
            shift = (index - slot % per_tile + per_tile) % per_tile * NZ
            packed = jnp.where(lane // NZ == index, pltpu.roll(tile, shift, 1), packed)
        out[row] = packed.astype(jnp.bfloat16)


def candidates(orbitals, src_slot):
    vmem = pl.BlockSpec(memory_space=pltpu.VMEM)
    return pl.pallas_call(
        candidates_kernel,
        out_shape=jax.ShapeDtypeStruct(orbitals.shape[:2] + (LANES,), jnp.bfloat16),
        in_specs=[pl.BlockSpec(memory_space=pltpu.SMEM), vmem],
        out_specs=vmem,
        name="candidates",
    )(src_slot, orbitals)


def messages_kernel(count, owner, orbitals, *refs):
    offered, (block, last, first, corner_low, corner_high) = refs[:count], refs[count:]
    groups = orbitals.shape[2] // LANES
    me = lax.axis_index("orb")
    lane = lax.broadcasted_iota(jnp.int32, (EDGE, LANES), 1)
    rounds, places = owner.shape
    wanted = jnp.zeros((EDGE, LANES), jnp.int32)
    for index in range(rounds * places):
        wanted = jnp.where(lane // NZ == index, owner[index // places, index % places], wanted)
    for group in range(groups + 1):
        lanes = pl.ds(group * LANES, LANES)
        tiles = []
        for row in range(EDGE):
            if group < groups:
                tile = orbitals[row, :, lanes].astype(jnp.float32)
            else:
                tile = offered[0][row].astype(jnp.float32)
                for step in range(1, count):
                    theirs = offered[step][row].astype(jnp.float32)
                    tile = jnp.where(wanted == lax.rem(me + count - step, count), theirs, tile)
            tiles.append(tile)
            block[row, :, lanes] = tile.astype(jnp.bfloat16)
            last[row, :, lanes] = tile[EDGE - HALO :].astype(jnp.bfloat16)
            first[row, :, lanes] = tile[:HALO].astype(jnp.bfloat16)
        for ref, cells in ((corner_low, CORNER_LOW), (corner_high, CORNER_HIGH)):
            parts = [tiles[row][start : start + rows] for row, start, rows in cells]
            ref[:, lanes] = jnp.concatenate(parts, axis=0).astype(jnp.bfloat16)


def messages(orbitals, mine, src_owner):
    count = lax.axis_size("orb")
    offered = [mine] + [lax.ppermute(mine, "orb", ring("orb", step)) for step in range(1, count)]
    width = orbitals.shape[2] + LANES
    corners = sum(rows for _, _, rows in CORNER_LOW)
    shapes = [(EDGE, EDGE, width)] + [(EDGE, HALO, width)] * 2 + [(corners, width)] * 2
    vmem = pl.BlockSpec(memory_space=pltpu.VMEM)
    return pl.pallas_call(
        functools.partial(messages_kernel, count),
        out_shape=[jax.ShapeDtypeStruct(shape, jnp.bfloat16) for shape in shapes],
        in_specs=[pl.BlockSpec(memory_space=pltpu.SMEM)] + [vmem] * (1 + count),
        out_specs=[vmem] * 5,
        name="messages",
    )(src_owner, orbitals, *offered)


def exchange(block, last, first, corner_low, corner_high):
    both = ("sx", "sy")
    if lax.axis_size("sx") == 2:
        low = lax.ppermute(corner_low, both, diagonal(1, 1))
        high = lax.ppermute(corner_high, both, diagonal(1, -1))
        across = lax.ppermute(block, "sx", ring("sx", 1))
    else:
        half = corner_low.shape[0] // 2

        def split(cells, step_y):
            return jnp.concatenate(
                [
                    lax.ppermute(cells[:half], both, diagonal(-1, step_y)),
                    lax.ppermute(cells[half:], both, diagonal(1, step_y)),
                ],
                axis=0,
            )

        low, high = split(corner_low, 1), split(corner_high, -1)
        across = jnp.concatenate(
            [
                lax.ppermute(block[:HALO], "sx", ring("sx", -1)),
                lax.ppermute(block[EDGE - HALO :], "sx", ring("sx", 1)),
            ],
            axis=0,
        )
    below = lax.ppermute(last, "sy", ring("sy", 1))
    above = lax.ppermute(first, "sy", ring("sy", -1))
    return across, below, above, low, high


def fill(cells, sources, own, across, below, above, corner_low, corner_high):
    groups = own.shape[2] // LANES - 1
    pitch = cells.shape[1] // (2 * HALO + EDGE)

    def put(x, y, rows, group, values):
        if group == groups:
            sources[x, pl.ds(y, rows), :] = values
        else:
            cells[x, pl.ds(y * pitch + group, rows, stride=pitch), :] = values

    for group in range(groups + 1):
        lanes = pl.ds(group * LANES, LANES)
        for row in range(EDGE):
            outer = row - EDGE if row >= HALO else row + EDGE
            put(HALO + row, HALO, EDGE, group, own[row, :, lanes].astype(jnp.float32))
            put(HALO + outer, HALO, EDGE, group, across[row, :, lanes].astype(jnp.float32))
            put(HALO + row, 0, HALO, group, below[row, :, lanes].astype(jnp.float32))
            put(HALO + row, HALO + EDGE, HALO, group, above[row, :, lanes].astype(jnp.float32))
        for ref, spots, shift in (
            (corner_low, CORNER_LOW, HALO - EDGE),
            (corner_high, CORNER_HIGH, HALO + EDGE),
        ):
            values = ref[:, lanes].astype(jnp.float32)
            at = 0
            for row, first, count in spots:
                outer = row - EDGE if row >= HALO else row + EDGE
                put(HALO + outer, first + shift, count, group, values[at : at + count])
                at += count


def reach(x, y):
    out_x = max(HALO - x, x - (HALO + EDGE - 1), 0)
    out_y = max(HALO - y, y - (HALO + EDGE - 1), 0)
    return out_x + out_y


def kernel(count, *refs):
    halo, (out, cells, rows_of, src, dens, work_a, work_b, acc) = refs[:6], refs[6:]
    groups = halo[0].shape[2] // LANES - 1
    size = 2 * HALO + EDGE
    pitch = cells.shape[1] // size
    halves = groups // SUB
    p0, p1, p2, p3, p4 = power_coeffs()
    tail = (p3 / p4, p2 / p4, p1 / p4, p0 / p4)

    fill(cells, rows_of, *halo)
    spots = [
        [[y for y in range(size) if reach(x, y) <= radius] for x in range(size)]
        for radius in range(HALO + 1)
    ]
    lane = lax.broadcasted_iota(jnp.int32, (SUB, LANES), 1)
    for x in range(size):
        for y in range(0, size, SUB):
            rows = rows_of[x, pl.ds(y, SUB), :]
            for place in range(count):
                one = jnp.where(lane // NZ == place, rows, 0.0)
                one = one + pltpu.roll(one, NZ, 1)
                one = one + pltpu.roll(one, 2 * NZ, 1)
                for step in range(SUB):
                    if y + step in spots[HALO][x]:
                        src[place, x, y + step] = jnp.broadcast_to(
                            one[step : step + 1], (SUB, LANES)
                        )

    inner = lane % NZ
    not_first, not_last = inner != 0, inner != NZ - 1

    def z_sum(v):
        lower = jnp.where(not_first, pltpu.roll(v, 1, 1), 0.0)
        upper = jnp.where(not_last, pltpu.roll(v, LANES - 1, 1), 0.0)
        return lower + upper

    def one_pass(index, carry):
        place, half = index // halves, index % halves
        base = half * SUB

        for x in range(size):
            row = spots[HALO][x]
            values = [cells[x, pl.ds(y * pitch + base, SUB), :] for y in row]
            spread = [src[place, x, y] for y in row]
            for y, value, other in zip(row, values, spread):
                dens[x, y] = value * other
        old = dens
        for step in range(DEGREE):
            new = (work_a, work_b, work_a, None)[step]
            targets = spots[HALO - 1 - step]
            known = spots[HALO - step]
            here, pair_prev = {y: old[0, y] for y in known[0]}, {}
            for x in range(size - 1):
                ahead = {y: old[x + 1, y] for y in known[x + 1]}
                pair = {}
                for y in range(size - 1):
                    if y in targets[x] or y + 1 in targets[x + 1]:
                        pair[y] = ahead[y] + here[y + 1]
                extra = [dens[x, y] for y in targets[x]]
                totals = []
                for y, density in zip(targets[x], extra):
                    total = pair[y] + pair_prev[y - 1] + z_sum(here[y])
                    totals.append(total + tail[step] * density)
                if new is not None:
                    for y, total in zip(targets[x], totals):
                        new[x, y] = total
                elif totals:
                    spread = [src[place, x, y] for y in targets[x]]
                    at = [((y - HALO) * pitch + base) for y in targets[x]]
                    before = [acc[x - HALO, pl.ds(start, SUB), :] for start in at]
                    for i, start in enumerate(at):
                        acc[x - HALO, pl.ds(start, SUB), :] = before[i] + totals[i] * spread[i]
                here, pair_prev = ahead, pair
            old = new
        return carry

    acc[...] = jnp.zeros(acc.shape, jnp.float32)
    lax.fori_loop(0, count * halves, one_pass, 0)
    for x in range(EDGE):
        for group in range(groups):
            tile = acc[x, pl.ds(group, EDGE, stride=pitch), :]
            out[x, :, pl.ds(group * LANES, LANES)] = tile * (-p4)


def fields(halo, count):
    rows_x, rows_y, width = halo[0].shape
    width = width - LANES
    size = 2 * HALO + EDGE
    pitch = width // LANES + 1
    vmem = pl.BlockSpec(memory_space=pltpu.VMEM)
    plane = pltpu.VMEM((size, size, SUB, LANES), jnp.float32)
    return pl.pallas_call(
        functools.partial(kernel, count),
        out_shape=jax.ShapeDtypeStruct((rows_x, rows_y, width), jnp.float32),
        in_specs=[vmem] * 6,
        out_specs=vmem,
        scratch_shapes=[
            pltpu.VMEM((size, size * pitch, LANES), jnp.float32),
            pltpu.VMEM((size, size, LANES), jnp.float32),
            pltpu.VMEM((count, size, size, SUB, LANES), jnp.float32),
            plane,
            plane,
            plane,
            pltpu.VMEM((rows_x, rows_y * pitch, LANES), jnp.float32),
        ],
        compiler_params=pltpu.CompilerParams(vmem_limit_bytes=40 * 2**20),
        name="fields",
    )(*halo)


def body(orbitals, src_owner, src_slot):
    packed = messages(orbitals, candidates(orbitals, src_slot), src_owner)
    return fields((packed[0], *exchange(*packed)), src_slot.size)


def solution(mesh):
    in_specs = (P("sx", "sy", "orb"), P(), P())
    out_specs = P("sx", "sy", "orb")
    return jax.shard_map(body, mesh=mesh, in_specs=in_specs, out_specs=out_specs, check_vma=False)
```

```python
import functools

import jax
import jax.numpy as jnp
from jax import lax
from jax.experimental import pallas as pl
from jax.experimental.pallas import tpu as pltpu
from jax.sharding import PartitionSpec as P

NZ = 32
LANES = 128
SUB = 8
ROWS = 16
DEGREE = 4
HALO = DEGREE
EDGE = 8

CHEB = (
    1.021021021021021,
    -1.7357357357357357,
    1.4753753753753753,
    -1.254069069069069,
    1.0659587087087088,
)


def power_coeffs():
    c0, c1, c2, c3, c4 = CHEB
    return (
        c0 - c2 + c4,
        -(c1 - 3.0 * c3) / 6.0,
        (2.0 * c2 - 8.0 * c4) / 36.0,
        -4.0 * c3 / 216.0,
        8.0 * c4 / 1296.0,
    )


CORNER_LOW = tuple(
    (x, y)
    for x in range(EDGE)
    for y in range(EDGE - HALO, EDGE)
    if min(x + 1, EDGE - x) + EDGE - y <= DEGREE
)
CORNER_HIGH = tuple((x, EDGE - 1 - y) for x, y in CORNER_LOW)
SPLIT = len(CORNER_LOW) // 2


def ring(axis, step):
    count = lax.axis_size(axis)
    return [(i, (i + step) % count) for i in range(count)]


def diagonal(step_x, step_y):
    count_x, count_y = lax.axis_size("sx"), lax.axis_size("sy")
    return [
        (i * count_y + j, (i + step_x) % count_x * count_y + (j + step_y) % count_y)
        for i in range(count_x)
        for j in range(count_y)
    ]


VMEM = pl.BlockSpec(memory_space=pltpu.VMEM)
SMEM = pl.BlockSpec(memory_space=pltpu.SMEM)
SMALL = pltpu.CompilerParams(vmem_limit_bytes=8 * 2**20)


def candidates_kernel(slots, orbitals, out):
    lane = lax.broadcasted_iota(jnp.int32, (EDGE, LANES), 1)
    per_tile = LANES // NZ
    rounds, places = slots.shape
    chosen = [slots[index // places, index % places] for index in range(rounds * places)]
    firsts = [pl.multiple_of(slot // per_tile * LANES, LANES) for slot in chosen]
    shifts = [
        (index - slot % per_tile + per_tile) % per_tile * NZ for index, slot in enumerate(chosen)
    ]
    rows = []
    for row in range(EDGE):
        packed = jnp.zeros((EDGE, LANES), jnp.float32)
        for index, (first, shift) in enumerate(zip(firsts, shifts)):
            tile = orbitals[row, :, pl.ds(first, LANES)].astype(jnp.float32)
            packed = jnp.where(lane // NZ == index, pltpu.roll(tile, shift, 1), packed)
        rows.append(packed)
    for tile in range(EDGE // 2):
        out[tile] = jnp.concatenate(rows[2 * tile : 2 * tile + 2], axis=0).astype(jnp.bfloat16)


def candidates(orbitals, src_slot):
    return pl.pallas_call(
        candidates_kernel,
        out_shape=jax.ShapeDtypeStruct((EDGE * EDGE // ROWS, ROWS, LANES), jnp.bfloat16),
        in_specs=[SMEM, VMEM],
        out_specs=VMEM,
        compiler_params=SMALL,
        name="candidates",
    )(src_slot, orbitals)


def cells_kernel(orbitals, out, scratch):
    for row in range(EDGE):
        for group in range(ROWS):
            tile = orbitals[row, :, pl.ds(group * LANES, LANES)].astype(jnp.float32)
            scratch[row, pl.ds(group, EDGE, stride=ROWS + 1), :] = tile
    for row in range(EDGE):
        for y in range(EDGE):
            tile = scratch[row, pl.ds(y * (ROWS + 1), ROWS), :]
            out[row * EDGE + y] = tile.astype(jnp.bfloat16)


def cells_of(orbitals):
    return pl.pallas_call(
        cells_kernel,
        out_shape=jax.ShapeDtypeStruct((EDGE * EDGE, ROWS, LANES), jnp.bfloat16),
        in_specs=[VMEM],
        out_specs=VMEM,
        scratch_shapes=[pltpu.VMEM((EDGE, EDGE * (ROWS + 1), LANES), jnp.float32)],
        compiler_params=SMALL,
        cost_estimate=pl.CostEstimate(flops=0, bytes_accessed=4 * 2**20, transcendentals=0),
        name="cells",
    )(orbitals)


def messages_kernel(count, owner, cells, *refs):
    offered, (block, last, first, corner_low, corner_high) = refs[:count], refs[count:]
    me = lax.axis_index("orb")
    lane = lax.broadcasted_iota(jnp.int32, (ROWS, LANES), 1)
    rounds, places = owner.shape
    wanted = jnp.zeros((ROWS, LANES), jnp.int32)
    for index in range(rounds * places):
        wanted = jnp.where(lane // NZ == index, owner[index // places, index % places], wanted)
    picked = []
    for tile in range(EDGE * EDGE // ROWS):
        value = offered[0][tile].astype(jnp.float32)
        for step in range(1, count):
            theirs = offered[step][tile].astype(jnp.float32)
            value = jnp.where(wanted == lax.rem(me + count - step, count), theirs, value)
        picked.append(value)

    def pack(ref, spots):
        for at, (x, y) in enumerate(spots):
            ref[at] = cells[x * EDGE + y]
        used = len(spots)
        runs = []
        for x, y in spots:
            if runs and runs[-1][0] == x and runs[-1][2] == y:
                runs[-1][2] = y + 1
            else:
                runs.append([x, y, y + 1])
        parts = [
            picked[x * EDGE // ROWS][x * EDGE % ROWS + low : x * EDGE % ROWS + high]
            for x, low, high in runs
        ]
        if used % ROWS:
            parts.append(jnp.zeros((ROWS - used % ROWS, LANES), jnp.float32))
        rows = jnp.concatenate(parts, axis=0).astype(jnp.bfloat16)
        for tile in range(rows.shape[0] // ROWS):
            ref[used + tile] = rows[tile * ROWS : (tile + 1) * ROWS]

    pack(block, [(x, y) for x in range(EDGE) for y in range(EDGE)])
    pack(last, [(x, y) for x in range(EDGE) for y in range(EDGE - HALO, EDGE)])
    pack(first, [(x, y) for x in range(EDGE) for y in range(HALO)])
    pack(corner_low, CORNER_LOW)
    pack(corner_high, CORNER_HIGH)


def tiles(spots):
    return spots + -(-spots // ROWS)


def messages(orbitals, mine, src_owner):
    count = lax.axis_size("orb")
    offered = [mine] + [lax.ppermute(mine, "orb", ring("orb", step)) for step in range(1, count)]
    lengths = [EDGE * EDGE] + [EDGE * HALO] * 2 + [len(CORNER_LOW)] * 2
    return pl.pallas_call(
        functools.partial(messages_kernel, count),
        out_shape=[
            jax.ShapeDtypeStruct((tiles(length), ROWS, LANES), jnp.bfloat16) for length in lengths
        ],
        in_specs=[SMEM] + [VMEM] * (1 + count),
        out_specs=[VMEM] * 5,
        compiler_params=SMALL,
        name="messages",
    )(src_owner, cells_of(orbitals), *offered)


def exchange(block, last, first, corner_low, corner_high):
    both = ("sx", "sy")
    if lax.axis_size("sx") == 2:
        low = lax.ppermute(corner_low, both, diagonal(1, 1))
        high = lax.ppermute(corner_high, both, diagonal(1, -1))
        across = lax.ppermute(block, "sx", ring("sx", 1))
    else:
        def two_ways(cells, half, axes, down, up, merge):
            end = 2 * half
            back = lax.ppermute(jnp.concatenate([cells[:half], cells[end:]]), axes, down)
            ahead = lax.ppermute(jnp.concatenate([cells[half:end], cells[end:]]), axes, up)
            return jnp.concatenate([back[:half], ahead[:half], merge(back[half:], ahead[half:])])

        def halves(back, ahead):
            return jnp.concatenate([back[: back.shape[0] // 2], ahead[ahead.shape[0] // 2 :]])

        def rows(back, ahead):
            return jnp.concatenate([back[:, :SPLIT], ahead[:, SPLIT:]], axis=1)

        low = two_ways(corner_low, SPLIT, both, diagonal(-1, 1), diagonal(1, 1), rows)
        high = two_ways(corner_high, SPLIT, both, diagonal(-1, -1), diagonal(1, -1), rows)
        across = two_ways(block, EDGE * HALO, "sx", ring("sx", -1), ring("sx", 1), halves)
    below = lax.ppermute(last, "sy", ring("sy", 1))
    above = lax.ppermute(first, "sy", ring("sy", -1))
    return across, below, above, low, high


def place_of(x, y):
    row, core_x = (x - HALO) % EDGE, HALO <= x < HALO + EDGE
    if HALO <= y < HALO + EDGE:
        return (0 if core_x else 1), row * EDGE + y - HALO
    if y < HALO:
        return (2, row * HALO + y) if core_x else (4, CORNER_LOW.index((row, y + EDGE - HALO)))
    y = y - HALO - EDGE
    return (3, row * HALO + y) if core_x else (5, CORNER_HIGH.index((row, y)))


def reach(x, y):
    out_x = max(HALO - x, x - (HALO + EDGE - 1), 0)
    out_y = max(HALO - y, y - (HALO + EDGE - 1), 0)
    return out_x + out_y


def kernel(count, *refs):
    halo, (out, rows_of, dens, work_a, work_b, acc) = refs[:6], refs[6:]
    size = 2 * HALO + EDGE
    pitch = ROWS + 1
    p0, p1, p2, p3, p4 = power_coeffs()
    tail = (p3 / p4, p2 / p4, p1 / p4, p0 / p4)
    spots = [
        [[y for y in range(size) if reach(x, y) <= radius] for x in range(size)]
        for radius in range(HALO + 1)
    ]

    shape = (LANES, LANES)
    lane = lax.broadcasted_iota(jnp.int32, shape, 1) % NZ
    line = lax.broadcasted_iota(jnp.int32, shape, 0)
    first_row = []
    total = 0
    for ref in halo:
        used = ref.shape[0] * ROWS // (ROWS + 1)
        packed = ref[used:].reshape(-1, LANES)
        first_row.append(total)
        for place in range(count):
            repeat = (line == lane + place * NZ).astype(jnp.bfloat16)
            rows_of[place, pl.ds(total, packed.shape[0]), :] = jnp.dot(
                packed, repeat, preferred_element_type=jnp.float32
            )
        total += packed.shape[0]

    def spread(place, x, y):
        which, at = place_of(x, y)
        row = rows_of[place, pl.ds(first_row[which] + at, 1), :]
        return jnp.broadcast_to(row, (SUB, LANES))

    inner = lax.broadcasted_iota(jnp.int32, (SUB, LANES), 1) % NZ
    not_first, not_last = inner != 0, inner != NZ - 1

    def z_sum(v):
        lower = jnp.where(not_first, pltpu.roll(v, 1, 1), 0.0)
        upper = jnp.where(not_last, pltpu.roll(v, LANES - 1, 1), 0.0)
        return lower + upper

    def one_half(place, half):
        base = half * SUB
        old = dens.at[half]
        for step in range(DEGREE):
            new = (work_a, work_b, work_a, None)[step]
            targets = spots[HALO - 1 - step]
            known = spots[HALO - step]
            here, pair_prev = {y: old[0, y] for y in known[0]}, {}
            for x in range(size - 1):
                ahead = {y: old[x + 1, y] for y in known[x + 1]}
                pair = {}
                for y in range(size - 1):
                    if y in targets[x] or y + 1 in targets[x + 1]:
                        pair[y] = ahead[y] + here[y + 1]
                extra = [dens[half, x, y] for y in targets[x]]
                totals = []
                for y, density in zip(targets[x], extra):
                    value = pair[y] + pair_prev[y - 1] + z_sum(here[y])
                    totals.append(value + tail[step] * density)
                if new is not None:
                    for y, value in zip(targets[x], totals):
                        new[x, y] = value
                elif totals:
                    others = [spread(place, x, y) for y in targets[x]]
                    at = [((y - HALO) * pitch + base) for y in targets[x]]
                    before = [acc[x - HALO, pl.ds(start, SUB), :] for start in at]
                    for i, start in enumerate(at):
                        acc[x - HALO, pl.ds(start, SUB), :] = before[i] + totals[i] * others[i]
                here, pair_prev = ahead, pair
            old = new

    def one_source(place, carry):
        for x in range(size):
            row = spots[HALO][x]
            values = []
            for y in row:
                which, at = place_of(x, y)
                values.append(halo[which][at].astype(jnp.float32))
            others = [spread(place, x, y) for y in row]
            for y, value, other in zip(row, values, others):
                for half in range(ROWS // SUB):
                    dens[half, x, y] = value[half * SUB : (half + 1) * SUB] * other

        def inner_loop(half, carry):
            one_half(place, half)
            return carry

        return lax.fori_loop(0, ROWS // SUB, inner_loop, carry)

    acc[...] = jnp.zeros(acc.shape, jnp.float32)
    lax.fori_loop(0, count, one_source, 0)
    for x in range(EDGE):
        for group in range(ROWS):
            tile = acc[x, pl.ds(group, EDGE, stride=pitch), :]
            out[x, :, pl.ds(group * LANES, LANES)] = tile * (-p4)


def fields(halo, count):
    size = 2 * HALO + EDGE
    plane = pltpu.VMEM((size, size, SUB, LANES), jnp.float32)
    rows = sum(array.shape[0] * ROWS // (ROWS + 1) + ROWS for array in halo)
    return pl.pallas_call(
        functools.partial(kernel, count),
        out_shape=jax.ShapeDtypeStruct((EDGE, EDGE, ROWS * LANES), jnp.float32),
        in_specs=[VMEM] * 6,
        out_specs=VMEM,
        scratch_shapes=[
            pltpu.VMEM((count, rows, LANES), jnp.float32),
            pltpu.VMEM((ROWS // SUB, size, size, SUB, LANES), jnp.float32),
            plane,
            plane,
            pltpu.VMEM((EDGE, EDGE * (ROWS + 1), LANES), jnp.float32),
        ],
        compiler_params=pltpu.CompilerParams(vmem_limit_bytes=16 * 2**20),
        name="fields",
    )(*halo)


def body(orbitals, src_owner, src_slot):
    packed = messages(orbitals, candidates(orbitals, src_slot), src_owner)
    return fields((packed[0], *exchange(*packed)), src_slot.size)


def solution(mesh):
    in_specs = (P("sx", "sy", "orb"), P(), P())
    out_specs = P("sx", "sy", "orb")
    return jax.shard_map(body, mesh=mesh, in_specs=in_specs, out_specs=out_specs, check_vma=False)
```

```python
import functools

import jax
import jax.numpy as jnp
import ml_dtypes
import numpy as np
from jax import lax
from jax.experimental import pallas as pl
from jax.experimental.pallas import tpu as pltpu
from jax.sharding import PartitionSpec as P

NZ = 32
LANES = 128
SUB = 8
ROWS = 16
DEGREE = 4
HALO = DEGREE
EDGE = 8

CHEB = (
    1.021021021021021,
    -1.7357357357357357,
    1.4753753753753753,
    -1.254069069069069,
    1.0659587087087088,
)


def power_coeffs():
    c0, c1, c2, c3, c4 = CHEB
    return (
        c0 - c2 + c4,
        -(c1 - 3.0 * c3) / 6.0,
        (2.0 * c2 - 8.0 * c4) / 36.0,
        -4.0 * c3 / 216.0,
        8.0 * c4 / 1296.0,
    )


CORNER_LOW = tuple(
    (x, y)
    for x in range(EDGE)
    for y in range(EDGE - HALO, EDGE)
    if min(x + 1, EDGE - x) + EDGE - y <= DEGREE
)
CORNER_HIGH = tuple((x, EDGE - 1 - y) for x, y in CORNER_LOW)
SPLIT = len(CORNER_LOW) // 2


def ring(axis, step):
    count = lax.axis_size(axis)
    return [(i, (i + step) % count) for i in range(count)]


def diagonal(step_x, step_y):
    count_x, count_y = lax.axis_size("sx"), lax.axis_size("sy")
    return [
        (i * count_y + j, (i + step_x) % count_x * count_y + (j + step_y) % count_y)
        for i in range(count_x)
        for j in range(count_y)
    ]


VMEM = pl.BlockSpec(memory_space=pltpu.VMEM)
SMEM = pl.BlockSpec(memory_space=pltpu.SMEM)
HBM = pl.BlockSpec(memory_space=pltpu.HBM)
SMALL = pltpu.CompilerParams(vmem_limit_bytes=8 * 2**20)


def candidates_kernel(slots, orbitals, out, chosen, tiles_of, slot_sem, tile_sems):
    copy = pltpu.make_async_copy(slots, chosen, slot_sem)
    copy.start()
    copy.wait()
    lane = lax.broadcasted_iota(jnp.int32, (EDGE, LANES), 1)
    per_tile = LANES // NZ
    rounds, places = slots.shape
    copies, shifts = [], []
    for index in range(rounds * places):
        slot = chosen[index // places, index % places]
        lanes = pl.ds(pl.multiple_of(slot // per_tile * LANES, LANES), LANES)
        copies.append(
            pltpu.make_async_copy(
                orbitals.at[:, :, lanes], tiles_of.at[index], tile_sems.at[index]
            )
        )
        copies[-1].start()
        shifts.append((index - slot % per_tile + per_tile) % per_tile * NZ)
    for copy in copies:
        copy.wait()
    rows = []
    for row in range(EDGE):
        packed = jnp.zeros((EDGE, LANES), jnp.float32)
        for index, shift in enumerate(shifts):
            tile = tiles_of[index, row].astype(jnp.float32)
            packed = jnp.where(lane // NZ == index, pltpu.roll(tile, shift, 1), packed)
        rows.append(packed)
    for tile in range(EDGE // 2):
        out[tile] = jnp.concatenate(rows[2 * tile : 2 * tile + 2], axis=0).astype(jnp.bfloat16)


def candidates(orbitals, src_slot):
    count = src_slot.size
    return pl.pallas_call(
        candidates_kernel,
        out_shape=jax.ShapeDtypeStruct((EDGE * EDGE // ROWS, ROWS, LANES), jnp.bfloat16),
        in_specs=[HBM, HBM],
        out_specs=VMEM,
        scratch_shapes=[
            pltpu.SMEM(src_slot.shape, jnp.int32),
            pltpu.VMEM((count, EDGE, EDGE, LANES), jnp.bfloat16),
            pltpu.SemaphoreType.DMA,
            pltpu.SemaphoreType.DMA((count,)),
        ],
        compiler_params=SMALL,
        name="candidates",
    )(src_slot, orbitals)


def cells_kernel(owner, orbitals, out, wanted, scratch):
    lane = lax.broadcasted_iota(jnp.int32, (ROWS, LANES), 1)
    rounds, places = owner.shape
    owners = jnp.zeros((ROWS, LANES), jnp.int32)
    for index in range(rounds * places):
        owners = jnp.where(lane // NZ == index, owner[index // places, index % places], owners)
    wanted[...] = owners
    for row in range(EDGE):
        for group in range(ROWS):
            tile = orbitals[row, :, pl.ds(group * LANES, LANES)].astype(jnp.float32)
            scratch[row, pl.ds(group, EDGE, stride=ROWS + 1), :] = tile
    for row in range(EDGE):
        for y in range(EDGE):
            tile = scratch[row, pl.ds(y * (ROWS + 1), ROWS), :]
            out[row * EDGE + y] = tile.astype(jnp.bfloat16)


def cells_of(orbitals, src_owner):
    return pl.pallas_call(
        cells_kernel,
        out_shape=[
            jax.ShapeDtypeStruct((EDGE * EDGE, ROWS, LANES), jnp.bfloat16),
            jax.ShapeDtypeStruct((ROWS, LANES), jnp.int32),
        ],
        in_specs=[SMEM, VMEM],
        out_specs=[VMEM, VMEM],
        scratch_shapes=[pltpu.VMEM((EDGE, EDGE * (ROWS + 1), LANES), jnp.float32)],
        compiler_params=SMALL,
        cost_estimate=pl.CostEstimate(flops=0, bytes_accessed=4 * 2**20, transcendentals=0),
        name="cells",
    )(src_owner, orbitals)


def messages_kernel(count, cells, owners, *refs):
    offered, (block, last, first, corner_low, corner_high) = refs[:count], refs[count:]
    me = lax.axis_index("orb")
    wanted = owners[...]
    picked = []
    for tile in range(EDGE * EDGE // ROWS):
        value = offered[0][tile].astype(jnp.float32)
        for step in range(1, count):
            theirs = offered[step][tile].astype(jnp.float32)
            value = jnp.where(wanted == lax.rem(me + count - step, count), theirs, value)
        picked.append(value)

    def pack(ref, spots):
        for at, (x, y) in enumerate(spots):
            ref[at] = cells[x * EDGE + y]
        used = len(spots)
        runs = []
        for x, y in spots:
            if runs and runs[-1][0] == x and runs[-1][2] == y:
                runs[-1][2] = y + 1
            else:
                runs.append([x, y, y + 1])
        parts = [
            picked[x * EDGE // ROWS][x * EDGE % ROWS + low : x * EDGE % ROWS + high]
            for x, low, high in runs
        ]
        if used % ROWS:
            parts.append(jnp.zeros((ROWS - used % ROWS, LANES), jnp.float32))
        rows = jnp.concatenate(parts, axis=0).astype(jnp.bfloat16)
        for tile in range(rows.shape[0] // ROWS):
            ref[used + tile] = rows[tile * ROWS : (tile + 1) * ROWS]

    pack(block, [(x, y) for x in range(EDGE) for y in range(EDGE)])
    pack(last, [(x, y) for x in range(EDGE) for y in range(EDGE - HALO, EDGE)])
    pack(first, [(x, y) for x in range(EDGE) for y in range(HALO)])
    pack(corner_low, CORNER_LOW)
    pack(corner_high, CORNER_HIGH)


def tiles(spots):
    return spots + -(-spots // ROWS)


def messages(orbitals, mine, src_owner):
    count = lax.axis_size("orb")
    offered = [mine] + [lax.ppermute(mine, "orb", ring("orb", step)) for step in range(1, count)]
    lengths = [EDGE * EDGE] + [EDGE * HALO] * 2 + [len(CORNER_LOW)] * 2
    return pl.pallas_call(
        functools.partial(messages_kernel, count),
        out_shape=[
            jax.ShapeDtypeStruct((tiles(length), ROWS, LANES), jnp.bfloat16) for length in lengths
        ],
        in_specs=[VMEM] * (2 + count),
        out_specs=[VMEM] * 5,
        compiler_params=SMALL,
        name="messages",
    )(*cells_of(orbitals, src_owner), *offered)


def exchange(block, last, first, corner_low, corner_high):
    both = ("sx", "sy")
    if lax.axis_size("sx") == 2:
        low = lax.ppermute(corner_low, both, diagonal(1, 1))
        high = lax.ppermute(corner_high, both, diagonal(1, -1))
        across = lax.ppermute(block, "sx", ring("sx", 1))
    else:
        def two_ways(cells, half, axes, down, up, merge):
            end = 2 * half
            back = lax.ppermute(jnp.concatenate([cells[:half], cells[end:]]), axes, down)
            ahead = lax.ppermute(jnp.concatenate([cells[half:end], cells[end:]]), axes, up)
            return jnp.concatenate([back[:half], ahead[:half], merge(back[half:], ahead[half:])])

        def halves(back, ahead):
            return jnp.concatenate([back[: back.shape[0] // 2], ahead[ahead.shape[0] // 2 :]])

        def rows(back, ahead):
            return jnp.concatenate([back[:, :SPLIT], ahead[:, SPLIT:]], axis=1)

        low = two_ways(corner_low, SPLIT, both, diagonal(-1, 1), diagonal(1, 1), rows)
        high = two_ways(corner_high, SPLIT, both, diagonal(-1, -1), diagonal(1, -1), rows)
        across = two_ways(block, EDGE * HALO, "sx", ring("sx", -1), ring("sx", 1), halves)
    below = lax.ppermute(last, "sy", ring("sy", 1))
    above = lax.ppermute(first, "sy", ring("sy", -1))
    return across, below, above, low, high


def place_of(x, y):
    row, core_x = (x - HALO) % EDGE, HALO <= x < HALO + EDGE
    if HALO <= y < HALO + EDGE:
        return (0 if core_x else 1), row * EDGE + y - HALO
    if y < HALO:
        return (2, row * HALO + y) if core_x else (4, CORNER_LOW.index((row, y + EDGE - HALO)))
    y = y - HALO - EDGE
    return (3, row * HALO + y) if core_x else (5, CORNER_HIGH.index((row, y)))


def reach(x, y):
    out_x = max(HALO - x, x - (HALO + EDGE - 1), 0)
    out_y = max(HALO - y, y - (HALO + EDGE - 1), 0)
    return out_x + out_y


def z_modes():
    index = np.arange(1, NZ + 1)
    modes = np.sqrt(2.0 / (NZ + 1)) * np.sin(np.pi * np.outer(index, index) / (NZ + 1))
    modes = np.kron(np.eye(LANES // NZ), modes)
    high = modes.astype(ml_dtypes.bfloat16)
    low = (modes - high.astype(np.float64)).astype(ml_dtypes.bfloat16)
    both = np.concatenate([high, low], axis=1)
    value = np.tile(2.0 * np.cos(np.pi * index / (NZ + 1)), LANES // NZ)
    p0, p1, p2, p3, p4 = power_coeffs()
    a3, a2, a1, a0 = p3 / p4, p2 / p4, p1 / p4, p0 / p4
    tail = [
        4.0 * value + a3,
        6.0 * value**2 + 3.0 * a3 * value + a2,
        4.0 * value**3 + 3.0 * a3 * value**2 + 2.0 * a2 * value + a1,
        value**4 + a3 * value**3 + a2 * value**2 + a1 * value + a0,
    ]
    tail = np.repeat(np.stack(tail)[:, None, :], SUB, axis=1).astype(np.float32)
    return np.concatenate([both, both], axis=0), tail


SIZE = 2 * HALO + EDGE


def within(radius):
    return [[y for y in range(SIZE) if reach(x, y) <= radius] for x in range(SIZE)]


CELLS = [(x, y) for x in range(SIZE) for y in within(HALO)[x]]
CORE = [(x, y) for x in range(HALO, HALO + EDGE) for y in range(HALO, HALO + EDGE)]


def kernel(count, *refs):
    halo, modes, tails = refs[:6], refs[6], refs[7]
    out, rows_of, parts, hat, work_a, work_b, last, acc = refs[8:]
    pitch = ROWS + 1
    number = {cell: at for at, cell in enumerate(CELLS)}

    shape = (LANES, LANES)
    lane = lax.broadcasted_iota(jnp.int32, shape, 1) % NZ
    line = lax.broadcasted_iota(jnp.int32, shape, 0)
    first_row = []
    total = 0
    for ref in halo:
        used = ref.shape[0] * ROWS // (ROWS + 1)
        packed = ref[used:].reshape(-1, LANES)
        first_row.append(total)
        for place in range(count):
            repeat = (line == lane + place * NZ).astype(jnp.bfloat16)
            rows_of[place, pl.ds(total, packed.shape[0]), :] = jnp.dot(
                packed, repeat, preferred_element_type=jnp.float32
            )
        total += packed.shape[0]

    def spread(place, x, y):
        which, at = place_of(x, y)
        row = rows_of[place, pl.ds(first_row[which] + at, 1), :]
        return jnp.broadcast_to(row, (ROWS, LANES))

    def keep(at, value):
        high = value.astype(jnp.bfloat16)
        low = (value - high.astype(jnp.float32)).astype(jnp.bfloat16)
        parts[at, :, :LANES] = high
        parts[at, :, LANES:] = low

    def turned(cells):
        rows = parts[:cells].reshape(cells * ROWS, 2 * LANES)
        both = jnp.dot(rows, modes[...], preferred_element_type=jnp.float32)
        return (both[:, :LANES] + both[:, LANES:]).reshape(cells, ROWS, LANES)

    def one_half(half):
        rows = pl.ds(pl.multiple_of(half * SUB, SUB), SUB)

        def start(x, y):
            return hat[number[x, y], rows, :]

        for step in range(DEGREE):
            new = (work_a, work_b, work_a, None)[step]
            old = (None, work_a, work_b, work_a)[step]
            targets, known = within(HALO - 1 - step), within(HALO - step)

            def load(x):
                return {y: start(x, y) if old is None else old[x, y] for y in known[x]}

            here, pair_prev = load(0), {}
            for x in range(SIZE - 1):
                ahead = load(x + 1)
                pair = {}
                for y in range(SIZE - 1):
                    if y in targets[x] or y + 1 in targets[x + 1]:
                        pair[y] = ahead[y] + here[y + 1]
                extra = [here[y] if old is None else start(x, y) for y in targets[x]]
                totals = [
                    pair[y] + pair_prev[y - 1] + tails[step] * density
                    for y, density in zip(targets[x], extra)
                ]
                for y, value in zip(targets[x], totals):
                    if new is not None:
                        new[x, y] = value
                    else:
                        last[CORE.index((x, y)), rows, :] = value
                here, pair_prev = ahead, pair

    def one_source(place, carry):
        for x in range(SIZE):
            row = within(HALO)[x]
            values = []
            for y in row:
                which, at = place_of(x, y)
                values.append(halo[which][at].astype(jnp.float32))
            others = [spread(place, x, y) for y in row]
            for y, value, other in zip(row, values, others):
                keep(number[x, y], value * other)
        hat[...] = turned(len(CELLS))

        def inner_loop(half, carry):
            one_half(half)
            return carry

        lax.fori_loop(0, ROWS // SUB, inner_loop, 0)
        for at in range(len(CORE)):
            keep(at, last[at])
        back = turned(len(CORE))
        for at, (x, y) in enumerate(CORE):
            rows = pl.ds((y - HALO) * pitch, ROWS)
            acc[x - HALO, rows, :] = acc[x - HALO, rows, :] + back[at] * spread(place, x, y)
        return carry

    acc[...] = jnp.zeros(acc.shape, jnp.float32)
    lax.fori_loop(0, count, one_source, 0)
    for x in range(EDGE):
        for group in range(ROWS):
            tile = acc[x, pl.ds(group, EDGE, stride=pitch), :]
            out[x, :, pl.ds(group * LANES, LANES)] = tile * (-power_coeffs()[-1])


def fields(halo, count):
    plane = pltpu.VMEM((SIZE, SIZE, SUB, LANES), jnp.float32)
    rows = sum(array.shape[0] * ROWS // (ROWS + 1) + ROWS for array in halo)
    modes, tails = z_modes()
    return pl.pallas_call(
        functools.partial(kernel, count),
        out_shape=jax.ShapeDtypeStruct((EDGE, EDGE, ROWS * LANES), jnp.float32),
        in_specs=[VMEM] * 8,
        out_specs=VMEM,
        scratch_shapes=[
            pltpu.VMEM((count, rows, LANES), jnp.float32),
            pltpu.VMEM((len(CELLS), ROWS, 2 * LANES), jnp.bfloat16),
            pltpu.VMEM((len(CELLS), ROWS, LANES), jnp.float32),
            plane,
            plane,
            pltpu.VMEM((len(CORE), ROWS, LANES), jnp.float32),
            pltpu.VMEM((EDGE, EDGE * (ROWS + 1), LANES), jnp.float32),
        ],
        compiler_params=pltpu.CompilerParams(vmem_limit_bytes=24 * 2**20),
        name="fields",
    )(*halo, modes, tails)


def body(orbitals, src_owner, src_slot):
    packed = messages(orbitals, candidates(orbitals, src_slot), src_owner)
    return fields((packed[0], *exchange(*packed)), src_slot.size)


def solution(mesh):
    in_specs = (P("sx", "sy", "orb"), P(), P())
    out_specs = P("sx", "sy", "orb")
    return jax.shard_map(body, mesh=mesh, in_specs=in_specs, out_specs=out_specs, check_vma=False)
```

```python
import functools

import jax
import jax.numpy as jnp
import ml_dtypes
import numpy as np
from jax import lax
from jax.experimental import pallas as pl
from jax.experimental.pallas import tpu as pltpu
from jax.sharding import PartitionSpec as P

NZ = 32
LANES = 128
SUB = 8
ROWS = 16
DEGREE = 4
HALO = DEGREE
EDGE = 8

CHEB = (
    1.021021021021021,
    -1.7357357357357357,
    1.4753753753753753,
    -1.254069069069069,
    1.0659587087087088,
)


def power_coeffs():
    c0, c1, c2, c3, c4 = CHEB
    return (
        c0 - c2 + c4,
        -(c1 - 3.0 * c3) / 6.0,
        (2.0 * c2 - 8.0 * c4) / 36.0,
        -4.0 * c3 / 216.0,
        8.0 * c4 / 1296.0,
    )


CORNER_LOW = tuple(
    (x, y)
    for x in range(EDGE)
    for y in range(EDGE - HALO, EDGE)
    if min(x + 1, EDGE - x) + EDGE - y <= DEGREE
)
CORNER_HIGH = tuple((x, EDGE - 1 - y) for x, y in CORNER_LOW)
SPLIT = len(CORNER_LOW) // 2


def ring(axis, step):
    count = lax.axis_size(axis)
    return [(i, (i + step) % count) for i in range(count)]


def diagonal(step_x, step_y):
    count_x, count_y = lax.axis_size("sx"), lax.axis_size("sy")
    return [
        (i * count_y + j, (i + step_x) % count_x * count_y + (j + step_y) % count_y)
        for i in range(count_x)
        for j in range(count_y)
    ]


VMEM = pl.BlockSpec(memory_space=pltpu.VMEM)
HBM = pl.BlockSpec(memory_space=pltpu.HBM)
SMALL = pltpu.CompilerParams(vmem_limit_bytes=8 * 2**20)


def candidates_kernel(
    owner, slots, orbitals, out, wanted, holders, chosen, tiles_of, small_sems, tile_sems
):
    owner_copy = pltpu.make_async_copy(owner, holders, small_sems.at[0])
    slot_copy = pltpu.make_async_copy(slots, chosen, small_sems.at[1])
    owner_copy.start()
    slot_copy.start()
    slot_copy.wait()
    lane = lax.broadcasted_iota(jnp.int32, (EDGE, LANES), 1)
    per_tile = LANES // NZ
    rounds, places = slots.shape
    copies, shifts = [], []
    for index in range(rounds * places):
        slot = chosen[index // places, index % places]
        lanes = pl.ds(pl.multiple_of(slot // per_tile * LANES, LANES), LANES)
        copies.append(
            pltpu.make_async_copy(
                orbitals.at[:, :, lanes], tiles_of.at[index], tile_sems.at[index]
            )
        )
        copies[-1].start()
        shifts.append((index - slot % per_tile + per_tile) % per_tile * NZ)
    owner_copy.wait()
    seat = lax.broadcasted_iota(jnp.int32, (ROWS, LANES), 1) // NZ
    owners = jnp.zeros((ROWS, LANES), jnp.int32)
    for index in range(rounds * places):
        owners = jnp.where(seat == index, holders[index // places, index % places], owners)
    wanted[...] = owners
    for copy in copies:
        copy.wait()
    rows = []
    for row in range(EDGE):
        packed = jnp.zeros((EDGE, LANES), jnp.float32)
        for index, shift in enumerate(shifts):
            tile = tiles_of[index, row].astype(jnp.float32)
            packed = jnp.where(lane // NZ == index, pltpu.roll(tile, shift, 1), packed)
        rows.append(packed)
    for tile in range(EDGE // 2):
        out[tile] = jnp.concatenate(rows[2 * tile : 2 * tile + 2], axis=0).astype(jnp.bfloat16)


def candidates(orbitals, src_owner, src_slot):
    count = src_slot.size
    return pl.pallas_call(
        candidates_kernel,
        out_shape=[
            jax.ShapeDtypeStruct((EDGE * EDGE // ROWS, ROWS, LANES), jnp.bfloat16),
            jax.ShapeDtypeStruct((ROWS, LANES), jnp.int32),
        ],
        in_specs=[HBM] * 3,
        out_specs=[VMEM] * 2,
        scratch_shapes=[
            pltpu.SMEM(src_owner.shape, jnp.int32),
            pltpu.SMEM(src_slot.shape, jnp.int32),
            pltpu.VMEM((count, EDGE, EDGE, LANES), jnp.bfloat16),
            pltpu.SemaphoreType.DMA((2,)),
            pltpu.SemaphoreType.DMA((count,)),
        ],
        compiler_params=pltpu.CompilerParams(vmem_limit_bytes=60 * 2**20),
        name="candidates",
    )(src_owner, src_slot, orbitals)


def cells_kernel(orbitals, out, last, first, scratch):
    for row in range(EDGE):
        for group in range(ROWS):
            tile = orbitals[row, :, pl.ds(group * LANES, LANES)].astype(jnp.float32)
            scratch[row, pl.ds(group, EDGE, stride=ROWS + 1), :] = tile
    for row in range(EDGE):
        for y in range(EDGE):
            tile = scratch[row, pl.ds(y * (ROWS + 1), ROWS), :].astype(jnp.bfloat16)
            out[row * EDGE + y] = tile
            if y < HALO:
                first[row * HALO + y] = tile
            if y >= EDGE - HALO:
                last[row * HALO + y + HALO - EDGE] = tile


def cells_of(orbitals):
    lengths = (EDGE * EDGE, EDGE * HALO, EDGE * HALO)
    return pl.pallas_call(
        cells_kernel,
        out_shape=[jax.ShapeDtypeStruct((length, ROWS, LANES), jnp.bfloat16) for length in lengths],
        in_specs=[VMEM],
        out_specs=[VMEM] * 3,
        scratch_shapes=[pltpu.VMEM((EDGE, EDGE * (ROWS + 1), LANES), jnp.float32)],
        compiler_params=SMALL,
        name="cells",
    )(orbitals)


def sources_kernel(count, cells, owners, *refs):
    offered, (block, last, first, corner_low, corner_high) = refs[:count], refs[count:]
    me = lax.axis_index("orb")
    wanted = owners[...]
    picked = []
    for tile in range(EDGE * EDGE // ROWS):
        value = offered[0][tile].astype(jnp.float32)
        for step in range(1, count):
            theirs = offered[step][tile].astype(jnp.float32)
            value = jnp.where(wanted == lax.rem(me + count - step, count), theirs, value)
        picked.append(value)
        block[tile] = value.astype(jnp.bfloat16)

    def pack(ref, used, spots):
        runs = []
        for x, y in spots:
            if runs and runs[-1][0] == x and runs[-1][2] == y:
                runs[-1][2] = y + 1
            else:
                runs.append([x, y, y + 1])
        parts = [
            picked[x * EDGE // ROWS][x * EDGE % ROWS + low : x * EDGE % ROWS + high]
            for x, low, high in runs
        ]
        if len(spots) % ROWS:
            parts.append(jnp.zeros((ROWS - len(spots) % ROWS, LANES), jnp.float32))
        rows = jnp.concatenate(parts, axis=0).astype(jnp.bfloat16)
        for tile in range(rows.shape[0] // ROWS):
            ref[used + tile] = rows[tile * ROWS : (tile + 1) * ROWS]

    pack(last, 0, [(x, y) for x in range(EDGE) for y in range(EDGE - HALO, EDGE)])
    pack(first, 0, [(x, y) for x in range(EDGE) for y in range(HALO)])
    for ref, spots in ((corner_low, CORNER_LOW), (corner_high, CORNER_HIGH)):
        for at, (x, y) in enumerate(spots):
            ref[at] = cells[x * EDGE + y]
        pack(ref, len(spots), spots)


def sources_of(cells, owners, offered):
    corner = len(CORNER_LOW) + 1
    lengths = (EDGE * EDGE // ROWS,) + (EDGE * HALO // ROWS,) * 2 + (corner,) * 2
    return pl.pallas_call(
        functools.partial(sources_kernel, len(offered)),
        out_shape=[jax.ShapeDtypeStruct((length, ROWS, LANES), jnp.bfloat16) for length in lengths],
        in_specs=[VMEM] * (2 + len(offered)),
        out_specs=[VMEM] * 5,
        compiler_params=SMALL,
        name="sources",
    )(cells, owners, *offered)


def across_x(block):
    if lax.axis_size("sx") == 2:
        return lax.ppermute(block, "sx", ring("sx", 1))
    half = block.shape[0] // 2
    low = lax.ppermute(block[:half], "sx", ring("sx", -1))
    return jnp.concatenate([low, lax.ppermute(block[half:], "sx", ring("sx", 1))], axis=0)


def across_corner(cells, step_y):
    both = ("sx", "sy")
    if lax.axis_size("sx") == 2:
        return lax.ppermute(cells, both, diagonal(1, step_y))
    low = lax.ppermute(cells[:SPLIT], both, diagonal(-1, step_y))
    high = lax.ppermute(cells[SPLIT : 2 * SPLIT], both, diagonal(1, step_y))
    rows = [lax.ppermute(cells[2 * SPLIT :], both, diagonal(step_x, step_y)) for step_x in (-1, 1)]
    rows = jnp.concatenate([rows[0][:, :SPLIT], rows[1][:, SPLIT:]], axis=1)
    return jnp.concatenate([low, high, rows], axis=0)


def across_y(last, first):
    return lax.ppermute(last, "sy", ring("sy", 1)), lax.ppermute(first, "sy", ring("sy", -1))


def place_of(x, y):
    row, core_x = (x - HALO) % EDGE, HALO <= x < HALO + EDGE
    if HALO <= y < HALO + EDGE:
        return (0 if core_x else 1), row * EDGE + y - HALO
    if y < HALO:
        return (2, row * HALO + y) if core_x else (4, CORNER_LOW.index((row, y + EDGE - HALO)))
    y = y - HALO - EDGE
    return (3, row * HALO + y) if core_x else (5, CORNER_HIGH.index((row, y)))


def reach(x, y):
    out_x = max(HALO - x, x - (HALO + EDGE - 1), 0)
    out_y = max(HALO - y, y - (HALO + EDGE - 1), 0)
    return out_x + out_y


def z_modes():
    index = np.arange(1, NZ + 1)
    modes = np.sqrt(2.0 / (NZ + 1)) * np.sin(np.pi * np.outer(index, index) / (NZ + 1))
    modes = np.kron(np.eye(LANES // NZ), modes)
    high = modes.astype(ml_dtypes.bfloat16)
    low = (modes - high.astype(np.float64)).astype(ml_dtypes.bfloat16)
    both = np.concatenate([high, low], axis=1)
    value = np.tile(2.0 * np.cos(np.pi * index / (NZ + 1)), LANES // NZ)
    p0, p1, p2, p3, p4 = power_coeffs()
    a3, a2, a1, a0 = p3 / p4, p2 / p4, p1 / p4, p0 / p4
    tail = [
        4.0 * value + a3,
        6.0 * value**2 + 3.0 * a3 * value + a2,
        4.0 * value**3 + 3.0 * a3 * value**2 + 2.0 * a2 * value + a1,
        value**4 + a3 * value**3 + a2 * value**2 + a1 * value + a0,
    ]
    tail = np.repeat(np.stack(tail)[:, None, :], SUB, axis=1).astype(np.float32)
    return np.concatenate([both, both], axis=0), tail


SIZE = 2 * HALO + EDGE


def within(radius):
    return [[y for y in range(SIZE) if reach(x, y) <= radius] for x in range(SIZE)]


CELLS = [(x, y) for x in range(SIZE) for y in within(HALO)[x]]
CORE = [(x, y) for x in range(HALO, HALO + EDGE) for y in range(HALO, HALO + EDGE)]


def kernel(count, *refs):
    halo, sources, modes, tails = refs[:6], refs[6:10], refs[10], refs[11]
    out, rows_of, parts, hat, work_a, work_b, last, acc = refs[12:]
    pitch = ROWS + 1
    number = {cell: at for at, cell in enumerate(CELLS)}

    shape = (LANES, LANES)
    lane = lax.broadcasted_iota(jnp.int32, shape, 1) % NZ
    line = lax.broadcasted_iota(jnp.int32, shape, 0)
    repeats = [(line == lane + place * NZ).astype(jnp.bfloat16) for place in range(count)]
    first_row = []
    total, edges = 0, ROWS * sum(ref.shape[0] for ref in sources)
    for ref in (*sources, *halo[4:]):
        packed = (ref[len(CORNER_LOW) :] if total >= edges else ref[...]).reshape(-1, LANES)
        first_row.append(total)
        for place, repeat in enumerate(repeats):
            rows_of[place, pl.ds(total, packed.shape[0]), :] = jnp.dot(
                packed, repeat, preferred_element_type=jnp.float32
            )
        total += packed.shape[0]

    def spread(place, x, y):
        which, at = place_of(x, y)
        row = rows_of[place, pl.ds(first_row[which] + at, 1), :]
        return jnp.broadcast_to(row, (ROWS, LANES))

    def keep(at, value):
        high = value.astype(jnp.bfloat16)
        low = (value - high.astype(jnp.float32)).astype(jnp.bfloat16)
        parts[at, :, :LANES] = high
        parts[at, :, LANES:] = low

    def turned(first, end):
        cells = end - first
        rows = parts[first:end].reshape(cells * ROWS, 2 * LANES)
        both = jnp.dot(rows, modes[...], preferred_element_type=jnp.float32)
        return (both[:, :LANES] + both[:, LANES:]).reshape(cells, ROWS, LANES)

    def one_half(half):
        rows = pl.ds(half * SUB, SUB)

        def start(x, y):
            return hat[number[x, y], rows, :]

        for step in range(DEGREE):
            new = (work_a, work_b, work_a, None)[step]
            old = (None, work_a, work_b, work_a)[step]
            targets, known = within(HALO - 1 - step), within(HALO - step)

            def load(x):
                return {y: start(x, y) if old is None else old[x, y] for y in known[x]}

            here, pair_prev = load(0), {}
            for x in range(SIZE - 1):
                ahead = load(x + 1)
                pair = {}
                for y in range(SIZE - 1):
                    if y in targets[x] or y + 1 in targets[x + 1]:
                        pair[y] = ahead[y] + here[y + 1]
                    if y in targets[x]:
                        density = here[y] if old is None else start(x, y)
                        value = pair[y] + pair_prev[y - 1] + tails[step] * density
                        if new is not None:
                            new[x, y] = value
                        else:
                            last[CORE.index((x, y)), rows, :] = value
                here, pair_prev = ahead, pair

    def one_source(place, carry):
        chunk = len(CELLS) // 4
        for first in range(0, len(CELLS), chunk):
            end = min(first + chunk, len(CELLS))
            for at in range(first, end):
                which, spot = place_of(*CELLS[at])
                keep(at, halo[which][spot].astype(jnp.float32) * spread(place, *CELLS[at]))
            hat[first:end] = turned(first, end)
        for half in range(ROWS // SUB):
            one_half(half)
        for at in range(len(CORE)):
            keep(at, last[at])
        back = turned(0, len(CORE))
        for at, (x, y) in enumerate(CORE):
            rows = pl.ds((y - HALO) * pitch, ROWS)
            acc[x - HALO, rows, :] = acc[x - HALO, rows, :] + back[at] * spread(place, x, y)
        return carry

    acc[...] = jnp.zeros(acc.shape, jnp.float32)
    lax.fori_loop(0, count, one_source, 0)
    for x in range(EDGE):
        for group in range(ROWS):
            tile = acc[x, pl.ds(group, EDGE, stride=pitch), :]
            out[x, :, pl.ds(group * LANES, LANES)] = tile * (-power_coeffs()[-1])


def fields(halo, sources, count):
    plane = pltpu.VMEM((SIZE, SIZE, SUB, LANES), jnp.float32)
    rows = ROWS * (sum(array.shape[0] for array in sources) + 2)
    modes, tails = z_modes()
    return pl.pallas_call(
        functools.partial(kernel, count),
        out_shape=jax.ShapeDtypeStruct((EDGE, EDGE, ROWS * LANES), jnp.float32),
        in_specs=[VMEM] * 12,
        out_specs=VMEM,
        scratch_shapes=[
            pltpu.VMEM((count, rows, LANES), jnp.float32),
            pltpu.VMEM((len(CELLS), ROWS, 2 * LANES), jnp.bfloat16),
            pltpu.VMEM((len(CELLS), ROWS, LANES), jnp.float32),
            plane,
            plane,
            pltpu.VMEM((len(CORE), ROWS, LANES), jnp.float32),
            pltpu.VMEM((EDGE, EDGE * (ROWS + 1), LANES), jnp.float32),
        ],
        compiler_params=pltpu.CompilerParams(vmem_limit_bytes=24 * 2**20),
        name="fields",
    )(*halo, *sources, modes, tails)


def body(orbitals, src_owner, src_slot):
    mine, owners = candidates(orbitals, src_owner, src_slot)
    cells, last, first = cells_of(orbitals)
    block = (cells, across_x(cells), *across_y(last, first))
    offered = [
        mine if step == 0 else lax.ppermute(mine, "orb", ring("orb", step))
        for step in range(lax.axis_size("orb"))
    ]
    picked, last, first, low, high = sources_of(cells, owners, offered)
    sources = (picked, across_x(picked), *across_y(last, first))
    corners = (across_corner(low, 1), across_corner(high, -1))
    return fields(block + corners, sources, src_slot.size)


def solution(mesh):
    in_specs = (P("sx", "sy", "orb"), P(), P())
    out_specs = P("sx", "sy", "orb")
    return jax.shard_map(body, mesh=mesh, in_specs=in_specs, out_specs=out_specs, check_vma=False)
```

```python
import functools

import jax
import jax.numpy as jnp
import ml_dtypes
import numpy as np
from jax import lax
from jax.experimental import pallas as pl
from jax.experimental.pallas import tpu as pltpu
from jax.sharding import PartitionSpec as P

NZ = 32
LANES = 128
SUB = 8
ROWS = 16
DEGREE = 4
HALO = DEGREE
EDGE = 8

CHEB = (
    1.021021021021021,
    -1.7357357357357357,
    1.4753753753753753,
    -1.254069069069069,
    1.0659587087087088,
)


def power_coeffs():
    c0, c1, c2, c3, c4 = CHEB
    return (
        c0 - c2 + c4,
        -(c1 - 3.0 * c3) / 6.0,
        (2.0 * c2 - 8.0 * c4) / 36.0,
        -4.0 * c3 / 216.0,
        8.0 * c4 / 1296.0,
    )


CORNER_LOW = tuple(
    (x, y)
    for x in range(EDGE)
    for y in range(EDGE - HALO, EDGE)
    if min(x + 1, EDGE - x) + EDGE - y <= DEGREE
)
CORNER_HIGH = tuple((x, EDGE - 1 - y) for x, y in CORNER_LOW)
SPLIT = len(CORNER_LOW) // 2


def ring(axis, step):
    count = lax.axis_size(axis)
    return [(i, (i + step) % count) for i in range(count)]


def diagonal(step_x, step_y):
    count_x, count_y = lax.axis_size("sx"), lax.axis_size("sy")
    return [
        (i * count_y + j, (i + step_x) % count_x * count_y + (j + step_y) % count_y)
        for i in range(count_x)
        for j in range(count_y)
    ]


VMEM = pl.BlockSpec(memory_space=pltpu.VMEM)
SMALL = pltpu.CompilerParams(vmem_limit_bytes=8 * 2**20)


def spread_out(values):
    return lax.broadcast_in_dim(values, values.shape + (ROWS, LANES), (0, 1))


def by_seat(entries):
    rounds, places, rows, lanes = entries.shape
    seat = lax.broadcasted_iota(jnp.int32, (rows, lanes), 1) // NZ
    value = entries[0, 0]
    for index in range(1, rounds * places):
        value = jnp.where(seat == index, entries[index // places, index % places], value)
    return value


def candidates_kernel(slots, orbitals, out):
    per_tile = LANES // NZ
    slot = by_seat(slots)[:EDGE]
    lane = lax.broadcasted_iota(jnp.int32, (EDGE, LANES), 1)
    group, turn = slot // per_tile, (lane // NZ - slot % per_tile + per_tile) % per_tile
    asked = [pltpu.roll(group, LANES - step * NZ, 1) if step else group for step in range(per_tile)]
    found = [[jnp.zeros((EDGE, LANES), jnp.float32)] * EDGE for _ in range(per_tile)]
    for number in range(ROWS):
        lanes = pl.ds(number * LANES, LANES)
        tiles = [orbitals[row, :, lanes].astype(jnp.float32) for row in range(EDGE)]
        for step in range(per_tile):
            here = asked[step] == number
            found[step] = [jnp.where(here, tile, old) for tile, old in zip(tiles, found[step])]
    rows = []
    for row in range(EDGE):
        packed = found[0][row]
        for step in range(1, per_tile):
            packed = jnp.where(turn == step, pltpu.roll(found[step][row], step * NZ, 1), packed)
        rows.append(packed)
    for tile in range(EDGE // 2):
        out[tile] = jnp.concatenate(rows[2 * tile : 2 * tile + 2], axis=0).astype(jnp.bfloat16)


def candidates(slots, orbitals):
    return pl.pallas_call(
        candidates_kernel,
        out_shape=jax.ShapeDtypeStruct((EDGE * EDGE // ROWS, ROWS, LANES), jnp.bfloat16),
        in_specs=[VMEM] * 2,
        out_specs=VMEM,
        compiler_params=SMALL,
        name="candidates",
    )(slots, orbitals)


def cells_kernel(orbitals, out, scratch):
    for row in range(EDGE):
        for group in range(ROWS):
            tile = orbitals[row, :, pl.ds(group * LANES, LANES)].astype(jnp.float32)
            scratch[row, pl.ds(group, EDGE, stride=ROWS + 1), :] = tile
    for row in range(EDGE):
        for y in range(EDGE):
            tile = scratch[row, pl.ds(y * (ROWS + 1), ROWS), :]
            out[row * EDGE + y] = tile.astype(jnp.bfloat16)


def cells_of(orbitals):
    return pl.pallas_call(
        cells_kernel,
        out_shape=jax.ShapeDtypeStruct((EDGE * EDGE, ROWS, LANES), jnp.bfloat16),
        in_specs=[VMEM],
        out_specs=VMEM,
        scratch_shapes=[pltpu.VMEM((EDGE, EDGE * (ROWS + 1), LANES), jnp.float32)],
        compiler_params=SMALL,
        cost_estimate=pl.CostEstimate(flops=0, bytes_accessed=4 * 2**20, transcendentals=0),
        name="cells",
    )(orbitals)


def chosen(owners, mine, others, bit):
    owner, me = by_seat(owners), lax.axis_index("orb")
    count = lax.axis_size("orb")
    picked = []
    for tile in range(mine.shape[0]):
        value = mine[tile].astype(jnp.float32)
        for step, other in enumerate(others, 1):
            if bit is None:
                here = owner == lax.rem(me + count - step, count)
            else:
                here = (owner >> bit & 1) != (me >> bit & 1)
            value = jnp.where(here, other[tile].astype(jnp.float32), value)
        picked.append(value)
    return picked


def nearer_kernel(bit, owners, mine, other, out):
    for tile, value in enumerate(chosen(owners, mine, [other], bit)):
        out[tile] = value.astype(jnp.bfloat16)


def gathered(owners, mine):
    count = lax.axis_size("orb")
    if count & (count - 1):
        others = [lax.ppermute(mine, "orb", ring("orb", step)) for step in range(1, count)]
        return mine, others, None
    bits = count.bit_length() - 1
    for bit in range(bits):
        other = lax.ppermute(mine, "orb", [(i, i ^ 1 << bit) for i in range(count)])
        if bit == bits - 1:
            return mine, [other], bit
        mine = pl.pallas_call(
            functools.partial(nearer_kernel, bit),
            out_shape=jax.ShapeDtypeStruct(mine.shape, mine.dtype),
            in_specs=[VMEM] * 3,
            out_specs=VMEM,
            compiler_params=SMALL,
            name="nearer",
        )(owners, mine, other)
    return mine, [], None


def messages_kernel(bit, owners, cells, mine, *refs):
    others, (block, last, first, corner_low, corner_high) = refs[:-5], refs[-5:]
    picked = chosen(owners, mine, others, bit)

    def pack(ref, spots):
        for at, (x, y) in enumerate(spots):
            ref[at] = cells[x * EDGE + y]
        used = len(spots)
        runs = []
        for x, y in spots:
            if runs and runs[-1][0] == x and runs[-1][2] == y:
                runs[-1][2] = y + 1
            else:
                runs.append([x, y, y + 1])
        parts = [
            picked[x * EDGE // ROWS][x * EDGE % ROWS + low : x * EDGE % ROWS + high]
            for x, low, high in runs
        ]
        if used % ROWS:
            parts.append(jnp.zeros((ROWS - used % ROWS, LANES), jnp.float32))
        rows = jnp.concatenate(parts, axis=0).astype(jnp.bfloat16)
        for tile in range(rows.shape[0] // ROWS):
            ref[used + tile] = rows[tile * ROWS : (tile + 1) * ROWS]

    pack(block, [(x, y) for x in range(EDGE) for y in range(EDGE)])
    pack(last, [(x, y) for x in range(EDGE) for y in range(EDGE - HALO, EDGE)])
    pack(first, [(x, y) for x in range(EDGE) for y in range(HALO)])
    pack(corner_low, CORNER_LOW)
    pack(corner_high, CORNER_HIGH)


def tiles(spots):
    return spots + -(-spots // ROWS)


def messages(orbitals, src_owner, src_slot):
    owners = spread_out(src_owner)
    mine, others, bit = gathered(owners, candidates(spread_out(src_slot), orbitals))
    lengths = [EDGE * EDGE] + [EDGE * HALO] * 2 + [len(CORNER_LOW)] * 2
    return pl.pallas_call(
        functools.partial(messages_kernel, bit),
        out_shape=[
            jax.ShapeDtypeStruct((tiles(length), ROWS, LANES), jnp.bfloat16) for length in lengths
        ],
        in_specs=[VMEM] * (3 + len(others)),
        out_specs=[VMEM] * 5,
        compiler_params=SMALL,
        name="messages",
    )(owners, cells_of(orbitals), mine, *others)


def exchange(block, last, first, corner_low, corner_high):
    both = ("sx", "sy")
    if lax.axis_size("sx") == 2:
        low = lax.ppermute(corner_low, both, diagonal(1, 1))
        high = lax.ppermute(corner_high, both, diagonal(1, -1))
        across = lax.ppermute(block, "sx", ring("sx", 1))
    else:
        def two_ways(cells, half, axes, down, up, merge):
            end = 2 * half
            back = lax.ppermute(jnp.concatenate([cells[:half], cells[end:]]), axes, down)
            ahead = lax.ppermute(jnp.concatenate([cells[half:end], cells[end:]]), axes, up)
            return jnp.concatenate([back[:half], ahead[:half], merge(back[half:], ahead[half:])])

        def halves(back, ahead):
            return jnp.concatenate([back[: back.shape[0] // 2], ahead[ahead.shape[0] // 2 :]])

        def rows(back, ahead):
            return jnp.concatenate([back[:, :SPLIT], ahead[:, SPLIT:]], axis=1)

        low = two_ways(corner_low, SPLIT, both, diagonal(-1, 1), diagonal(1, 1), rows)
        high = two_ways(corner_high, SPLIT, both, diagonal(-1, -1), diagonal(1, -1), rows)
        across = two_ways(block, EDGE * HALO, "sx", ring("sx", -1), ring("sx", 1), halves)
    below = lax.ppermute(last, "sy", ring("sy", 1))
    above = lax.ppermute(first, "sy", ring("sy", -1))
    return across, below, above, low, high


def place_of(x, y):
    row, core_x = (x - HALO) % EDGE, HALO <= x < HALO + EDGE
    if HALO <= y < HALO + EDGE:
        return (0 if core_x else 1), row * EDGE + y - HALO
    if y < HALO:
        return (2, row * HALO + y) if core_x else (4, CORNER_LOW.index((row, y + EDGE - HALO)))
    y = y - HALO - EDGE
    return (3, row * HALO + y) if core_x else (5, CORNER_HIGH.index((row, y)))


def reach(x, y):
    out_x = max(HALO - x, x - (HALO + EDGE - 1), 0)
    out_y = max(HALO - y, y - (HALO + EDGE - 1), 0)
    return out_x + out_y


def z_modes():
    index = np.arange(1, NZ + 1)
    modes = np.sqrt(2.0 / (NZ + 1)) * np.sin(np.pi * np.outer(index, index) / (NZ + 1))
    modes = np.kron(np.eye(LANES // NZ), modes)
    high = modes.astype(ml_dtypes.bfloat16)
    low = (modes - high.astype(np.float64)).astype(ml_dtypes.bfloat16)
    both = np.concatenate([high, low], axis=1)
    value = np.tile(2.0 * np.cos(np.pi * index / (NZ + 1)), LANES // NZ)
    p0, p1, p2, p3, p4 = power_coeffs()
    a3, a2, a1, a0 = p3 / p4, p2 / p4, p1 / p4, p0 / p4
    tail = [
        4.0 * value + a3,
        6.0 * value**2 + 3.0 * a3 * value + a2,
        4.0 * value**3 + 3.0 * a3 * value**2 + 2.0 * a2 * value + a1,
        value**4 + a3 * value**3 + a2 * value**2 + a1 * value + a0,
    ]
    tail = np.repeat(np.stack(tail)[:, None, :], SUB, axis=1).astype(np.float32)
    return np.concatenate([both, both], axis=0), tail


SIZE = 2 * HALO + EDGE


def within(radius):
    return [[y for y in range(SIZE) if reach(x, y) <= radius] for x in range(SIZE)]


CELLS = [(x, y) for x in range(SIZE) for y in within(HALO)[x]]
CORE = [(x, y) for x in range(HALO, HALO + EDGE) for y in range(HALO, HALO + EDGE)]


def kernel(count, *refs):
    halo, modes, tails = refs[:6], refs[6], refs[7]
    out, rows_of, parts, hat, work_a, work_b, last, acc = refs[8:]
    pitch = ROWS + 1
    number = {cell: at for at, cell in enumerate(CELLS)}

    shape = (LANES, LANES)
    lane = lax.broadcasted_iota(jnp.int32, shape, 1) % NZ
    line = lax.broadcasted_iota(jnp.int32, shape, 0)
    repeats = [(line == lane + place * NZ).astype(jnp.bfloat16) for place in range(count)]
    first_row = []
    total = 0
    for ref in halo:
        packed = ref[ref.shape[0] * ROWS // (ROWS + 1) :].reshape(-1, LANES)
        first_row.append(total)
        for place, repeat in enumerate(repeats):
            rows_of[place, pl.ds(total, packed.shape[0]), :] = jnp.dot(
                packed, repeat, preferred_element_type=jnp.float32
            )
        total += packed.shape[0]

    def spread(place, x, y):
        which, at = place_of(x, y)
        row = rows_of[place, pl.ds(first_row[which] + at, 1), :]
        return jnp.broadcast_to(row, (ROWS, LANES))

    def keep(at, value):
        high = value.astype(jnp.bfloat16)
        low = (value - high.astype(jnp.float32)).astype(jnp.bfloat16)
        parts[at, :, :LANES] = high
        parts[at, :, LANES:] = low

    def turned(first, end):
        cells = end - first
        rows = parts[first:end].reshape(cells * ROWS, 2 * LANES)
        both = jnp.dot(rows, modes[...], preferred_element_type=jnp.float32)
        return (both[:, :LANES] + both[:, LANES:]).reshape(cells, ROWS, LANES)

    def one_half(half):
        rows = pl.ds(half * SUB, SUB)

        def start(x, y):
            return hat[number[x, y], rows, :]

        for step in range(DEGREE):
            new = (work_a, work_b, work_a, None)[step]
            old = (None, work_a, work_b, work_a)[step]
            targets, known = within(HALO - 1 - step), within(HALO - step)

            def load(x):
                return {y: start(x, y) if old is None else old[x, y] for y in known[x]}

            here, pair_prev = load(0), {}
            for x in range(SIZE - 1):
                ahead = load(x + 1)
                pair = {}
                for y in range(SIZE - 1):
                    if y in targets[x] or y + 1 in targets[x + 1]:
                        pair[y] = ahead[y] + here[y + 1]
                    if y in targets[x]:
                        density = here[y] if old is None else start(x, y)
                        value = pair[y] + pair_prev[y - 1] + tails[step] * density
                        if new is not None:
                            new[x, y] = value
                        else:
                            last[CORE.index((x, y)), rows, :] = value
                here, pair_prev = ahead, pair

    def one_source(place, carry):
        chunk = len(CELLS) // 4
        for first in range(0, len(CELLS), chunk):
            end = min(first + chunk, len(CELLS))
            for at in range(first, end):
                which, spot = place_of(*CELLS[at])
                keep(at, halo[which][spot].astype(jnp.float32) * spread(place, *CELLS[at]))
            hat[first:end] = turned(first, end)
        for half in range(ROWS // SUB):
            one_half(half)
        for at in range(len(CORE)):
            keep(at, last[at])
        back = turned(0, len(CORE))
        for at, (x, y) in enumerate(CORE):
            rows = pl.ds((y - HALO) * pitch, ROWS)
            acc[x - HALO, rows, :] = acc[x - HALO, rows, :] + back[at] * spread(place, x, y)
        return carry

    acc[...] = jnp.zeros(acc.shape, jnp.float32)
    lax.fori_loop(0, count, one_source, 0)
    for x in range(EDGE):
        for group in range(ROWS):
            tile = acc[x, pl.ds(group, EDGE, stride=pitch), :]
            out[x, :, pl.ds(group * LANES, LANES)] = tile * (-power_coeffs()[-1])


def fields(halo, count):
    plane = pltpu.VMEM((SIZE, SIZE, SUB, LANES), jnp.float32)
    rows = sum(array.shape[0] * ROWS // (ROWS + 1) + ROWS for array in halo)
    modes, tails = z_modes()
    return pl.pallas_call(
        functools.partial(kernel, count),
        out_shape=jax.ShapeDtypeStruct((EDGE, EDGE, ROWS * LANES), jnp.float32),
        in_specs=[VMEM] * 8,
        out_specs=VMEM,
        scratch_shapes=[
            pltpu.VMEM((count, rows, LANES), jnp.float32),
            pltpu.VMEM((len(CELLS), ROWS, 2 * LANES), jnp.bfloat16),
            pltpu.VMEM((len(CELLS), ROWS, LANES), jnp.float32),
            plane,
            plane,
            pltpu.VMEM((len(CORE), ROWS, LANES), jnp.float32),
            pltpu.VMEM((EDGE, EDGE * (ROWS + 1), LANES), jnp.float32),
        ],
        compiler_params=pltpu.CompilerParams(vmem_limit_bytes=24 * 2**20),
        name="fields",
    )(*halo, modes, tails)


def body(orbitals, src_owner, src_slot):
    packed = messages(orbitals, src_owner, src_slot)
    return fields((packed[0], *exchange(*packed)), src_slot.size)


def solution(mesh):
    in_specs = (P("sx", "sy", "orb"), P(), P())
    out_specs = P("sx", "sy", "orb")
    return jax.shard_map(body, mesh=mesh, in_specs=in_specs, out_specs=out_specs, check_vma=False)
```

```python
import functools

import jax
import jax.numpy as jnp
import ml_dtypes
import numpy as np
from jax import lax
from jax.experimental import pallas as pl
from jax.experimental.pallas import tpu as pltpu
from jax.sharding import PartitionSpec as P

NZ = 32
LANES = 128
SUB = 8
ROWS = 16
DEGREE = 4
HALO = DEGREE
EDGE = 8

CHEB = (
    1.021021021021021,
    -1.7357357357357357,
    1.4753753753753753,
    -1.254069069069069,
    1.0659587087087088,
)


def power_coeffs():
    c0, c1, c2, c3, c4 = CHEB
    return (
        c0 - c2 + c4,
        -(c1 - 3.0 * c3) / 6.0,
        (2.0 * c2 - 8.0 * c4) / 36.0,
        -4.0 * c3 / 216.0,
        8.0 * c4 / 1296.0,
    )


CORNER_LOW = tuple(
    (x, y)
    for x in range(EDGE)
    for y in range(EDGE - HALO, EDGE)
    if min(x + 1, EDGE - x) + EDGE - y <= DEGREE
)
CORNER_HIGH = tuple((x, EDGE - 1 - y) for x, y in CORNER_LOW)
SPLIT = len(CORNER_LOW) // 2


def ring(axis, step):
    count = lax.axis_size(axis)
    return [(i, (i + step) % count) for i in range(count)]


def diagonal(step_x, step_y):
    count_x, count_y = lax.axis_size("sx"), lax.axis_size("sy")
    return [
        (i * count_y + j, (i + step_x) % count_x * count_y + (j + step_y) % count_y)
        for i in range(count_x)
        for j in range(count_y)
    ]


VMEM = pl.BlockSpec(memory_space=pltpu.VMEM)
SMALL = pltpu.CompilerParams(vmem_limit_bytes=8 * 2**20)


def spread_out(values):
    return lax.broadcast_in_dim(values, values.shape + (ROWS, LANES), (0, 1))


def by_seat(entries):
    rounds, places, rows, lanes = entries.shape
    seat = lax.broadcasted_iota(jnp.int32, (rows, lanes), 1) // NZ
    value = entries[0, 0]
    for index in range(1, rounds * places):
        value = jnp.where(seat == index, entries[index // places, index % places], value)
    return value


def candidates_kernel(slots, orbitals, out):
    per_tile = LANES // NZ
    slot = by_seat(slots)[:EDGE]
    lane = lax.broadcasted_iota(jnp.int32, (EDGE, LANES), 1)
    group, turn = slot // per_tile, (lane // NZ - slot % per_tile + per_tile) % per_tile
    asked = [pltpu.roll(group, LANES - step * NZ, 1) if step else group for step in range(per_tile)]
    found = [[jnp.zeros((EDGE, LANES), jnp.float32)] * EDGE for _ in range(per_tile)]
    for number in range(ROWS):
        lanes = pl.ds(number * LANES, LANES)
        tiles = [orbitals[row, :, lanes].astype(jnp.float32) for row in range(EDGE)]
        for step in range(per_tile):
            here = asked[step] == number
            found[step] = [jnp.where(here, tile, old) for tile, old in zip(tiles, found[step])]
    rows = []
    for row in range(EDGE):
        packed = found[0][row]
        for step in range(1, per_tile):
            packed = jnp.where(turn == step, pltpu.roll(found[step][row], step * NZ, 1), packed)
        rows.append(packed)
    for tile in range(EDGE // 2):
        out[tile] = jnp.concatenate(rows[2 * tile : 2 * tile + 2], axis=0).astype(jnp.bfloat16)


def candidates(slots, orbitals):
    return pl.pallas_call(
        candidates_kernel,
        out_shape=jax.ShapeDtypeStruct((EDGE * EDGE // ROWS, ROWS, LANES), jnp.bfloat16),
        in_specs=[VMEM] * 2,
        out_specs=VMEM,
        compiler_params=SMALL,
        name="candidates",
    )(slots, orbitals)


def cells_kernel(orbitals, out, scratch):
    for row in range(EDGE):
        for group in range(ROWS):
            tile = orbitals[row, :, pl.ds(group * LANES, LANES)].astype(jnp.float32)
            scratch[row, pl.ds(group, EDGE, stride=ROWS + 1), :] = tile
    for row in range(EDGE):
        for y in range(EDGE):
            tile = scratch[row, pl.ds(y * (ROWS + 1), ROWS), :]
            out[row * EDGE + y] = tile.astype(jnp.bfloat16)


def cells_of(orbitals):
    return pl.pallas_call(
        cells_kernel,
        out_shape=jax.ShapeDtypeStruct((EDGE * EDGE, ROWS, LANES), jnp.bfloat16),
        in_specs=[VMEM],
        out_specs=VMEM,
        scratch_shapes=[pltpu.VMEM((EDGE, EDGE * (ROWS + 1), LANES), jnp.float32)],
        compiler_params=SMALL,
        cost_estimate=pl.CostEstimate(flops=0, bytes_accessed=4 * 2**20, transcendentals=0),
        name="cells",
    )(orbitals)


def chosen(owners, mine, others, bit):
    owner, me = by_seat(owners), lax.axis_index("orb")
    count = lax.axis_size("orb")
    picked = []
    for tile in range(mine.shape[0]):
        value = mine[tile].astype(jnp.float32)
        for step, other in enumerate(others, 1):
            if bit is None:
                here = owner == lax.rem(me + count - step, count)
            else:
                here = (owner >> bit & 1) != (me >> bit & 1)
            value = jnp.where(here, other[tile].astype(jnp.float32), value)
        picked.append(value)
    return picked


def nearer_kernel(bit, owners, mine, other, out):
    for tile, value in enumerate(chosen(owners, mine, [other], bit)):
        out[tile] = value.astype(jnp.bfloat16)


def gathered(owners, mine):
    count = lax.axis_size("orb")
    if count & (count - 1):
        others = [lax.ppermute(mine, "orb", ring("orb", step)) for step in range(1, count)]
        return mine, others, None
    bits = count.bit_length() - 1
    for bit in range(bits):
        other = lax.ppermute(mine, "orb", [(i, i ^ 1 << bit) for i in range(count)])
        if bit == bits - 1:
            return mine, [other], bit
        mine = pl.pallas_call(
            functools.partial(nearer_kernel, bit),
            out_shape=jax.ShapeDtypeStruct(mine.shape, mine.dtype),
            in_specs=[VMEM] * 3,
            out_specs=VMEM,
            compiler_params=SMALL,
            name="nearer",
        )(owners, mine, other)
    return mine, [], None


def messages_kernel(bit, owners, cells, mine, *refs):
    others, (block, last, first, corner_low, corner_high) = refs[:-5], refs[-5:]
    picked = chosen(owners, mine, others, bit)

    def pack(ref, spots):
        for at, (x, y) in enumerate(spots):
            ref[at] = cells[x * EDGE + y]
        used = len(spots)
        runs = []
        for x, y in spots:
            if runs and runs[-1][0] == x and runs[-1][2] == y:
                runs[-1][2] = y + 1
            else:
                runs.append([x, y, y + 1])
        parts = [
            picked[x * EDGE // ROWS][x * EDGE % ROWS + low : x * EDGE % ROWS + high]
            for x, low, high in runs
        ]
        if used % ROWS:
            parts.append(jnp.zeros((ROWS - used % ROWS, LANES), jnp.float32))
        rows = jnp.concatenate(parts, axis=0).astype(jnp.bfloat16)
        for tile in range(rows.shape[0] // ROWS):
            ref[used + tile] = rows[tile * ROWS : (tile + 1) * ROWS]

    pack(block, [(x, y) for x in range(EDGE) for y in range(EDGE)])
    pack(last, [(x, y) for x in range(EDGE) for y in range(EDGE - HALO, EDGE)])
    pack(first, [(x, y) for x in range(EDGE) for y in range(HALO)])
    pack(corner_low, CORNER_LOW)
    pack(corner_high, CORNER_HIGH)


def tiles(spots):
    return spots + -(-spots // ROWS)


def spots_of(length):
    return length * ROWS // (ROWS + 1)


def messages(orbitals, src_owner, src_slot):
    owners = spread_out(src_owner)
    mine, others, bit = gathered(owners, candidates(spread_out(src_slot), orbitals))
    lengths = [EDGE * EDGE] + [EDGE * HALO] * 2 + [len(CORNER_LOW)] * 2
    return pl.pallas_call(
        functools.partial(messages_kernel, bit),
        out_shape=[
            jax.ShapeDtypeStruct((tiles(length), ROWS, LANES), jnp.bfloat16) for length in lengths
        ],
        in_specs=[VMEM] * (3 + len(others)),
        out_specs=[VMEM] * 5,
        compiler_params=SMALL,
        name="messages",
    )(owners, cells_of(orbitals), mine, *others)


def exchange(block, last, first, corner_low, corner_high):
    both = ("sx", "sy")
    if lax.axis_size("sx") == 2:
        low = lax.ppermute(corner_low, both, diagonal(1, 1))
        high = lax.ppermute(corner_high, both, diagonal(1, -1))
        across = lax.ppermute(block, "sx", ring("sx", 1))
    else:
        def two_ways(cells, half, axes, down, up, merge):
            end = 2 * half
            back = lax.ppermute(jnp.concatenate([cells[:half], cells[end:]]), axes, down)
            ahead = lax.ppermute(jnp.concatenate([cells[half:end], cells[end:]]), axes, up)
            return jnp.concatenate([back[:half], ahead[:half], merge(back[half:], ahead[half:])])

        def halves(back, ahead):
            return jnp.concatenate([back[: back.shape[0] // 2], ahead[ahead.shape[0] // 2 :]])

        def rows(back, ahead):
            return jnp.concatenate([back[:, :SPLIT], ahead[:, SPLIT:]], axis=1)

        low = two_ways(corner_low, SPLIT, both, diagonal(-1, 1), diagonal(1, 1), rows)
        high = two_ways(corner_high, SPLIT, both, diagonal(-1, -1), diagonal(1, -1), rows)
        across = two_ways(block, EDGE * HALO, "sx", ring("sx", -1), ring("sx", 1), halves)
    below = lax.ppermute(last, "sy", ring("sy", 1))
    above = lax.ppermute(first, "sy", ring("sy", -1))
    return across, below, above, low, high


def place_of(x, y):
    row, core_x = (x - HALO) % EDGE, HALO <= x < HALO + EDGE
    if HALO <= y < HALO + EDGE:
        return (0 if core_x else 1), row * EDGE + y - HALO
    if y < HALO:
        return (2, row * HALO + y) if core_x else (4, CORNER_LOW.index((row, y + EDGE - HALO)))
    y = y - HALO - EDGE
    return (3, row * HALO + y) if core_x else (5, CORNER_HIGH.index((row, y)))


def reach(x, y):
    out_x = max(HALO - x, x - (HALO + EDGE - 1), 0)
    out_y = max(HALO - y, y - (HALO + EDGE - 1), 0)
    return out_x + out_y


def z_modes():
    index = np.arange(1, NZ + 1)
    modes = np.sqrt(2.0 / (NZ + 1)) * np.sin(np.pi * np.outer(index, index) / (NZ + 1))
    modes = np.kron(np.eye(LANES // NZ), modes)
    high = modes.astype(ml_dtypes.bfloat16)
    low = (modes - high.astype(np.float64)).astype(ml_dtypes.bfloat16)
    both = np.concatenate([high, low], axis=1)
    value = np.tile(2.0 * np.cos(np.pi * index / (NZ + 1)), LANES // NZ)
    p0, p1, p2, p3, p4 = power_coeffs()
    a3, a2, a1, a0 = p3 / p4, p2 / p4, p1 / p4, p0 / p4
    tail = [
        4.0 * value + a3,
        6.0 * value**2 + 3.0 * a3 * value + a2,
        4.0 * value**3 + 3.0 * a3 * value**2 + 2.0 * a2 * value + a1,
        value**4 + a3 * value**3 + a2 * value**2 + a1 * value + a0,
    ]
    tail = np.repeat(np.stack(tail)[:, None, :], SUB, axis=1).astype(np.float32)
    return np.concatenate([both, both], axis=0), tail


SIZE = 2 * HALO + EDGE


def within(radius):
    return [[y for y in range(SIZE) if reach(x, y) <= radius] for x in range(SIZE)]


CORE = [(x, y) for x in range(HALO, HALO + EDGE) for y in range(HALO, HALO + EDGE)]


def source_rows(ref, out, first):
    shape = (LANES, LANES)
    lane = lax.broadcasted_iota(jnp.int32, shape, 1) % NZ
    line = lax.broadcasted_iota(jnp.int32, shape, 0)
    packed = ref[spots_of(ref.shape[0]) :].reshape(-1, LANES)
    for place in range(out.shape[0]):
        repeat = (line == lane + place * NZ).astype(jnp.bfloat16)
        out[place, pl.ds(first, packed.shape[0]), :] = jnp.dot(
            packed, repeat, preferred_element_type=jnp.float32
        )
    return first + packed.shape[0]


def keep(parts, at, value):
    high = value.astype(jnp.bfloat16)
    low = (value - high.astype(jnp.float32)).astype(jnp.bfloat16)
    parts[at, :, :LANES] = high
    parts[at, :, LANES:] = low


def turned(parts, first, end, modes):
    cells = end - first
    rows = parts[first:end].reshape(cells * ROWS, 2 * LANES)
    both = jnp.dot(rows, modes[...], preferred_element_type=jnp.float32)
    return (both[:, :LANES] + both[:, LANES:]).reshape(cells, ROWS, LANES)


def densities(refs, rows, firsts, place, parts, modes, put):
    cells = [(ref, at, first + at) for ref, first in zip(refs, firsts) for at in range(spots_of(ref.shape[0]))]
    chunk = 48
    for start in range(0, len(cells), chunk):
        end = min(start + chunk, len(cells))
        for number in range(start, end):
            ref, at, row = cells[number]
            other = jnp.broadcast_to(rows[place, pl.ds(row, 1), :], (ROWS, LANES))
            keep(parts, number, ref[at].astype(jnp.float32) * other)
        put(start, end, turned(parts, start, end, modes))


def modes_kernel(count, *refs):
    halo, modes, (hat, own_rows, rows, parts) = refs[:4], refs[4], refs[5:]
    firsts = [0]
    for ref in halo:
        firsts.append(source_rows(ref, rows, firsts[-1]))
    own_rows[...] = rows[:, : own_rows.shape[1], :]

    def one_source(place, carry):
        def put(start, end, value):
            hat[place, start:end] = value

        densities(halo, rows, firsts, place, parts, modes, put)
        return carry

    lax.fori_loop(0, count, one_source, 0)


def modes_of(halo, modes, count):
    cells = sum(spots_of(array.shape[0]) for array in halo)
    return pl.pallas_call(
        functools.partial(modes_kernel, count),
        out_shape=[
            jax.ShapeDtypeStruct((count, cells, ROWS, LANES), jnp.float32),
            jax.ShapeDtypeStruct((count, len(CORE), LANES), jnp.float32),
        ],
        in_specs=[VMEM] * 5,
        out_specs=[VMEM] * 2,
        scratch_shapes=[
            pltpu.VMEM((count, cells, LANES), jnp.float32),
            pltpu.VMEM((cells, ROWS, 2 * LANES), jnp.bfloat16),
        ],
        compiler_params=pltpu.CompilerParams(vmem_limit_bytes=20 * 2**20),
        cost_estimate=pl.CostEstimate(flops=0, bytes_accessed=8 * 2**20, transcendentals=0),
        name="modes",
    )(*halo, modes)


def fields_kernel(count, beside, own_rows, low, high, modes, tails, *refs):
    out, rows, parts, corners, work_a, work_b, last, acc = refs
    pitch = ROWS + 1
    offset = (0, EDGE * EDGE, 2 * EDGE * EDGE, 2 * EDGE * EDGE + EDGE * HALO)

    firsts = [0, source_rows(low, rows, 0)]
    source_rows(high, rows, firsts[1])
    for place in range(count):

        def put(start, end, value, place=place):
            corners[place, start:end] = value

        densities((low, high), rows, firsts, place, parts, modes, put)

    def spread(place, at):
        return jnp.broadcast_to(own_rows[place, pl.ds(at, 1), :], (ROWS, LANES))

    def one_half(place, half):
        rows = pl.ds(half * SUB, SUB)

        def start(x, y):
            which, at = place_of(x, y)
            if which < 4:
                return beside[place, offset[which] + at, rows, :]
            return corners[place, (which - 4) * len(CORNER_LOW) + at, rows, :]

        for step in range(DEGREE):
            new = (work_a, work_b, work_a, None)[step]
            old = (None, work_a, work_b, work_a)[step]
            targets, known = within(HALO - 1 - step), within(HALO - step)

            def load(x):
                return {y: start(x, y) if old is None else old[x, y] for y in known[x]}

            here, pair_prev = load(0), {}
            for x in range(SIZE - 1):
                ahead = load(x + 1)
                pair = {}
                for y in range(SIZE - 1):
                    if y in targets[x] or y + 1 in targets[x + 1]:
                        pair[y] = ahead[y] + here[y + 1]
                    if y in targets[x]:
                        density = here[y] if old is None else start(x, y)
                        value = pair[y] + pair_prev[y - 1] + tails[step] * density
                        if new is not None:
                            new[x, y] = value
                        else:
                            last[CORE.index((x, y)), rows, :] = value
                here, pair_prev = ahead, pair

    def one_source(place, carry):
        for half in range(ROWS // SUB):
            one_half(place, half)
        for at in range(len(CORE)):
            keep(parts, at, last[at])
        back = turned(parts, 0, len(CORE), modes)
        for at, (x, y) in enumerate(CORE):
            rows = pl.ds((y - HALO) * pitch, ROWS)
            acc[x - HALO, rows, :] = acc[x - HALO, rows, :] + back[at] * spread(place, at)
        return carry

    acc[...] = jnp.zeros(acc.shape, jnp.float32)
    lax.fori_loop(0, count, one_source, 0)
    for x in range(EDGE):
        for group in range(ROWS):
            tile = acc[x, pl.ds(group, EDGE, stride=pitch), :]
            out[x, :, pl.ds(group * LANES, LANES)] = tile * (-power_coeffs()[-1])


def fields(halo, count):
    plane = pltpu.VMEM((SIZE, SIZE, SUB, LANES), jnp.float32)
    modes, tails = z_modes()
    beside, own_rows = modes_of(halo[:4], modes, count)
    corners = 2 * len(CORNER_LOW)
    return pl.pallas_call(
        functools.partial(fields_kernel, count),
        out_shape=jax.ShapeDtypeStruct((EDGE, EDGE, ROWS * LANES), jnp.float32),
        in_specs=[VMEM] * 6,
        out_specs=VMEM,
        scratch_shapes=[
            pltpu.VMEM((count, 2 * ROWS, LANES), jnp.float32),
            pltpu.VMEM((len(CORE), ROWS, 2 * LANES), jnp.bfloat16),
            pltpu.VMEM((count, corners, ROWS, LANES), jnp.float32),
            plane,
            plane,
            pltpu.VMEM((len(CORE), ROWS, LANES), jnp.float32),
            pltpu.VMEM((EDGE, EDGE * (ROWS + 1), LANES), jnp.float32),
        ],
        compiler_params=pltpu.CompilerParams(vmem_limit_bytes=24 * 2**20),
        name="fields",
    )(beside, own_rows, *halo[4:], modes, tails)


def body(orbitals, src_owner, src_slot):
    packed = messages(orbitals, src_owner, src_slot)
    return fields((packed[0], *exchange(*packed)), src_slot.size)


def solution(mesh):
    in_specs = (P("sx", "sy", "orb"), P(), P())
    out_specs = P("sx", "sy", "orb")
    return jax.shard_map(body, mesh=mesh, in_specs=in_specs, out_specs=out_specs, check_vma=False)
```

```python
import functools

import jax
import jax.numpy as jnp
import ml_dtypes
import numpy as np
from jax import lax
from jax.experimental import pallas as pl
from jax.experimental.pallas import tpu as pltpu
from jax.sharding import PartitionSpec as P

NZ = 32
LANES = 128
SUB = 8
ROWS = 16
DEGREE = 4
HALO = DEGREE
EDGE = 8

CHEB = (
    1.021021021021021,
    -1.7357357357357357,
    1.4753753753753753,
    -1.254069069069069,
    1.0659587087087088,
)


def power_coeffs():
    c0, c1, c2, c3, c4 = CHEB
    return (
        c0 - c2 + c4,
        -(c1 - 3.0 * c3) / 6.0,
        (2.0 * c2 - 8.0 * c4) / 36.0,
        -4.0 * c3 / 216.0,
        8.0 * c4 / 1296.0,
    )


CORNER_LOW = tuple(
    (x, y)
    for x in range(EDGE)
    for y in range(EDGE - HALO, EDGE)
    if min(x + 1, EDGE - x) + EDGE - y <= DEGREE
)
CORNER_HIGH = tuple((x, EDGE - 1 - y) for x, y in CORNER_LOW)
SPLIT = len(CORNER_LOW) // 2


def ring(axis, step):
    count = lax.axis_size(axis)
    return [(i, (i + step) % count) for i in range(count)]


def diagonal(step_x, step_y):
    count_x, count_y = lax.axis_size("sx"), lax.axis_size("sy")
    return [
        (i * count_y + j, (i + step_x) % count_x * count_y + (j + step_y) % count_y)
        for i in range(count_x)
        for j in range(count_y)
    ]


VMEM = pl.BlockSpec(memory_space=pltpu.VMEM)
SMALL = pltpu.CompilerParams(vmem_limit_bytes=8 * 2**20)


def spread_out(values):
    return lax.broadcast_in_dim(values, values.shape + (ROWS, LANES), (0, 1))


def by_seat(entries):
    rounds, places, rows, lanes = entries.shape
    seat = lax.broadcasted_iota(jnp.int32, (rows, lanes), 1) // NZ
    value = entries[0, 0]
    for index in range(1, rounds * places):
        value = jnp.where(seat == index, entries[index // places, index % places], value)
    return value


def candidates_kernel(slots, orbitals, out):
    per_tile = LANES // NZ
    slot = by_seat(slots)[:EDGE]
    lane = lax.broadcasted_iota(jnp.int32, (EDGE, LANES), 1)
    group, turn = slot // per_tile, (lane // NZ - slot % per_tile + per_tile) % per_tile
    asked = [pltpu.roll(group, LANES - step * NZ, 1) if step else group for step in range(per_tile)]
    found = [[jnp.zeros((EDGE, LANES), jnp.float32)] * EDGE for _ in range(per_tile)]
    for number in range(ROWS):
        lanes = pl.ds(number * LANES, LANES)
        tiles = [orbitals[row, :, lanes].astype(jnp.float32) for row in range(EDGE)]
        for step in range(per_tile):
            here = asked[step] == number
            found[step] = [jnp.where(here, tile, old) for tile, old in zip(tiles, found[step])]
    rows = []
    for row in range(EDGE):
        packed = found[0][row]
        for step in range(1, per_tile):
            packed = jnp.where(turn == step, pltpu.roll(found[step][row], step * NZ, 1), packed)
        rows.append(packed)
    for tile in range(EDGE // 2):
        pair = jnp.concatenate(rows[2 * tile : 2 * tile + 2], axis=0).astype(jnp.bfloat16)
        for target in range(out.shape[0]):
            out[target, tile] = pair


def candidates(slots, orbitals, count):
    return pl.pallas_call(
        candidates_kernel,
        out_shape=jax.ShapeDtypeStruct((count, EDGE * EDGE // ROWS, ROWS, LANES), jnp.bfloat16),
        in_specs=[VMEM] * 2,
        out_specs=VMEM,
        compiler_params=SMALL,
        name="candidates",
    )(slots, orbitals)


def cells_kernel(orbitals, out, scratch):
    for row in range(EDGE):
        for group in range(ROWS):
            tile = orbitals[row, :, pl.ds(group * LANES, LANES)].astype(jnp.float32)
            scratch[row, pl.ds(group, EDGE, stride=ROWS + 1), :] = tile
    for row in range(EDGE):
        for y in range(EDGE):
            tile = scratch[row, pl.ds(y * (ROWS + 1), ROWS), :]
            out[row * EDGE + y] = tile.astype(jnp.bfloat16)


def cells_of(orbitals):
    return pl.pallas_call(
        cells_kernel,
        out_shape=jax.ShapeDtypeStruct((EDGE * EDGE, ROWS, LANES), jnp.bfloat16),
        in_specs=[VMEM],
        out_specs=VMEM,
        scratch_shapes=[pltpu.VMEM((EDGE, EDGE * (ROWS + 1), LANES), jnp.float32)],
        compiler_params=SMALL,
        cost_estimate=pl.CostEstimate(flops=0, bytes_accessed=4 * 2**20, transcendentals=0),
        name="cells",
    )(orbitals)


def chosen(owners, offered):
    owner = by_seat(owners)
    picked = []
    for tile in range(offered.shape[1]):
        value = offered[0, tile].astype(jnp.float32)
        for holder in range(1, offered.shape[0]):
            value = jnp.where(owner == holder, offered[holder, tile].astype(jnp.float32), value)
        picked.append(value)
    return picked


def messages_kernel(owners, cells, offered, block, last, first, corner_low, corner_high):
    picked = chosen(owners, offered)

    def pack(ref, spots):
        for at, (x, y) in enumerate(spots):
            ref[at] = cells[x * EDGE + y]
        used = len(spots)
        runs = []
        for x, y in spots:
            if runs and runs[-1][0] == x and runs[-1][2] == y:
                runs[-1][2] = y + 1
            else:
                runs.append([x, y, y + 1])
        parts = [
            picked[x * EDGE // ROWS][x * EDGE % ROWS + low : x * EDGE % ROWS + high]
            for x, low, high in runs
        ]
        if used % ROWS:
            parts.append(jnp.zeros((ROWS - used % ROWS, LANES), jnp.float32))
        rows = jnp.concatenate(parts, axis=0).astype(jnp.bfloat16)
        for tile in range(rows.shape[0] // ROWS):
            ref[used + tile] = rows[tile * ROWS : (tile + 1) * ROWS]

    pack(block, [(x, y) for x in range(EDGE) for y in range(EDGE)])
    pack(last, [(x, y) for x in range(EDGE) for y in range(EDGE - HALO, EDGE)])
    pack(first, [(x, y) for x in range(EDGE) for y in range(HALO)])
    pack(corner_low, CORNER_LOW)
    pack(corner_high, CORNER_HIGH)


def tiles(spots):
    return spots + -(-spots // ROWS)


def messages(orbitals, src_owner, src_slot):
    count = lax.axis_size("orb")
    mine = candidates(spread_out(src_slot), orbitals, count)
    offered = lax.all_to_all(mine, "orb", 0, 0, tiled=True)
    lengths = [EDGE * EDGE] + [EDGE * HALO] * 2 + [len(CORNER_LOW)] * 2
    return pl.pallas_call(
        messages_kernel,
        out_shape=[
            jax.ShapeDtypeStruct((tiles(length), ROWS, LANES), jnp.bfloat16) for length in lengths
        ],
        in_specs=[VMEM] * 3,
        out_specs=[VMEM] * 5,
        compiler_params=SMALL,
        name="messages",
    )(spread_out(src_owner), cells_of(orbitals), offered)


def exchange(block, last, first, corner_low, corner_high):
    both = ("sx", "sy")
    if lax.axis_size("sx") == 2:
        low = lax.ppermute(corner_low, both, diagonal(1, 1))
        high = lax.ppermute(corner_high, both, diagonal(1, -1))
        across = lax.ppermute(block, "sx", ring("sx", 1))
    else:
        def two_ways(cells, half, axes, down, up, merge):
            end = 2 * half
            back = lax.ppermute(jnp.concatenate([cells[:half], cells[end:]]), axes, down)
            ahead = lax.ppermute(jnp.concatenate([cells[half:end], cells[end:]]), axes, up)
            return jnp.concatenate([back[:half], ahead[:half], merge(back[half:], ahead[half:])])

        def halves(back, ahead):
            return jnp.concatenate([back[: back.shape[0] // 2], ahead[ahead.shape[0] // 2 :]])

        def rows(back, ahead):
            return jnp.concatenate([back[:, :SPLIT], ahead[:, SPLIT:]], axis=1)

        low = two_ways(corner_low, SPLIT, both, diagonal(-1, 1), diagonal(1, 1), rows)
        high = two_ways(corner_high, SPLIT, both, diagonal(-1, -1), diagonal(1, -1), rows)
        across = two_ways(block, EDGE * HALO, "sx", ring("sx", -1), ring("sx", 1), halves)
    below = lax.ppermute(last, "sy", ring("sy", 1))
    above = lax.ppermute(first, "sy", ring("sy", -1))
    return across, below, above, low, high


def place_of(x, y):
    row, core_x = (x - HALO) % EDGE, HALO <= x < HALO + EDGE
    if HALO <= y < HALO + EDGE:
        return (0 if core_x else 1), row * EDGE + y - HALO
    if y < HALO:
        return (2, row * HALO + y) if core_x else (4, CORNER_LOW.index((row, y + EDGE - HALO)))
    y = y - HALO - EDGE
    return (3, row * HALO + y) if core_x else (5, CORNER_HIGH.index((row, y)))


def reach(x, y):
    out_x = max(HALO - x, x - (HALO + EDGE - 1), 0)
    out_y = max(HALO - y, y - (HALO + EDGE - 1), 0)
    return out_x + out_y


def z_modes():
    index = np.arange(1, NZ + 1)
    modes = np.sqrt(2.0 / (NZ + 1)) * np.sin(np.pi * np.outer(index, index) / (NZ + 1))
    modes = np.kron(np.eye(LANES // NZ), modes)
    high = modes.astype(ml_dtypes.bfloat16)
    low = (modes - high.astype(np.float64)).astype(ml_dtypes.bfloat16)
    both = np.concatenate([high, low], axis=1)
    value = np.tile(2.0 * np.cos(np.pi * index / (NZ + 1)), LANES // NZ)
    p0, p1, p2, p3, p4 = power_coeffs()
    a3, a2, a1, a0 = p3 / p4, p2 / p4, p1 / p4, p0 / p4
    tail = [
        4.0 * value + a3,
        6.0 * value**2 + 3.0 * a3 * value + a2,
        4.0 * value**3 + 3.0 * a3 * value**2 + 2.0 * a2 * value + a1,
        value**4 + a3 * value**3 + a2 * value**2 + a1 * value + a0,
    ]
    tail = np.repeat(np.stack(tail)[:, None, :], SUB, axis=1).astype(np.float32)
    return np.concatenate([both, both], axis=0), tail


SIZE = 2 * HALO + EDGE


def within(radius):
    return [[y for y in range(SIZE) if reach(x, y) <= radius] for x in range(SIZE)]


CELLS = [(x, y) for x in range(SIZE) for y in within(HALO)[x]]
CORE = [(x, y) for x in range(HALO, HALO + EDGE) for y in range(HALO, HALO + EDGE)]


def kernel(count, *refs):
    halo, modes, tails = refs[:6], refs[6], refs[7]
    out, rows_of, parts, hat, work_a, work_b, last, acc = refs[8:]
    pitch = ROWS + 1
    number = {cell: at for at, cell in enumerate(CELLS)}

    shape = (LANES, LANES)
    lane = lax.broadcasted_iota(jnp.int32, shape, 1) % NZ
    line = lax.broadcasted_iota(jnp.int32, shape, 0)
    repeats = [(line == lane + place * NZ).astype(jnp.bfloat16) for place in range(count)]
    first_row = []
    total = 0
    for ref in halo:
        packed = ref[ref.shape[0] * ROWS // (ROWS + 1) :].reshape(-1, LANES)
        first_row.append(total)
        for place, repeat in enumerate(repeats):
            rows_of[place, pl.ds(total, packed.shape[0]), :] = jnp.dot(
                packed, repeat, preferred_element_type=jnp.float32
            )
        total += packed.shape[0]

    def spread(place, x, y):
        which, at = place_of(x, y)
        row = rows_of[place, pl.ds(first_row[which] + at, 1), :]
        return jnp.broadcast_to(row, (ROWS, LANES))

    def keep(at, value):
        high = value.astype(jnp.bfloat16)
        low = (value - high.astype(jnp.float32)).astype(jnp.bfloat16)
        parts[at, :, :LANES] = high
        parts[at, :, LANES:] = low

    def turned(first, end):
        cells = end - first
        rows = parts[first:end].reshape(cells * ROWS, 2 * LANES)
        both = jnp.dot(rows, modes[...], preferred_element_type=jnp.float32)
        return (both[:, :LANES] + both[:, LANES:]).reshape(cells, ROWS, LANES)

    def one_half(half):
        rows = pl.ds(half * SUB, SUB)

        def start(x, y):
            return hat[number[x, y], rows, :]

        for step in range(DEGREE):
            new = (work_a, work_b, work_a, None)[step]
            old = (None, work_a, work_b, work_a)[step]
            targets, known = within(HALO - 1 - step), within(HALO - step)

            def load(x):
                return {y: start(x, y) if old is None else old[x, y] for y in known[x]}

            here, pair_prev = load(0), {}
            for x in range(SIZE - 1):
                ahead = load(x + 1)
                pair = {}
                for y in range(SIZE - 1):
                    if y in targets[x] or y + 1 in targets[x + 1]:
                        pair[y] = ahead[y] + here[y + 1]
                    if y in targets[x]:
                        density = here[y] if old is None else start(x, y)
                        value = pair[y] + pair_prev[y - 1] + tails[step] * density
                        if new is not None:
                            new[x, y] = value
                        else:
                            last[CORE.index((x, y)), rows, :] = value
                here, pair_prev = ahead, pair

    def one_source(place, carry):
        chunk = len(CELLS) // 4
        for first in range(0, len(CELLS), chunk):
            end = min(first + chunk, len(CELLS))
            for at in range(first, end):
                which, spot = place_of(*CELLS[at])
                keep(at, halo[which][spot].astype(jnp.float32) * spread(place, *CELLS[at]))
            hat[first:end] = turned(first, end)
        for half in range(ROWS // SUB):
            one_half(half)
        for at in range(len(CORE)):
            keep(at, last[at])
        back = turned(0, len(CORE))
        for at, (x, y) in enumerate(CORE):
            rows = pl.ds((y - HALO) * pitch, ROWS)
            acc[x - HALO, rows, :] = acc[x - HALO, rows, :] + back[at] * spread(place, x, y)
        return carry

    acc[...] = jnp.zeros(acc.shape, jnp.float32)
    lax.fori_loop(0, count, one_source, 0)
    for x in range(EDGE):
        for group in range(ROWS):
            tile = acc[x, pl.ds(group, EDGE, stride=pitch), :]
            out[x, :, pl.ds(group * LANES, LANES)] = tile * (-power_coeffs()[-1])


def fields(halo, count):
    plane = pltpu.VMEM((SIZE, SIZE, SUB, LANES), jnp.float32)
    rows = sum(array.shape[0] * ROWS // (ROWS + 1) + ROWS for array in halo)
    modes, tails = z_modes()
    return pl.pallas_call(
        functools.partial(kernel, count),
        out_shape=jax.ShapeDtypeStruct((EDGE, EDGE, ROWS * LANES), jnp.float32),
        in_specs=[VMEM] * 8,
        out_specs=VMEM,
        scratch_shapes=[
            pltpu.VMEM((count, rows, LANES), jnp.float32),
            pltpu.VMEM((len(CELLS), ROWS, 2 * LANES), jnp.bfloat16),
            pltpu.VMEM((len(CELLS), ROWS, LANES), jnp.float32),
            plane,
            plane,
            pltpu.VMEM((len(CORE), ROWS, LANES), jnp.float32),
            pltpu.VMEM((EDGE, EDGE * (ROWS + 1), LANES), jnp.float32),
        ],
        compiler_params=pltpu.CompilerParams(vmem_limit_bytes=24 * 2**20),
        name="fields",
    )(*halo, modes, tails)


def body(orbitals, src_owner, src_slot):
    packed = messages(orbitals, src_owner, src_slot)
    return fields((packed[0], *exchange(*packed)), src_slot.size)


def solution(mesh):
    in_specs = (P("sx", "sy", "orb"), P(), P())
    out_specs = P("sx", "sy", "orb")
    return jax.shard_map(body, mesh=mesh, in_specs=in_specs, out_specs=out_specs, check_vma=False)
```

```python
import functools
import math

import jax
import jax.numpy as jnp
from jax import lax
from jax.experimental import pallas as pl
from jax.experimental.pallas import tpu as pltpu
from jax.sharding import PartitionSpec as P

NZ = 32
LANES = 128
SUB = 8
ROWS = 16
DEGREE = 4
HALO = DEGREE
EDGE = 8

CHEB = (
    1.021021021021021,
    -1.7357357357357357,
    1.4753753753753753,
    -1.254069069069069,
    1.0659587087087088,
)


def power_coeffs():
    c0, c1, c2, c3, c4 = CHEB
    return (
        c0 - c2 + c4,
        -(c1 - 3.0 * c3) / 6.0,
        (2.0 * c2 - 8.0 * c4) / 36.0,
        -4.0 * c3 / 216.0,
        8.0 * c4 / 1296.0,
    )


CORNER_LOW = tuple(
    (x, y)
    for x in range(EDGE)
    for y in range(EDGE - HALO, EDGE)
    if min(x + 1, EDGE - x) + EDGE - y <= DEGREE
)
CORNER_HIGH = tuple((x, EDGE - 1 - y) for x, y in CORNER_LOW)
SPLIT = len(CORNER_LOW) // 2


def ring(axis, step):
    count = lax.axis_size(axis)
    return [(i, (i + step) % count) for i in range(count)]


def diagonal(step_x, step_y):
    count_x, count_y = lax.axis_size("sx"), lax.axis_size("sy")
    return [
        (i * count_y + j, (i + step_x) % count_x * count_y + (j + step_y) % count_y)
        for i in range(count_x)
        for j in range(count_y)
    ]


VMEM = pl.BlockSpec(memory_space=pltpu.VMEM)
SMALL = pltpu.CompilerParams(vmem_limit_bytes=8 * 2**20)


def spread_out(values):
    return lax.broadcast_in_dim(
        values, values.shape + (ROWS, LANES), tuple(range(values.ndim))
    )


def by_seat(entries):
    rounds, places, rows, lanes = entries.shape
    seat = lax.broadcasted_iota(jnp.int32, (rows, lanes), 1) // NZ
    value = entries[0, 0]
    for index in range(1, rounds * places):
        value = jnp.where(seat == index, entries[index // places, index % places], value)
    return value


def prepare_kernel(entries, orbitals, out, cells, scratch):
    per_tile = LANES // NZ
    slot = by_seat(entries[0])[:EDGE]
    lane = lax.broadcasted_iota(jnp.int32, (EDGE, LANES), 1)
    group, turn = slot // per_tile, (lane // NZ - slot % per_tile + per_tile) % per_tile
    asked = [pltpu.roll(group, LANES - step * NZ, 1) if step else group for step in range(per_tile)]
    found = [[jnp.zeros((EDGE, LANES), jnp.float32)] * EDGE for _ in range(per_tile)]
    for number in range(ROWS):
        lanes = pl.ds(number * LANES, LANES)
        tiles = [orbitals[row, :, lanes].astype(jnp.float32) for row in range(EDGE)]
        for step in range(per_tile):
            here = asked[step] == number
            found[step] = [jnp.where(here, tile, old) for tile, old in zip(tiles, found[step])]
    rows = []
    for row in range(EDGE):
        packed = found[0][row]
        for step in range(1, per_tile):
            packed = jnp.where(turn == step, pltpu.roll(found[step][row], step * NZ, 1), packed)
        rows.append(packed)
    for tile in range(EDGE // 2):
        out[tile] = jnp.concatenate(rows[2 * tile : 2 * tile + 2], axis=0).astype(jnp.bfloat16)
    for row in range(EDGE):
        for group in range(ROWS):
            tile = orbitals[row, :, pl.ds(group * LANES, LANES)].astype(jnp.float32)
            scratch[row, pl.ds(group, EDGE, stride=ROWS + 1), :] = tile
    for row in range(EDGE):
        for y in range(EDGE):
            tile = scratch[row, pl.ds(y * (ROWS + 1), ROWS), :]
            cells[row * EDGE + y] = tile.astype(jnp.bfloat16)


def prepare(entries, orbitals):
    lengths = (EDGE * EDGE // ROWS, EDGE * EDGE)
    return pl.pallas_call(
        prepare_kernel,
        out_shape=[jax.ShapeDtypeStruct((length, ROWS, LANES), jnp.bfloat16) for length in lengths],
        in_specs=[VMEM] * 2,
        out_specs=[VMEM] * 2,
        scratch_shapes=[pltpu.VMEM((EDGE, EDGE * (ROWS + 1), LANES), jnp.float32)],
        compiler_params=SMALL,
        name="prepare",
    )(entries, orbitals)


def chosen(entries, mine, others, bit):
    owner, me = by_seat(entries[1]), lax.axis_index("orb")
    count = lax.axis_size("orb")
    picked = []
    for tile in range(mine.shape[0]):
        value = mine[tile].astype(jnp.float32)
        for step, other in enumerate(others, 1):
            if bit is None:
                here = owner == lax.rem(me + count - step, count)
            else:
                here = (owner >> bit & 1) != (me >> bit & 1)
            value = jnp.where(here, other[tile].astype(jnp.float32), value)
        picked.append(value)
    return picked


def nearer_kernel(bit, entries, mine, other, out):
    for tile, value in enumerate(chosen(entries, mine, [other], bit)):
        out[tile] = value.astype(jnp.bfloat16)


def gathered(entries, mine):
    count = lax.axis_size("orb")
    if count & (count - 1):
        others = [lax.ppermute(mine, "orb", ring("orb", step)) for step in range(1, count)]
        return mine, others, None
    bits = count.bit_length() - 1
    for bit in range(bits):
        other = lax.ppermute(mine, "orb", [(i, i ^ 1 << bit) for i in range(count)])
        if bit == bits - 1:
            return mine, [other], bit
        mine = pl.pallas_call(
            functools.partial(nearer_kernel, bit),
            out_shape=jax.ShapeDtypeStruct(mine.shape, mine.dtype),
            in_specs=[VMEM] * 3,
            out_specs=VMEM,
            compiler_params=SMALL,
            name="nearer",
        )(entries, mine, other)
    return mine, [], None


def messages_kernel(bit, entries, cells, mine, *refs):
    others, (block, last, first, corner_low, corner_high) = refs[:-5], refs[-5:]
    picked = chosen(entries, mine, others, bit)

    def pack(ref, spots):
        for at, (x, y) in enumerate(spots):
            ref[at] = cells[x * EDGE + y]
        used = len(spots)
        runs = []
        for x, y in spots:
            if runs and runs[-1][0] == x and runs[-1][2] == y:
                runs[-1][2] = y + 1
            else:
                runs.append([x, y, y + 1])
        parts = [
            picked[x * EDGE // ROWS][x * EDGE % ROWS + low : x * EDGE % ROWS + high]
            for x, low, high in runs
        ]
        if used % ROWS:
            parts.append(jnp.zeros((ROWS - used % ROWS, LANES), jnp.float32))
        rows = jnp.concatenate(parts, axis=0).astype(jnp.bfloat16)
        for tile in range(rows.shape[0] // ROWS):
            ref[used + tile] = rows[tile * ROWS : (tile + 1) * ROWS]

    pack(block, [(x, y) for x in range(EDGE) for y in range(EDGE)])
    pack(last, [(x, y) for x in range(EDGE) for y in range(EDGE - HALO, EDGE)])
    pack(first, [(x, y) for x in range(EDGE) for y in range(HALO)])
    pack(corner_low, CORNER_LOW)
    pack(corner_high, CORNER_HIGH)


def tiles(spots):
    return spots + -(-spots // ROWS)


def spots_of(length):
    return length * ROWS // (ROWS + 1)


def messages(orbitals, src_owner, src_slot):
    entries = spread_out(jnp.stack([src_slot, src_owner]))
    mine, cells = prepare(entries, orbitals)
    mine, others, bit = gathered(entries, mine)
    lengths = [EDGE * EDGE] + [EDGE * HALO] * 2 + [len(CORNER_LOW)] * 2
    return pl.pallas_call(
        functools.partial(messages_kernel, bit),
        out_shape=[
            jax.ShapeDtypeStruct((tiles(length), ROWS, LANES), jnp.bfloat16) for length in lengths
        ],
        in_specs=[VMEM] * (3 + len(others)),
        out_specs=[VMEM] * 5,
        compiler_params=SMALL,
        name="messages",
    )(entries, cells, mine, *others)


def exchange(block, last, first, corner_low, corner_high):
    both = ("sx", "sy")
    if lax.axis_size("sx") == 2:
        low = lax.ppermute(corner_low, both, diagonal(1, 1))
        high = lax.ppermute(corner_high, both, diagonal(1, -1))
        across = lax.ppermute(block, "sx", ring("sx", 1))
    else:
        def two_ways(cells, half, axes, down, up, merge):
            end = 2 * half
            back = lax.ppermute(jnp.concatenate([cells[:half], cells[end:]]), axes, down)
            ahead = lax.ppermute(jnp.concatenate([cells[half:end], cells[end:]]), axes, up)
            return jnp.concatenate([back[:half], ahead[:half], merge(back[half:], ahead[half:])])

        def halves(back, ahead):
            return jnp.concatenate([back[: back.shape[0] // 2], ahead[ahead.shape[0] // 2 :]])

        def rows(back, ahead):
            return jnp.concatenate([back[:, :SPLIT], ahead[:, SPLIT:]], axis=1)

        low = two_ways(corner_low, SPLIT, both, diagonal(-1, 1), diagonal(1, 1), rows)
        high = two_ways(corner_high, SPLIT, both, diagonal(-1, -1), diagonal(1, -1), rows)
        across = two_ways(block, EDGE * HALO, "sx", ring("sx", -1), ring("sx", 1), halves)
    below = lax.ppermute(last, "sy", ring("sy", 1))
    above = lax.ppermute(first, "sy", ring("sy", -1))
    return across, below, above, low, high


def place_of(x, y):
    row, core_x = (x - HALO) % EDGE, HALO <= x < HALO + EDGE
    if HALO <= y < HALO + EDGE:
        return (0 if core_x else 1), row * EDGE + y - HALO
    if y < HALO:
        return (2, row * HALO + y) if core_x else (4, CORNER_LOW.index((row, y + EDGE - HALO)))
    y = y - HALO - EDGE
    return (3, row * HALO + y) if core_x else (5, CORNER_HIGH.index((row, y)))


def reach(x, y):
    out_x = max(HALO - x, x - (HALO + EDGE - 1), 0)
    out_y = max(HALO - y, y - (HALO + EDGE - 1), 0)
    return out_x + out_y


def z_modes(out):
    shape = (LANES, LANES)
    row, col = (lax.broadcasted_iota(jnp.int32, shape, axis) for axis in range(2))
    product = ((row % NZ + 1) * (col % NZ + 1)).astype(jnp.float32)
    period = 2.0 * (NZ + 1)
    turn = product - period * jnp.floor((product + 0.5) / period)
    value = math.sqrt(2.0 / (NZ + 1)) * jnp.sin(turn * (math.pi / (NZ + 1)))
    value = jnp.where(row // NZ == col // NZ, value, 0.0)
    high = value.astype(jnp.bfloat16)
    low = (value - high.astype(jnp.float32)).astype(jnp.bfloat16)
    for first in (0, LANES):
        out[pl.ds(first, LANES), pl.ds(0, LANES)] = high
        out[pl.ds(first, LANES), pl.ds(LANES, LANES)] = low


def z_tails():
    lane = lax.broadcasted_iota(jnp.int32, (SUB, LANES), 1) % NZ
    value = 2.0 * jnp.cos((lane + 1).astype(jnp.float32) * (math.pi / (NZ + 1)))
    p0, p1, p2, p3, p4 = power_coeffs()
    a3, a2, a1, a0 = p3 / p4, p2 / p4, p1 / p4, p0 / p4
    return (
        4.0 * value + a3,
        (6.0 * value + 3.0 * a3) * value + a2,
        ((4.0 * value + 3.0 * a3) * value + 2.0 * a2) * value + a1,
        (((value + a3) * value + a2) * value + a1) * value + a0,
    )


SIZE = 2 * HALO + EDGE


def within(radius):
    return [[y for y in range(SIZE) if reach(x, y) <= radius] for x in range(SIZE)]


CORE = [(x, y) for x in range(HALO, HALO + EDGE) for y in range(HALO, HALO + EDGE)]


def source_rows(ref, out, first):
    shape = (LANES, LANES)
    lane = lax.broadcasted_iota(jnp.int32, shape, 1) % NZ
    line = lax.broadcasted_iota(jnp.int32, shape, 0)
    packed = ref[spots_of(ref.shape[0]) :].reshape(-1, LANES)
    for place in range(out.shape[0]):
        repeat = (line == lane + place * NZ).astype(jnp.bfloat16)
        out[place, pl.ds(first, packed.shape[0]), :] = jnp.dot(
            packed, repeat, preferred_element_type=jnp.float32
        )
    return first + packed.shape[0]


def keep(parts, at, value):
    high = value.astype(jnp.bfloat16)
    low = (value - high.astype(jnp.float32)).astype(jnp.bfloat16)
    parts[at, :, :LANES] = high
    parts[at, :, LANES:] = low


def turned(parts, first, end, modes):
    cells = end - first
    rows = parts[first:end].reshape(cells * ROWS, 2 * LANES)
    both = jnp.dot(rows, modes[...], preferred_element_type=jnp.float32)
    return (both[:, :LANES] + both[:, LANES:]).reshape(cells, ROWS, LANES)


def densities(refs, rows, firsts, place, parts, modes, put):
    cells = [
        (ref, at, first + at)
        for ref, first in zip(refs, firsts)
        for at in range(spots_of(ref.shape[0]))
    ]
    pieces = -(-len(cells) // 48)
    for piece in range(pieces):
        start, end = (len(cells) * at // pieces for at in (piece, piece + 1))
        for number in range(start, end):
            ref, at, row = cells[number]
            other = jnp.broadcast_to(rows[place, pl.ds(row, 1), :], (ROWS, LANES))
            keep(parts, number, ref[at].astype(jnp.float32) * other)
        put(start, end, turned(parts, start, end, modes))


def all_rows(refs, rows):
    firsts = [0]
    for ref in refs:
        firsts.append(source_rows(ref, rows, firsts[-1]))
    return firsts


def modes_kernel(own, across, hat, own_rows, modes, rows, parts):
    z_modes(modes)
    firsts = all_rows((own, across), rows)
    own_rows[...] = rows[:, : own_rows.shape[1], :]

    def one_source(place, carry):
        def put(start, end, value):
            hat[place, start:end] = value

        densities((own, across), rows, firsts, place, parts, modes, put)
        return carry

    lax.fori_loop(0, hat.shape[0], one_source, 0)


def modes_of(own, across, count):
    cells = 2 * len(CORE)
    return pl.pallas_call(
        modes_kernel,
        out_shape=[
            jax.ShapeDtypeStruct((count, cells, ROWS, LANES), jnp.float32),
            jax.ShapeDtypeStruct((count, len(CORE), LANES), jnp.float32),
            jax.ShapeDtypeStruct((2 * LANES, 2 * LANES), jnp.bfloat16),
        ],
        in_specs=[VMEM] * 2,
        out_specs=[VMEM] * 3,
        scratch_shapes=[
            pltpu.VMEM((count, cells, LANES), jnp.float32),
            pltpu.VMEM((cells, ROWS, 2 * LANES), jnp.bfloat16),
        ],
        compiler_params=pltpu.CompilerParams(vmem_limit_bytes=20 * 2**20),
        cost_estimate=pl.CostEstimate(flops=0, bytes_accessed=6 * 2**20, transcendentals=0),
        name="modes",
    )(own, across)


def in_turn(*works):
    works = [list(work) for work in works]
    done = [0] * len(works)
    for _ in range(sum(map(len, works))):
        at = min(
            (at for at in range(len(works)) if done[at] < len(works[at])),
            key=lambda at: (done[at] + 0.5) / len(works[at]),
        )
        works[at][done[at]]()
        done[at] += 1


def fields_kernel(beside, own_rows, below, above, low, high, modes, *refs):
    out, rows, parts, back, hat, work_a, work_b, last_a, last_b, acc = refs
    count = beside.shape[0]
    pitch = ROWS + 1
    tails = z_tails()
    later = (below, above, low, high)
    firsts = all_rows(later, rows)
    offset = [0]
    for ref in later:
        offset.append(offset[-1] + spots_of(ref.shape[0]))

    def one_density(place, carry):
        def put(start, end, value):
            hat[place, start:end] = value

        densities(later, rows, firsts, place, parts, modes, put)
        return carry

    def steps(place, half, last):
        part = pl.ds(half * SUB, SUB)

        def start(x, y):
            which, at = place_of(x, y)
            if which < 2:
                return beside[place, which * len(CORE) + at, part, :]
            return hat[place, offset[which - 2] + at, part, :]

        def one_row(step, x, state):
            new = (work_a, work_b, work_a, None)[step]
            old = (None, work_a, work_b, work_a)[step]
            targets, known = within(HALO - 1 - step), within(HALO - step)

            def load(x):
                return {y: start(x, y) if old is None else old[x, y] for y in known[x]}

            here, pair_prev = state.get(step) or (load(x), {})
            ahead, pair = load(x + 1), {}
            for y in range(SIZE - 1):
                if y in targets[x] or y + 1 in targets[x + 1]:
                    pair[y] = ahead[y] + here[y + 1]
                if y in targets[x]:
                    density = here[y] if old is None else start(x, y)
                    value = pair[y] + pair_prev[y - 1] + tails[step] * density
                    if new is not None:
                        new[x, y] = value
                    else:
                        last[CORE.index((x, y)), part, :] = value
            state[step] = (ahead, pair)

        state = {}
        return [
            functools.partial(one_row, step, x, state)
            for step in range(DEGREE)
            for x in range(step, SIZE - 1 - step)
        ]

    def way_back(place, last):
        pieces = 2
        size = len(CORE) // pieces

        def split(at):
            keep(back, at, last[at])

        def turn(piece, held):
            held[piece] = turned(back, piece * size, (piece + 1) * size, modes)

        def add(at, held):
            x, y = CORE[at]
            lanes = pl.ds((y - HALO) * pitch, ROWS)
            other = jnp.broadcast_to(own_rows[place, pl.ds(at, 1), :], (ROWS, LANES))
            value = held[at // size][at % size] * other
            acc[x - HALO, lanes, :] = acc[x - HALO, lanes, :] + value

        held = {}
        work = []
        for piece in range(pieces):
            cells = range(piece * size, (piece + 1) * size)
            work += [functools.partial(split, at) for at in cells]
            work.append(functools.partial(turn, piece, held))
            work += [functools.partial(add, at, held) for at in cells]
        return work

    def two_sources(pair, carry):
        first, second = 2 * pair, 2 * pair + 1
        in_turn(
            steps(first, 0, last_a) + steps(first, 1, last_a),
            way_back(lax.max(first - 1, 0), last_b),
        )
        in_turn(
            steps(second, 0, last_b) + steps(second, 1, last_b),
            way_back(first, last_a),
        )
        return carry

    lax.fori_loop(0, count, one_density, 0)
    acc[...] = jnp.zeros(acc.shape, jnp.float32)
    last_b[...] = jnp.zeros(last_b.shape, jnp.float32)
    lax.fori_loop(0, count // 2, two_sources, 0)
    in_turn(way_back(count - 1, last_b))
    for x in range(EDGE):
        for group in range(ROWS):
            tile = acc[x, pl.ds(group, EDGE, stride=pitch), :]
            out[x, :, pl.ds(group * LANES, LANES)] = tile * (-power_coeffs()[-1])


def fields(halo, count):
    own, across, *later = halo
    beside, own_rows, modes = modes_of(own, across, count)
    plane = pltpu.VMEM((SIZE, SIZE, SUB, LANES), jnp.float32)
    core = pltpu.VMEM((len(CORE), ROWS, LANES), jnp.float32)
    cells = sum(spots_of(array.shape[0]) for array in later)
    rows = ROWS * sum(array.shape[0] - spots_of(array.shape[0]) for array in later)
    return pl.pallas_call(
        fields_kernel,
        out_shape=jax.ShapeDtypeStruct((EDGE, EDGE, ROWS * LANES), jnp.float32),
        in_specs=[VMEM] * 7,
        out_specs=VMEM,
        scratch_shapes=[
            pltpu.VMEM((count, rows, LANES), jnp.float32),
            pltpu.VMEM((cells, ROWS, 2 * LANES), jnp.bfloat16),
            pltpu.VMEM((len(CORE), ROWS, 2 * LANES), jnp.bfloat16),
            pltpu.VMEM((count, cells, ROWS, LANES), jnp.float32),
            plane,
            plane,
            core,
            core,
            pltpu.VMEM((EDGE, EDGE * (ROWS + 1), LANES), jnp.float32),
        ],
        compiler_params=pltpu.CompilerParams(vmem_limit_bytes=24 * 2**20),
        name="fields",
    )(beside, own_rows, *later, modes)


def body(orbitals, src_owner, src_slot):
    packed = messages(orbitals, src_owner, src_slot)
    return fields((packed[0], *exchange(*packed)), src_slot.size)


def solution(mesh):
    in_specs = (P("sx", "sy", "orb"), P(), P())
    out_specs = P("sx", "sy", "orb")
    return jax.shard_map(body, mesh=mesh, in_specs=in_specs, out_specs=out_specs, check_vma=False)
```

```python
import functools
import math

import jax
import jax.numpy as jnp
from jax import lax
from jax.experimental import pallas as pl
from jax.experimental.pallas import tpu as pltpu
from jax.sharding import PartitionSpec as P

NZ = 32
LANES = 128
SUB = 8
ROWS = 16
DEGREE = 4
HALO = DEGREE
EDGE = 8

CHEB = (
    1.021021021021021,
    -1.7357357357357357,
    1.4753753753753753,
    -1.254069069069069,
    1.0659587087087088,
)


def power_coeffs():
    c0, c1, c2, c3, c4 = CHEB
    return (
        c0 - c2 + c4,
        -(c1 - 3.0 * c3) / 6.0,
        (2.0 * c2 - 8.0 * c4) / 36.0,
        -4.0 * c3 / 216.0,
        8.0 * c4 / 1296.0,
    )


CORNER_LOW = tuple(
    (x, y)
    for x in range(EDGE)
    for y in range(EDGE - HALO, EDGE)
    if min(x + 1, EDGE - x) + EDGE - y <= DEGREE
)
CORNER_HIGH = tuple((x, EDGE - 1 - y) for x, y in CORNER_LOW)
SPLIT = len(CORNER_LOW) // 2


def ring(axis, step):
    count = lax.axis_size(axis)
    return [(i, (i + step) % count) for i in range(count)]


def diagonal(step_x, step_y):
    count_x, count_y = lax.axis_size("sx"), lax.axis_size("sy")
    return [
        (i * count_y + j, (i + step_x) % count_x * count_y + (j + step_y) % count_y)
        for i in range(count_x)
        for j in range(count_y)
    ]


VMEM = pl.BlockSpec(memory_space=pltpu.VMEM)
SMALL = pltpu.CompilerParams(vmem_limit_bytes=8 * 2**20)


def spread_out(values):
    return lax.broadcast_in_dim(
        values, values.shape + (ROWS, LANES), tuple(range(values.ndim))
    )


def by_seat(entries):
    rounds, places, rows, lanes = entries.shape
    seat = lax.broadcasted_iota(jnp.int32, (rows, lanes), 1) // NZ
    value = entries[0, 0]
    for index in range(1, rounds * places):
        value = jnp.where(seat == index, entries[index // places, index % places], value)
    return value


def prepare_kernel(entries, orbitals, out, cells, scratch):
    per_tile = LANES // NZ
    slot = by_seat(entries[0])[:EDGE]
    lane = lax.broadcasted_iota(jnp.int32, (EDGE, LANES), 1)
    group, turn = slot // per_tile, (lane // NZ - slot % per_tile + per_tile) % per_tile
    asked = [pltpu.roll(group, LANES - step * NZ, 1) if step else group for step in range(per_tile)]
    found = [[jnp.zeros((EDGE, LANES), jnp.float32)] * EDGE for _ in range(per_tile)]
    for number in range(ROWS):
        lanes = pl.ds(number * LANES, LANES)
        tiles = [orbitals[row, :, lanes].astype(jnp.float32) for row in range(EDGE)]
        for step in range(per_tile):
            here = asked[step] == number
            found[step] = [jnp.where(here, tile, old) for tile, old in zip(tiles, found[step])]
    rows = []
    for row in range(EDGE):
        packed = found[0][row]
        for step in range(1, per_tile):
            packed = jnp.where(turn == step, pltpu.roll(found[step][row], step * NZ, 1), packed)
        rows.append(packed)
    for tile in range(EDGE // 2):
        out[tile] = jnp.concatenate(rows[2 * tile : 2 * tile + 2], axis=0).astype(jnp.bfloat16)
    for row in range(EDGE):
        for group in range(ROWS):
            tile = orbitals[row, :, pl.ds(group * LANES, LANES)].astype(jnp.float32)
            scratch[row, pl.ds(group, EDGE, stride=ROWS + 1), :] = tile
    for row in range(EDGE):
        for y in range(EDGE):
            tile = scratch[row, pl.ds(y * (ROWS + 1), ROWS), :]
            cells[row * EDGE + y] = tile.astype(jnp.bfloat16)


def prepare(entries, orbitals):
    lengths = (EDGE * EDGE // ROWS, EDGE * EDGE)
    return pl.pallas_call(
        prepare_kernel,
        out_shape=[jax.ShapeDtypeStruct((length, ROWS, LANES), jnp.bfloat16) for length in lengths],
        in_specs=[VMEM] * 2,
        out_specs=[VMEM] * 2,
        scratch_shapes=[pltpu.VMEM((EDGE, EDGE * (ROWS + 1), LANES), jnp.float32)],
        compiler_params=SMALL,
        name="prepare",
    )(entries, orbitals)


def chosen(entries, mine, others, bit):
    owner, me = by_seat(entries[1]), lax.axis_index("orb")
    count = lax.axis_size("orb")
    picked = []
    for tile in range(mine.shape[0]):
        value = mine[tile].astype(jnp.float32)
        for step, other in enumerate(others, 1):
            if bit is None:
                here = owner == lax.rem(me + count - step, count)
            else:
                here = (owner >> bit & 1) != (me >> bit & 1)
            value = jnp.where(here, other[tile].astype(jnp.float32), value)
        picked.append(value)
    return picked


def nearer_kernel(bit, entries, mine, other, out):
    for tile, value in enumerate(chosen(entries, mine, [other], bit)):
        out[tile] = value.astype(jnp.bfloat16)


def gathered(entries, mine):
    count = lax.axis_size("orb")
    if count & (count - 1):
        others = [lax.ppermute(mine, "orb", ring("orb", step)) for step in range(1, count)]
        return mine, others, None
    bits = count.bit_length() - 1
    for bit in range(bits):
        other = lax.ppermute(mine, "orb", [(i, i ^ 1 << bit) for i in range(count)])
        if bit == bits - 1:
            return mine, [other], bit
        mine = pl.pallas_call(
            functools.partial(nearer_kernel, bit),
            out_shape=jax.ShapeDtypeStruct(mine.shape, mine.dtype),
            in_specs=[VMEM] * 3,
            out_specs=VMEM,
            compiler_params=SMALL,
            name="nearer",
        )(entries, mine, other)
    return mine, [], None


def messages_kernel(bit, before, entries, cells, mine, *refs):
    others, (block, last, first, corner_low, corner_high) = refs[:-5], refs[-5:]
    picked = chosen(entries, mine, others, bit)

    def pack(ref, spots):
        for at, (x, y) in enumerate(spots):
            ref[at] = cells[x * EDGE + y]
        used = len(spots)
        runs = []
        for x, y in spots:
            if runs and runs[-1][0] == x and runs[-1][2] == y:
                runs[-1][2] = y + 1
            else:
                runs.append([x, y, y + 1])
        parts = [
            picked[x * EDGE // ROWS][x * EDGE % ROWS + low : x * EDGE % ROWS + high]
            for x, low, high in runs
        ]
        if used % ROWS:
            parts.append(jnp.zeros((ROWS - used % ROWS, LANES), jnp.float32))
        rows = jnp.concatenate(parts, axis=0).astype(jnp.bfloat16)
        for tile in range(rows.shape[0] // ROWS):
            ref[used + tile] = rows[tile * ROWS : (tile + 1) * ROWS]

    pack(block, [(x, y) for x in range(EDGE) for y in range(EDGE)])
    pack(last, [(x, y) for x in range(EDGE) for y in range(EDGE - HALO, EDGE)])
    pack(first, [(x, y) for x in range(EDGE) for y in range(HALO)])
    pack(corner_low, CORNER_LOW)
    pack(corner_high, CORNER_HIGH)


def tiles(spots):
    return spots + -(-spots // ROWS)


def spots_of(length):
    return length * ROWS // (ROWS + 1)


def messages(orbitals, src_owner, src_slot):
    entries = spread_out(jnp.stack([src_slot, src_owner]))
    mine, cells = prepare(entries, orbitals)
    mine, others, bit = gathered(entries, mine)
    lengths = [EDGE * EDGE] + [EDGE * HALO] * 2 + [len(CORNER_LOW)] * 2
    modes = sines(mine)
    packed = pl.pallas_call(
        functools.partial(messages_kernel, bit),
        out_shape=[
            jax.ShapeDtypeStruct((tiles(length), ROWS, LANES), jnp.bfloat16) for length in lengths
        ],
        in_specs=[pl.BlockSpec(memory_space=pl.ANY)] + [VMEM] * (3 + len(others)),
        out_specs=[VMEM] * 5,
        compiler_params=SMALL,
        name="messages",
    )(modes, entries, cells, mine, *others)
    return packed, modes


def exchange(block, last, first, corner_low, corner_high):
    both = ("sx", "sy")
    if lax.axis_size("sx") == 2:
        low = lax.ppermute(corner_low, both, diagonal(1, 1))
        high = lax.ppermute(corner_high, both, diagonal(1, -1))
        across = lax.ppermute(block, "sx", ring("sx", 1))
    else:
        def two_ways(cells, half, axes, down, up, merge):
            end = 2 * half
            back = lax.ppermute(jnp.concatenate([cells[:half], cells[end:]]), axes, down)
            ahead = lax.ppermute(jnp.concatenate([cells[half:end], cells[end:]]), axes, up)
            return jnp.concatenate([back[:half], ahead[:half], merge(back[half:], ahead[half:])])

        def halves(back, ahead):
            return jnp.concatenate([back[: back.shape[0] // 2], ahead[ahead.shape[0] // 2 :]])

        def rows(back, ahead):
            return jnp.concatenate([back[:, :SPLIT], ahead[:, SPLIT:]], axis=1)

        low = two_ways(corner_low, SPLIT, both, diagonal(-1, 1), diagonal(1, 1), rows)
        high = two_ways(corner_high, SPLIT, both, diagonal(-1, -1), diagonal(1, -1), rows)
        across = two_ways(block, EDGE * HALO, "sx", ring("sx", -1), ring("sx", 1), halves)
    below = lax.ppermute(last, "sy", ring("sy", 1))
    above = lax.ppermute(first, "sy", ring("sy", -1))
    return across, below, above, low, high


def place_of(x, y):
    row, core_x = (x - HALO) % EDGE, HALO <= x < HALO + EDGE
    if HALO <= y < HALO + EDGE:
        return (0 if core_x else 1), row * EDGE + y - HALO
    if y < HALO:
        return (2, row * HALO + y) if core_x else (4, CORNER_LOW.index((row, y + EDGE - HALO)))
    y = y - HALO - EDGE
    return (3, row * HALO + y) if core_x else (5, CORNER_HIGH.index((row, y)))


def reach(x, y):
    out_x = max(HALO - x, x - (HALO + EDGE - 1), 0)
    out_y = max(HALO - y, y - (HALO + EDGE - 1), 0)
    return out_x + out_y


def sines_kernel(after, out):
    shape = (LANES, LANES)
    row, col = (lax.broadcasted_iota(jnp.int32, shape, axis) for axis in range(2))
    product = ((row % NZ + 1) * (col % NZ + 1)).astype(jnp.float32)
    period = 2.0 * (NZ + 1)
    turn = product - period * jnp.floor((product + 0.5) / period)
    value = math.sqrt(2.0 / (NZ + 1)) * jnp.sin(turn * (math.pi / (NZ + 1)))
    value = jnp.where(row // NZ == col // NZ, value, 0.0)
    high = value.astype(jnp.bfloat16)
    low = (value - high.astype(jnp.float32)).astype(jnp.bfloat16)
    for first in (0, LANES):
        out[pl.ds(first, LANES), pl.ds(0, LANES)] = high
        out[pl.ds(first, LANES), pl.ds(LANES, LANES)] = low


def sines(after):
    return pl.pallas_call(
        sines_kernel,
        out_shape=jax.ShapeDtypeStruct((2 * LANES, 2 * LANES), jnp.bfloat16),
        in_specs=[pl.BlockSpec(memory_space=pl.ANY)],
        out_specs=VMEM,
        compiler_params=SMALL,
        cost_estimate=pl.CostEstimate(flops=0, bytes_accessed=2 * 2**20, transcendentals=0),
        name="sines",
    )(after)


def z_tails():
    lane = lax.broadcasted_iota(jnp.int32, (SUB, LANES), 1) % NZ
    value = 2.0 * jnp.cos((lane + 1).astype(jnp.float32) * (math.pi / (NZ + 1)))
    p0, p1, p2, p3, p4 = power_coeffs()
    a3, a2, a1, a0 = p3 / p4, p2 / p4, p1 / p4, p0 / p4
    return (
        4.0 * value + a3,
        (6.0 * value + 3.0 * a3) * value + a2,
        ((4.0 * value + 3.0 * a3) * value + 2.0 * a2) * value + a1,
        (((value + a3) * value + a2) * value + a1) * value + a0,
    )


SIZE = 2 * HALO + EDGE


def within(radius):
    return [[y for y in range(SIZE) if reach(x, y) <= radius] for x in range(SIZE)]


CORE = [(x, y) for x in range(HALO, HALO + EDGE) for y in range(HALO, HALO + EDGE)]


def source_rows(ref, out, first):
    shape = (LANES, LANES)
    lane = lax.broadcasted_iota(jnp.int32, shape, 1) % NZ
    line = lax.broadcasted_iota(jnp.int32, shape, 0)
    packed = ref[spots_of(ref.shape[0]) :].reshape(-1, LANES)
    for place in range(out.shape[0]):
        repeat = (line == lane + place * NZ).astype(jnp.bfloat16)
        out[place, pl.ds(first, packed.shape[0]), :] = jnp.dot(
            packed, repeat, preferred_element_type=jnp.float32
        )
    return first + packed.shape[0]


def keep(parts, at, value):
    high = value.astype(jnp.bfloat16)
    low = (value - high.astype(jnp.float32)).astype(jnp.bfloat16)
    parts[at, :, :LANES] = high
    parts[at, :, LANES:] = low


def turned(parts, first, end, modes):
    cells = end - first
    rows = parts[first:end].reshape(cells * ROWS, 2 * LANES)
    both = jnp.dot(rows, modes[...], preferred_element_type=jnp.float32)
    return (both[:, :LANES] + both[:, LANES:]).reshape(cells, ROWS, LANES)


def densities(refs, rows, firsts, place, parts, modes, put):
    cells = [
        (ref, at, first + at)
        for ref, first in zip(refs, firsts)
        for at in range(spots_of(ref.shape[0]))
    ]
    pieces = -(-len(cells) // 48)
    for piece in range(pieces):
        start, end = (len(cells) * at // pieces for at in (piece, piece + 1))
        for number in range(start, end):
            ref, at, row = cells[number]
            other = jnp.broadcast_to(rows[place, pl.ds(row, 1), :], (ROWS, LANES))
            keep(parts, number, ref[at].astype(jnp.float32) * other)
        put(start, end, turned(parts, start, end, modes))


def all_rows(refs, rows):
    firsts = [0]
    for ref in refs:
        firsts.append(source_rows(ref, rows, firsts[-1]))
    return firsts


def modes_kernel(own, across, modes, hat, own_rows, rows, parts):
    firsts = all_rows((own, across), rows)
    own_rows[...] = rows[:, : own_rows.shape[1], :]

    def one_source(place, carry):
        def put(start, end, value):
            hat[place, start:end] = value

        densities((own, across), rows, firsts, place, parts, modes, put)
        return carry

    lax.fori_loop(0, hat.shape[0], one_source, 0)


def modes_of(own, across, modes, count):
    cells = 2 * len(CORE)
    return pl.pallas_call(
        modes_kernel,
        out_shape=[
            jax.ShapeDtypeStruct((count, cells, ROWS, LANES), jnp.float32),
            jax.ShapeDtypeStruct((count, len(CORE), LANES), jnp.float32),
        ],
        in_specs=[VMEM] * 3,
        out_specs=[VMEM] * 2,
        scratch_shapes=[
            pltpu.VMEM((count, cells, LANES), jnp.float32),
            pltpu.VMEM((cells, ROWS, 2 * LANES), jnp.bfloat16),
        ],
        compiler_params=pltpu.CompilerParams(vmem_limit_bytes=20 * 2**20),
        cost_estimate=pl.CostEstimate(flops=0, bytes_accessed=6 * 2**20, transcendentals=0),
        name="modes",
    )(own, across, modes)


def fields_kernel(beside, own_rows, below, above, low, high, modes, *refs):
    out, rows, parts, back, hat, work_a, work_b, last, acc = refs
    count = beside.shape[0]
    pitch = ROWS + 1
    tails = z_tails()
    later = (below, above, low, high)
    firsts = all_rows(later, rows)
    offset = [0]
    for ref in later:
        offset.append(offset[-1] + spots_of(ref.shape[0]))

    def one_density(place, carry):
        def put(start, end, value):
            hat[place, start:end] = value

        densities(later, rows, firsts, place, parts, modes, put)
        return carry

    def steps(place, half):
        part = pl.ds(half * SUB, SUB)

        def start(x, y):
            which, at = place_of(x, y)
            if which < 2:
                return beside[place, which * len(CORE) + at, part, :]
            return hat[place, offset[which - 2] + at, part, :]

        for step in range(DEGREE):
            new = (work_a, work_b, work_a, None)[step]
            old = (None, work_a, work_b, work_a)[step]
            targets, known = within(HALO - 1 - step), within(HALO - step)

            def load(x):
                return {y: start(x, y) if old is None else old[x, y] for y in known[x]}

            here, pair_prev = load(step), {}
            for x in range(step, SIZE - 1 - step):
                ahead, pair = load(x + 1), {}
                for y in range(SIZE - 1):
                    if y in targets[x] or y + 1 in targets[x + 1]:
                        pair[y] = ahead[y] + here[y + 1]
                    if y in targets[x]:
                        density = here[y] if old is None else start(x, y)
                        value = pair[y] + pair_prev[y - 1] + tails[step] * density
                        if new is not None:
                            new[x, y] = value
                        else:
                            last[CORE.index((x, y)), part, :] = value
                here, pair_prev = ahead, pair

    def one_source(place, carry):
        for half in range(ROWS // SUB):
            steps(place, half)
        for at in range(len(CORE)):
            keep(back, at, last[at])
        result = turned(back, 0, len(CORE), modes)
        for at, (x, y) in enumerate(CORE):
            lanes = pl.ds((y - HALO) * pitch, ROWS)
            other = jnp.broadcast_to(own_rows[place, pl.ds(at, 1), :], (ROWS, LANES))
            acc[x - HALO, lanes, :] = acc[x - HALO, lanes, :] + result[at] * other
        return carry

    lax.fori_loop(0, count, one_density, 0)
    acc[...] = jnp.zeros(acc.shape, jnp.float32)
    lax.fori_loop(0, count, one_source, 0)
    for x in range(EDGE):
        for group in range(ROWS):
            tile = acc[x, pl.ds(group, EDGE, stride=pitch), :]
            out[x, :, pl.ds(group * LANES, LANES)] = tile * (-power_coeffs()[-1])


def fields(halo, modes, count):
    own, across, *later = halo
    beside, own_rows = modes_of(own, across, modes, count)
    plane = pltpu.VMEM((SIZE, SIZE, SUB, LANES), jnp.float32)
    core = pltpu.VMEM((len(CORE), ROWS, LANES), jnp.float32)
    cells = sum(spots_of(array.shape[0]) for array in later)
    rows = ROWS * sum(array.shape[0] - spots_of(array.shape[0]) for array in later)
    return pl.pallas_call(
        fields_kernel,
        out_shape=jax.ShapeDtypeStruct((EDGE, EDGE, ROWS * LANES), jnp.float32),
        in_specs=[VMEM] * 7,
        out_specs=VMEM,
        scratch_shapes=[
            pltpu.VMEM((count, rows, LANES), jnp.float32),
            pltpu.VMEM((cells, ROWS, 2 * LANES), jnp.bfloat16),
            pltpu.VMEM((len(CORE), ROWS, 2 * LANES), jnp.bfloat16),
            pltpu.VMEM((count, cells, ROWS, LANES), jnp.float32),
            plane,
            plane,
            core,
            pltpu.VMEM((EDGE, EDGE * (ROWS + 1), LANES), jnp.float32),
        ],
        compiler_params=pltpu.CompilerParams(vmem_limit_bytes=24 * 2**20),
        name="fields",
    )(beside, own_rows, *later, modes)


def body(orbitals, src_owner, src_slot):
    packed, modes = messages(orbitals, src_owner, src_slot)
    return fields((packed[0], *exchange(*packed)), modes, src_slot.size)


def solution(mesh):
    in_specs = (P("sx", "sy", "orb"), P(), P())
    out_specs = P("sx", "sy", "orb")
    return jax.shard_map(body, mesh=mesh, in_specs=in_specs, out_specs=out_specs, check_vma=False)
```

```python
import functools
import math

import jax
import jax.numpy as jnp
from jax import lax
from jax.experimental import pallas as pl
from jax.experimental.pallas import tpu as pltpu
from jax.sharding import PartitionSpec as P

NZ = 32
LANES = 128
SUB = 8
ROWS = 16
DEGREE = 4
HALO = DEGREE
EDGE = 8

CHEB = (
    1.021021021021021,
    -1.7357357357357357,
    1.4753753753753753,
    -1.254069069069069,
    1.0659587087087088,
)


def power_coeffs():
    c0, c1, c2, c3, c4 = CHEB
    return (
        c0 - c2 + c4,
        -(c1 - 3.0 * c3) / 6.0,
        (2.0 * c2 - 8.0 * c4) / 36.0,
        -4.0 * c3 / 216.0,
        8.0 * c4 / 1296.0,
    )


CORNER_LOW = tuple(
    (x, y)
    for x in range(EDGE)
    for y in range(EDGE - HALO, EDGE)
    if min(x + 1, EDGE - x) + EDGE - y <= DEGREE
)
CORNER_HIGH = tuple((x, EDGE - 1 - y) for x, y in CORNER_LOW)
SPLIT = len(CORNER_LOW) // 2


def ring(axis, step):
    count = lax.axis_size(axis)
    return [(i, (i + step) % count) for i in range(count)]


def diagonal(step_x, step_y):
    count_x, count_y = lax.axis_size("sx"), lax.axis_size("sy")
    return [
        (i * count_y + j, (i + step_x) % count_x * count_y + (j + step_y) % count_y)
        for i in range(count_x)
        for j in range(count_y)
    ]


VMEM = pl.BlockSpec(memory_space=pltpu.VMEM)
SMALL = pltpu.CompilerParams(vmem_limit_bytes=8 * 2**20)


def spread_out(values):
    return lax.broadcast_in_dim(
        values, values.shape + (ROWS, LANES), tuple(range(values.ndim))
    )


def by_seat(entries):
    rounds, places, rows, lanes = entries.shape
    seat = lax.broadcasted_iota(jnp.int32, (rows, lanes), 1) // NZ
    value = entries[0, 0]
    for index in range(1, rounds * places):
        value = jnp.where(seat == index, entries[index // places, index % places], value)
    return value


def prepare_kernel(entries, orbitals, out, cells, scratch):
    per_tile = LANES // NZ
    slot = by_seat(entries[0])[:EDGE]
    lane = lax.broadcasted_iota(jnp.int32, (EDGE, LANES), 1)
    group, turn = slot // per_tile, (lane // NZ - slot % per_tile + per_tile) % per_tile
    asked = [pltpu.roll(group, LANES - step * NZ, 1) if step else group for step in range(per_tile)]
    found = [[jnp.zeros((EDGE, LANES), jnp.float32)] * EDGE for _ in range(per_tile)]
    for number in range(ROWS):
        lanes = pl.ds(number * LANES, LANES)
        tiles = [orbitals[row, :, lanes].astype(jnp.float32) for row in range(EDGE)]
        for step in range(per_tile):
            here = asked[step] == number
            found[step] = [jnp.where(here, tile, old) for tile, old in zip(tiles, found[step])]
    rows = []
    for row in range(EDGE):
        packed = found[0][row]
        for step in range(1, per_tile):
            packed = jnp.where(turn == step, pltpu.roll(found[step][row], step * NZ, 1), packed)
        rows.append(packed)
    for tile in range(EDGE // 2):
        out[tile] = jnp.concatenate(rows[2 * tile : 2 * tile + 2], axis=0).astype(jnp.bfloat16)
    for row in range(EDGE):
        for group in range(ROWS):
            tile = orbitals[row, :, pl.ds(group * LANES, LANES)].astype(jnp.float32)
            scratch[row, pl.ds(group, EDGE, stride=ROWS + 1), :] = tile
    for row in range(EDGE):
        for y in range(EDGE):
            tile = scratch[row, pl.ds(y * (ROWS + 1), ROWS), :]
            cells[row * EDGE + y] = tile.astype(jnp.bfloat16)


def prepare(entries, orbitals):
    lengths = (EDGE * EDGE // ROWS, EDGE * EDGE)
    return pl.pallas_call(
        prepare_kernel,
        out_shape=[jax.ShapeDtypeStruct((length, ROWS, LANES), jnp.bfloat16) for length in lengths],
        in_specs=[VMEM] * 2,
        out_specs=[VMEM] * 2,
        scratch_shapes=[pltpu.VMEM((EDGE, EDGE * (ROWS + 1), LANES), jnp.float32)],
        compiler_params=SMALL,
        name="prepare",
    )(entries, orbitals)


def chosen(entries, mine, others, bit):
    owner, me = by_seat(entries[1]), lax.axis_index("orb")
    count = lax.axis_size("orb")
    picked = []
    for tile in range(mine.shape[0]):
        value = mine[tile].astype(jnp.float32)
        for step, other in enumerate(others, 1):
            if bit is None:
                here = owner == lax.rem(me + count - step, count)
            else:
                here = (owner >> bit & 1) != (me >> bit & 1)
            value = jnp.where(here, other[tile].astype(jnp.float32), value)
        picked.append(value)
    return picked


def nearer_kernel(bit, entries, mine, other, out):
    for tile, value in enumerate(chosen(entries, mine, [other], bit)):
        out[tile] = value.astype(jnp.bfloat16)


def gathered(entries, mine):
    count = lax.axis_size("orb")
    if count & (count - 1):
        others = [lax.ppermute(mine, "orb", ring("orb", step)) for step in range(1, count)]
        return mine, others, None
    bits = count.bit_length() - 1
    for bit in range(bits):
        other = lax.ppermute(mine, "orb", [(i, i ^ 1 << bit) for i in range(count)])
        if bit == bits - 1:
            return mine, [other], bit
        mine = pl.pallas_call(
            functools.partial(nearer_kernel, bit),
            out_shape=jax.ShapeDtypeStruct(mine.shape, mine.dtype),
            in_specs=[VMEM] * 3,
            out_specs=VMEM,
            compiler_params=SMALL,
            name="nearer",
        )(entries, mine, other)
    return mine, [], None


def messages_kernel(bit, before, entries, cells, mine, *refs):
    others, (block, last, first, corner_low, corner_high) = refs[:-5], refs[-5:]
    picked = chosen(entries, mine, others, bit)

    def pack(ref, spots):
        for at, (x, y) in enumerate(spots):
            ref[at] = cells[x * EDGE + y]
        used = len(spots)
        runs = []
        for x, y in spots:
            if runs and runs[-1][0] == x and runs[-1][2] == y:
                runs[-1][2] = y + 1
            else:
                runs.append([x, y, y + 1])
        parts = [
            picked[x * EDGE // ROWS][x * EDGE % ROWS + low : x * EDGE % ROWS + high]
            for x, low, high in runs
        ]
        if used % ROWS:
            parts.append(jnp.zeros((ROWS - used % ROWS, LANES), jnp.float32))
        rows = jnp.concatenate(parts, axis=0).astype(jnp.bfloat16)
        for tile in range(rows.shape[0] // ROWS):
            ref[used + tile] = rows[tile * ROWS : (tile + 1) * ROWS]

    pack(block, [(x, y) for x in range(EDGE) for y in range(EDGE)])
    pack(last, [(x, y) for x in range(EDGE) for y in range(EDGE - HALO, EDGE)])
    pack(first, [(x, y) for x in range(EDGE) for y in range(HALO)])
    pack(corner_low, CORNER_LOW)
    pack(corner_high, CORNER_HIGH)


def tiles(spots):
    return spots + -(-spots // ROWS)


def spots_of(length):
    return length * ROWS // (ROWS + 1)


def messages(orbitals, src_owner, src_slot):
    entries = spread_out(jnp.stack([src_slot, src_owner]))
    mine, cells = prepare(entries, orbitals)
    mine, others, bit = gathered(entries, mine)
    lengths = [EDGE * EDGE] + [EDGE * HALO] * 2 + [len(CORNER_LOW)] * 2
    modes = sines(mine)
    packed = pl.pallas_call(
        functools.partial(messages_kernel, bit),
        out_shape=[
            jax.ShapeDtypeStruct((tiles(length), ROWS, LANES), jnp.bfloat16) for length in lengths
        ],
        in_specs=[pl.BlockSpec(memory_space=pl.ANY)] + [VMEM] * (3 + len(others)),
        out_specs=[VMEM] * 5,
        compiler_params=SMALL,
        name="messages",
    )(modes, entries, cells, mine, *others)
    return packed, modes


def exchange(block, last, first, corner_low, corner_high):
    both = ("sx", "sy")
    if lax.axis_size("sx") == 2:
        low = lax.ppermute(corner_low, both, diagonal(1, 1))
        high = lax.ppermute(corner_high, both, diagonal(1, -1))
        across = lax.ppermute(block, "sx", ring("sx", 1))
    else:
        def two_ways(cells, half, axes, down, up, merge):
            end = 2 * half
            back = lax.ppermute(jnp.concatenate([cells[:half], cells[end:]]), axes, down)
            ahead = lax.ppermute(jnp.concatenate([cells[half:end], cells[end:]]), axes, up)
            return jnp.concatenate([back[:half], ahead[:half], merge(back[half:], ahead[half:])])

        def halves(back, ahead):
            return jnp.concatenate([back[: back.shape[0] // 2], ahead[ahead.shape[0] // 2 :]])

        def rows(back, ahead):
            return jnp.concatenate([back[:, :SPLIT], ahead[:, SPLIT:]], axis=1)

        low = two_ways(corner_low, SPLIT, both, diagonal(-1, 1), diagonal(1, 1), rows)
        high = two_ways(corner_high, SPLIT, both, diagonal(-1, -1), diagonal(1, -1), rows)
        across = two_ways(block, EDGE * HALO, "sx", ring("sx", -1), ring("sx", 1), halves)
    below = lax.ppermute(last, "sy", ring("sy", 1))
    above = lax.ppermute(first, "sy", ring("sy", -1))
    return across, below, above, low, high


def place_of(x, y):
    row, core_x = (x - HALO) % EDGE, HALO <= x < HALO + EDGE
    if HALO <= y < HALO + EDGE:
        return (0 if core_x else 1), row * EDGE + y - HALO
    if y < HALO:
        return (2, row * HALO + y) if core_x else (4, CORNER_LOW.index((row, y + EDGE - HALO)))
    y = y - HALO - EDGE
    return (3, row * HALO + y) if core_x else (5, CORNER_HIGH.index((row, y)))


def reach(x, y):
    out_x = max(HALO - x, x - (HALO + EDGE - 1), 0)
    out_y = max(HALO - y, y - (HALO + EDGE - 1), 0)
    return out_x + out_y


def sines_kernel(after, out):
    shape = (LANES, LANES)
    row, col = (lax.broadcasted_iota(jnp.int32, shape, axis) for axis in range(2))
    product = ((row % NZ + 1) * (col % NZ + 1)).astype(jnp.float32)
    period = 2.0 * (NZ + 1)
    turn = product - period * jnp.floor((product + 0.5) / period)
    value = math.sqrt(2.0 / (NZ + 1)) * jnp.sin(turn * (math.pi / (NZ + 1)))
    value = jnp.where(row // NZ == col // NZ, value, 0.0)
    high = value.astype(jnp.bfloat16)
    low = (value - high.astype(jnp.float32)).astype(jnp.bfloat16)
    for first in (0, LANES):
        out[pl.ds(first, LANES), pl.ds(0, LANES)] = high
        out[pl.ds(first, LANES), pl.ds(LANES, LANES)] = low


def sines(after):
    return pl.pallas_call(
        sines_kernel,
        out_shape=jax.ShapeDtypeStruct((2 * LANES, 2 * LANES), jnp.bfloat16),
        in_specs=[pl.BlockSpec(memory_space=pl.ANY)],
        out_specs=VMEM,
        compiler_params=SMALL,
        cost_estimate=pl.CostEstimate(flops=0, bytes_accessed=2 * 2**20, transcendentals=0),
        name="sines",
    )(after)


def z_tails():
    lane = lax.broadcasted_iota(jnp.int32, (SUB, LANES), 1) % NZ
    value = 2.0 * jnp.cos((lane + 1).astype(jnp.float32) * (math.pi / (NZ + 1)))
    p0, p1, p2, p3, p4 = power_coeffs()
    a3, a2, a1, a0 = p3 / p4, p2 / p4, p1 / p4, p0 / p4
    return (
        4.0 * value + a3,
        (6.0 * value + 3.0 * a3) * value + a2,
        ((4.0 * value + 3.0 * a3) * value + 2.0 * a2) * value + a1,
        (((value + a3) * value + a2) * value + a1) * value + a0,
    )


SIZE = 2 * HALO + EDGE


def within(radius):
    return [[y for y in range(SIZE) if reach(x, y) <= radius] for x in range(SIZE)]


CORE = [(x, y) for x in range(HALO, HALO + EDGE) for y in range(HALO, HALO + EDGE)]


def source_rows(ref, out, first):
    shape = (LANES, LANES)
    lane = lax.broadcasted_iota(jnp.int32, shape, 1) % NZ
    line = lax.broadcasted_iota(jnp.int32, shape, 0)
    packed = ref[spots_of(ref.shape[0]) :].reshape(-1, LANES)
    for place in range(out.shape[0]):
        repeat = (line == lane + place * NZ).astype(jnp.bfloat16)
        out[place, pl.ds(first, packed.shape[0]), :] = jnp.dot(
            packed, repeat, preferred_element_type=jnp.float32
        )
    return first + packed.shape[0]


def keep(parts, at, value):
    high = value.astype(jnp.bfloat16)
    low = (value - high.astype(jnp.float32)).astype(jnp.bfloat16)
    parts[at, :, :LANES] = high
    parts[at, :, LANES:] = low


def turned(parts, first, end, modes):
    cells = end - first
    rows = parts[first:end].reshape(cells * ROWS, 2 * LANES)
    both = jnp.dot(rows, modes[...], preferred_element_type=jnp.float32)
    return (both[:, :LANES] + both[:, LANES:]).reshape(cells, ROWS, LANES)


def densities(refs, rows, firsts, place, parts, modes, put):
    cells = [
        (ref, at, first + at)
        for ref, first in zip(refs, firsts)
        for at in range(spots_of(ref.shape[0]))
    ]
    pieces = -(-len(cells) // 48)
    for piece in range(pieces):
        start, end = (len(cells) * at // pieces for at in (piece, piece + 1))
        for number in range(start, end):
            ref, at, row = cells[number]
            other = jnp.broadcast_to(rows[place, pl.ds(row, 1), :], (ROWS, LANES))
            keep(parts, number, ref[at].astype(jnp.float32) * other)
        put(start, end, turned(parts, start, end, modes))


def all_rows(refs, rows):
    firsts = [0]
    for ref in refs:
        firsts.append(source_rows(ref, rows, firsts[-1]))
    return firsts


def modes_kernel(own, across, modes, hat, own_rows, rows, parts):
    firsts = all_rows((own, across), rows)
    own_rows[...] = rows[:, : own_rows.shape[1], :]

    for place in range(hat.shape[0]):

        def put(start, end, value, place=place):
            hat[place, start:end] = value

        densities((own, across), rows, firsts, place, parts, modes, put)


def modes_of(own, across, modes, count):
    cells = 2 * len(CORE)
    return pl.pallas_call(
        modes_kernel,
        out_shape=[
            jax.ShapeDtypeStruct((count, cells, ROWS, LANES), jnp.float32),
            jax.ShapeDtypeStruct((count, len(CORE), LANES), jnp.float32),
        ],
        in_specs=[VMEM] * 3,
        out_specs=[VMEM] * 2,
        scratch_shapes=[
            pltpu.VMEM((count, cells, LANES), jnp.float32),
            pltpu.VMEM((cells, ROWS, 2 * LANES), jnp.bfloat16),
        ],
        compiler_params=pltpu.CompilerParams(vmem_limit_bytes=20 * 2**20),
        cost_estimate=pl.CostEstimate(flops=0, bytes_accessed=6 * 2**20, transcendentals=0),
        name="modes",
    )(own, across, modes)


def fields_kernel(beside, own_rows, below, above, low, high, modes, *refs):
    out, rows, parts, back, hat, work_a, work_b, last, acc, tails = refs
    count = beside.shape[0]
    pitch = ROWS + 1
    for step, tail in enumerate(z_tails()):
        tails[step] = tail
    later = (below, above, low, high)
    firsts = all_rows(later, rows)
    offset = [0]
    for ref in later:
        offset.append(offset[-1] + spots_of(ref.shape[0]))

    def put(start, end, value):
        hat[start:end] = value

    def steps(place, half):
        part = pl.ds(half * SUB, SUB)

        def start(x, y):
            which, at = place_of(x, y)
            if which < 2:
                return beside[place, which * len(CORE) + at, part, :]
            return hat[offset[which - 2] + at, part, :]

        for step in range(DEGREE):
            new = (work_a, work_b, work_a, None)[step]
            old = (None, work_a, work_b, work_a)[step]
            targets, known = within(HALO - 1 - step), within(HALO - step)

            def load(x):
                return {y: start(x, y) if old is None else old[x, y] for y in known[x]}

            here, pair_prev = load(step), {}
            for x in range(step, SIZE - 1 - step):
                ahead, pair = load(x + 1), {}
                for y in range(SIZE - 1):
                    if y in targets[x] or y + 1 in targets[x + 1]:
                        pair[y] = ahead[y] + here[y + 1]
                    if y in targets[x]:
                        density = here[y] if old is None else start(x, y)
                        value = pair[y] + pair_prev[y - 1] + tails[step] * density
                        if new is not None:
                            new[x, y] = value
                        else:
                            last[CORE.index((x, y)), part, :] = value
                here, pair_prev = ahead, pair

    for place in range(count):
        densities(later, rows, firsts, place, parts, modes, put)
        for half in range(ROWS // SUB):
            steps(place, half)
        for at in range(len(CORE)):
            keep(back, at, last[at])
        result = turned(back, 0, len(CORE), modes)
        for at, (x, y) in enumerate(CORE):
            lanes = pl.ds((y - HALO) * pitch, ROWS)
            other = jnp.broadcast_to(own_rows[place, pl.ds(at, 1), :], (ROWS, LANES))
            value = result[at] * other
            acc[x - HALO, lanes, :] = acc[x - HALO, lanes, :] + value if place else value
    for x in range(EDGE):
        for group in range(ROWS):
            tile = acc[x, pl.ds(group, EDGE, stride=pitch), :]
            out[x, :, pl.ds(group * LANES, LANES)] = tile * (-power_coeffs()[-1])


def fields(halo, modes, count):
    own, across, *later = halo
    beside, own_rows = modes_of(own, across, modes, count)
    plane = pltpu.VMEM((SIZE, SIZE, SUB, LANES), jnp.float32)
    core = pltpu.VMEM((len(CORE), ROWS, LANES), jnp.float32)
    cells = sum(spots_of(array.shape[0]) for array in later)
    rows = ROWS * sum(array.shape[0] - spots_of(array.shape[0]) for array in later)
    return pl.pallas_call(
        fields_kernel,
        out_shape=jax.ShapeDtypeStruct((EDGE, EDGE, ROWS * LANES), jnp.float32),
        in_specs=[VMEM] * 7,
        out_specs=VMEM,
        scratch_shapes=[
            pltpu.VMEM((count, rows, LANES), jnp.float32),
            pltpu.VMEM((cells, ROWS, 2 * LANES), jnp.bfloat16),
            pltpu.VMEM((len(CORE), ROWS, 2 * LANES), jnp.bfloat16),
            pltpu.VMEM((cells, ROWS, LANES), jnp.float32),
            plane,
            plane,
            core,
            pltpu.VMEM((EDGE, EDGE * (ROWS + 1), LANES), jnp.float32),
            pltpu.VMEM((DEGREE, SUB, LANES), jnp.float32),
        ],
        compiler_params=pltpu.CompilerParams(vmem_limit_bytes=24 * 2**20),
        name="fields",
    )(beside, own_rows, *later, modes)


def body(orbitals, src_owner, src_slot):
    packed, modes = messages(orbitals, src_owner, src_slot)
    return fields((packed[0], *exchange(*packed)), modes, src_slot.size)


def solution(mesh):
    in_specs = (P("sx", "sy", "orb"), P(), P())
    out_specs = P("sx", "sy", "orb")
    return jax.shard_map(body, mesh=mesh, in_specs=in_specs, out_specs=out_specs, check_vma=False)
```

```python
import functools
import math

import jax
import jax.numpy as jnp
from jax import lax
from jax.experimental import pallas as pl
from jax.experimental.pallas import tpu as pltpu
from jax.sharding import PartitionSpec as P

NZ = 32
LANES = 128
SUB = 8
ROWS = 16
DEGREE = 4
HALO = DEGREE
EDGE = 8

CHEB = (
    1.021021021021021,
    -1.7357357357357357,
    1.4753753753753753,
    -1.254069069069069,
    1.0659587087087088,
)


def power_coeffs():
    c0, c1, c2, c3, c4 = CHEB
    return (
        c0 - c2 + c4,
        -(c1 - 3.0 * c3) / 6.0,
        (2.0 * c2 - 8.0 * c4) / 36.0,
        -4.0 * c3 / 216.0,
        8.0 * c4 / 1296.0,
    )


CORNER_LOW = tuple(
    (x, y)
    for x in range(EDGE)
    for y in range(EDGE - HALO, EDGE)
    if min(x + 1, EDGE - x) + EDGE - y <= DEGREE
)
CORNER_HIGH = tuple((x, EDGE - 1 - y) for x, y in CORNER_LOW)
SPLIT = len(CORNER_LOW) // 2


def ring(axis, step):
    count = lax.axis_size(axis)
    return [(i, (i + step) % count) for i in range(count)]


def diagonal(step_x, step_y):
    count_x, count_y = lax.axis_size("sx"), lax.axis_size("sy")
    return [
        (i * count_y + j, (i + step_x) % count_x * count_y + (j + step_y) % count_y)
        for i in range(count_x)
        for j in range(count_y)
    ]


VMEM = pl.BlockSpec(memory_space=pltpu.VMEM)
SMALL = pltpu.CompilerParams(vmem_limit_bytes=8 * 2**20)


def spread_out(values):
    return lax.broadcast_in_dim(
        values, values.shape + (ROWS, LANES), tuple(range(values.ndim))
    )


def by_seat(entries):
    rounds, places, rows, lanes = entries.shape
    seat = lax.broadcasted_iota(jnp.int32, (rows, lanes), 1) // NZ
    value = entries[0, 0]
    for index in range(1, rounds * places):
        value = jnp.where(seat == index, entries[index // places, index % places], value)
    return value


def prepare_kernel(entries, orbitals, out, cells, scratch):
    per_tile = LANES // NZ
    slot = by_seat(entries[0])[:EDGE]
    lane = lax.broadcasted_iota(jnp.int32, (EDGE, LANES), 1)
    group, turn = slot // per_tile, (lane // NZ - slot % per_tile + per_tile) % per_tile
    asked = [pltpu.roll(group, LANES - step * NZ, 1) if step else group for step in range(per_tile)]
    found = [[jnp.zeros((EDGE, LANES), jnp.float32)] * EDGE for _ in range(per_tile)]
    for number in range(ROWS):
        lanes = pl.ds(number * LANES, LANES)
        tiles = [orbitals[row, :, lanes].astype(jnp.float32) for row in range(EDGE)]
        for step in range(per_tile):
            here = asked[step] == number
            found[step] = [jnp.where(here, tile, old) for tile, old in zip(tiles, found[step])]
    rows = []
    for row in range(EDGE):
        packed = found[0][row]
        for step in range(1, per_tile):
            packed = jnp.where(turn == step, pltpu.roll(found[step][row], step * NZ, 1), packed)
        rows.append(packed)
    for tile in range(EDGE // 2):
        out[tile] = jnp.concatenate(rows[2 * tile : 2 * tile + 2], axis=0).astype(jnp.bfloat16)
    for row in range(EDGE):
        for group in range(ROWS):
            tile = orbitals[row, :, pl.ds(group * LANES, LANES)].astype(jnp.float32)
            scratch[row, pl.ds(group, EDGE, stride=ROWS + 1), :] = tile
    for row in range(EDGE):
        for y in range(EDGE):
            tile = scratch[row, pl.ds(y * (ROWS + 1), ROWS), :]
            cells[row * EDGE + y] = tile.astype(jnp.bfloat16)


def prepare(entries, orbitals):
    lengths = (EDGE * EDGE // ROWS, EDGE * EDGE)
    return pl.pallas_call(
        prepare_kernel,
        out_shape=[jax.ShapeDtypeStruct((length, ROWS, LANES), jnp.bfloat16) for length in lengths],
        in_specs=[VMEM] * 2,
        out_specs=[VMEM] * 2,
        scratch_shapes=[pltpu.VMEM((EDGE, EDGE * (ROWS + 1), LANES), jnp.float32)],
        compiler_params=SMALL,
        name="prepare",
    )(entries, orbitals)


def chosen(entries, mine, others, bit):
    owner, me = by_seat(entries[1]), lax.axis_index("orb")
    count = lax.axis_size("orb")
    picked = []
    for tile in range(mine.shape[0]):
        value = mine[tile].astype(jnp.float32)
        for step, other in enumerate(others, 1):
            if bit is None:
                here = owner == lax.rem(me + count - step, count)
            else:
                here = (owner >> bit & 1) != (me >> bit & 1)
            value = jnp.where(here, other[tile].astype(jnp.float32), value)
        picked.append(value)
    return picked


def nearer_kernel(bit, entries, mine, other, out):
    for tile, value in enumerate(chosen(entries, mine, [other], bit)):
        out[tile] = value.astype(jnp.bfloat16)


def gathered(entries, mine):
    count = lax.axis_size("orb")
    if count & (count - 1):
        others = [lax.ppermute(mine, "orb", ring("orb", step)) for step in range(1, count)]
        return mine, others, None
    bits = count.bit_length() - 1
    for bit in range(bits):
        other = lax.ppermute(mine, "orb", [(i, i ^ 1 << bit) for i in range(count)])
        if bit == bits - 1:
            return mine, [other], bit
        mine = pl.pallas_call(
            functools.partial(nearer_kernel, bit),
            out_shape=jax.ShapeDtypeStruct(mine.shape, mine.dtype),
            in_specs=[VMEM] * 3,
            out_specs=VMEM,
            compiler_params=SMALL,
            name="nearer",
        )(entries, mine, other)
    return mine, [], None


def messages_kernel(bit, before, entries, cells, mine, *refs):
    others, (block, last, first, corner_low, corner_high) = refs[:-5], refs[-5:]
    picked = chosen(entries, mine, others, bit)

    def pack(ref, spots):
        for at, (x, y) in enumerate(spots):
            ref[at] = cells[x * EDGE + y]
        used = len(spots)
        runs = []
        for x, y in spots:
            if runs and runs[-1][0] == x and runs[-1][2] == y:
                runs[-1][2] = y + 1
            else:
                runs.append([x, y, y + 1])
        parts = [
            picked[x * EDGE // ROWS][x * EDGE % ROWS + low : x * EDGE % ROWS + high]
            for x, low, high in runs
        ]
        if used % ROWS:
            parts.append(jnp.zeros((ROWS - used % ROWS, LANES), jnp.float32))
        rows = jnp.concatenate(parts, axis=0).astype(jnp.bfloat16)
        for tile in range(rows.shape[0] // ROWS):
            ref[used + tile] = rows[tile * ROWS : (tile + 1) * ROWS]

    pack(block, [(x, y) for x in range(EDGE) for y in range(EDGE)])
    pack(last, [(x, y) for x in range(EDGE) for y in range(EDGE - HALO, EDGE)])
    pack(first, [(x, y) for x in range(EDGE) for y in range(HALO)])
    pack(corner_low, CORNER_LOW)
    pack(corner_high, CORNER_HIGH)


def tiles(spots):
    return spots + -(-spots // ROWS)


def spots_of(length):
    return length * ROWS // (ROWS + 1)


def messages(orbitals, src_owner, src_slot):
    entries = spread_out(jnp.stack([src_slot, src_owner]))
    mine, cells = prepare(entries, orbitals)
    mine, others, bit = gathered(entries, mine)
    lengths = [EDGE * EDGE] + [EDGE * HALO] * 2 + [len(CORNER_LOW)] * 2
    modes = sines(mine)
    packed = pl.pallas_call(
        functools.partial(messages_kernel, bit),
        out_shape=[
            jax.ShapeDtypeStruct((tiles(length), ROWS, LANES), jnp.bfloat16) for length in lengths
        ],
        in_specs=[pl.BlockSpec(memory_space=pl.ANY)] + [VMEM] * (3 + len(others)),
        out_specs=[VMEM] * 5,
        compiler_params=SMALL,
        name="messages",
    )(modes, entries, cells, mine, *others)
    return packed, modes


def exchange(block, last, first, corner_low, corner_high):
    both = ("sx", "sy")
    if lax.axis_size("sx") == 2:
        low = lax.ppermute(corner_low, both, diagonal(1, 1))
        high = lax.ppermute(corner_high, both, diagonal(1, -1))
        across = lax.ppermute(block, "sx", ring("sx", 1))
    else:
        def two_ways(cells, half, axes, down, up, merge):
            end = 2 * half
            back = lax.ppermute(jnp.concatenate([cells[:half], cells[end:]]), axes, down)
            ahead = lax.ppermute(jnp.concatenate([cells[half:end], cells[end:]]), axes, up)
            return jnp.concatenate([back[:half], ahead[:half], merge(back[half:], ahead[half:])])

        def halves(back, ahead):
            return jnp.concatenate([back[: back.shape[0] // 2], ahead[ahead.shape[0] // 2 :]])

        def rows(back, ahead):
            return jnp.concatenate([back[:, :SPLIT], ahead[:, SPLIT:]], axis=1)

        low = two_ways(corner_low, SPLIT, both, diagonal(-1, 1), diagonal(1, 1), rows)
        high = two_ways(corner_high, SPLIT, both, diagonal(-1, -1), diagonal(1, -1), rows)
        across = two_ways(block, EDGE * HALO, "sx", ring("sx", -1), ring("sx", 1), halves)
    below = lax.ppermute(last, "sy", ring("sy", 1))
    above = lax.ppermute(first, "sy", ring("sy", -1))
    return across, below, above, low, high


def place_of(x, y):
    row, core_x = (x - HALO) % EDGE, HALO <= x < HALO + EDGE
    if HALO <= y < HALO + EDGE:
        return (0 if core_x else 1), row * EDGE + y - HALO
    if y < HALO:
        return (2, row * HALO + y) if core_x else (4, CORNER_LOW.index((row, y + EDGE - HALO)))
    y = y - HALO - EDGE
    return (3, row * HALO + y) if core_x else (5, CORNER_HIGH.index((row, y)))


def reach(x, y):
    out_x = max(HALO - x, x - (HALO + EDGE - 1), 0)
    out_y = max(HALO - y, y - (HALO + EDGE - 1), 0)
    return out_x + out_y


def sines_kernel(after, out):
    shape = (LANES, LANES)
    row, col = (lax.broadcasted_iota(jnp.int32, shape, axis) for axis in range(2))
    product = ((row % NZ + 1) * (col % NZ + 1)).astype(jnp.float32)
    period = 2.0 * (NZ + 1)
    turn = product - period * jnp.floor((product + 0.5) / period)
    value = math.sqrt(2.0 / (NZ + 1)) * jnp.sin(turn * (math.pi / (NZ + 1)))
    value = jnp.where(row // NZ == col // NZ, value, 0.0)
    high = value.astype(jnp.bfloat16)
    low = (value - high.astype(jnp.float32)).astype(jnp.bfloat16)
    for first in (0, LANES):
        out[pl.ds(first, LANES), pl.ds(0, LANES)] = high
        out[pl.ds(first, LANES), pl.ds(LANES, LANES)] = low


def sines(after):
    return pl.pallas_call(
        sines_kernel,
        out_shape=jax.ShapeDtypeStruct((2 * LANES, 2 * LANES), jnp.bfloat16),
        in_specs=[pl.BlockSpec(memory_space=pl.ANY)],
        out_specs=VMEM,
        compiler_params=SMALL,
        cost_estimate=pl.CostEstimate(flops=0, bytes_accessed=2 * 2**20, transcendentals=0),
        name="sines",
    )(after)


def z_tails():
    lane = lax.broadcasted_iota(jnp.int32, (SUB, LANES), 1) % NZ
    value = 2.0 * jnp.cos((lane + 1).astype(jnp.float32) * (math.pi / (NZ + 1)))
    p0, p1, p2, p3, p4 = power_coeffs()
    a3, a2, a1, a0 = p3 / p4, p2 / p4, p1 / p4, p0 / p4
    return (
        4.0 * value + a3,
        (6.0 * value + 3.0 * a3) * value + a2,
        ((4.0 * value + 3.0 * a3) * value + 2.0 * a2) * value + a1,
        (((value + a3) * value + a2) * value + a1) * value + a0,
    )


SIZE = 2 * HALO + EDGE


def within(radius):
    return [[y for y in range(SIZE) if reach(x, y) <= radius] for x in range(SIZE)]


CORE = [(x, y) for x in range(HALO, HALO + EDGE) for y in range(HALO, HALO + EDGE)]


def source_rows(ref, out, first):
    shape = (LANES, LANES)
    lane = lax.broadcasted_iota(jnp.int32, shape, 1) % NZ
    line = lax.broadcasted_iota(jnp.int32, shape, 0)
    packed = ref[spots_of(ref.shape[0]) :].reshape(-1, LANES)
    for place in range(out.shape[0]):
        repeat = (line == lane + place * NZ).astype(jnp.bfloat16)
        out[place, pl.ds(first, packed.shape[0]), :] = jnp.dot(
            packed, repeat, preferred_element_type=jnp.float32
        )
    return first + packed.shape[0]


def keep(parts, at, value):
    high = value.astype(jnp.bfloat16)
    low = (value - high.astype(jnp.float32)).astype(jnp.bfloat16)
    parts[at, :, :LANES] = high
    parts[at, :, LANES:] = low


def turned(parts, first, end, modes):
    cells = end - first
    rows = parts[first:end].reshape(cells * ROWS, 2 * LANES)
    both = jnp.dot(rows, modes[...], preferred_element_type=jnp.float32)
    return (both[:, :LANES] + both[:, LANES:]).reshape(cells, ROWS, LANES)


def densities(refs, rows, firsts, place, parts, modes, put):
    cells = [
        (ref, at, first + at)
        for ref, first in zip(refs, firsts)
        for at in range(spots_of(ref.shape[0]))
    ]
    pieces = -(-len(cells) // 48)
    for piece in range(pieces):
        start, end = (len(cells) * at // pieces for at in (piece, piece + 1))
        for number in range(start, end):
            ref, at, row = cells[number]
            other = jnp.broadcast_to(rows[place, pl.ds(row, 1), :], (ROWS, LANES))
            keep(parts, number, ref[at].astype(jnp.float32) * other)
        put(start, end, turned(parts, start, end, modes))


def all_rows(refs, rows):
    firsts = [0]
    for ref in refs:
        firsts.append(source_rows(ref, rows, firsts[-1]))
    return firsts


def early(step):
    cells = [
        (x, y)
        for x in range(1 + step, SIZE - 1 - step)
        for y in range(HALO + 1 + step, HALO + EDGE - 1 - step)
    ]
    return {cell: at for at, cell in enumerate(cells)}


EARLY = [early(step) for step in range(DEGREE - 1)]


def one_step(targets, old, tail, density, put):
    pairs = targets | {(x - 1, y - 1) for x, y in targets}
    wanted = {(x + 1, y) for x, y in pairs} | {(x, y + 1) for x, y in pairs}
    loaded, summed = {}, {}
    rows = sorted({x for x, _ in pairs})
    for x in rows:
        for cell in sorted(cell for cell in wanted if cell[0] in (x, x + 1)):
            if cell not in loaded:
                loaded[cell] = old(*cell)
        for y in range(SIZE):
            if (x, y) in pairs:
                summed[x, y] = loaded[x + 1, y] + loaded[x, y + 1]
            if (x, y) in targets:
                here = loaded.get((x, y)) if old is density else None
                here = density(x, y) if here is None else here
                put(x, y, summed[x, y] + summed[x - 1, y - 1] + tail[...] * here)


def modes_kernel(own, across, modes, hat, own_rows, *refs):
    stages, (rows, parts, tails) = refs[: DEGREE - 1], refs[DEGREE - 1 :]
    for step, tail in enumerate(z_tails()):
        tails[step] = tail
    firsts = all_rows((own, across), rows)
    own_rows[...] = rows[:, : own_rows.shape[1], :]
    for place in range(hat.shape[0]):

        def put(start, end, value, place=place):
            hat[place, start:end] = value

        densities((own, across), rows, firsts, place, parts, modes, put)
        for half in range(ROWS // SUB):
            part = pl.ds(half * SUB, SUB)

            def start(x, y, place=place, part=part):
                which, at = place_of(x, y)
                return hat[place, which * len(CORE) + at, part, :]

            old = start
            for step, stage in enumerate(stages):

                def load(x, y, place=place, part=part, stage=stage, step=step):
                    return stage[place, EARLY[step][x, y], part, :]

                def store(x, y, value, place=place, part=part, stage=stage, step=step):
                    stage[place, EARLY[step][x, y], part, :] = value

                one_step(set(EARLY[step]), old, tails.at[step], start, store)
                old = load


def modes_of(own, across, modes, count):
    cells = 2 * len(CORE)
    lengths = [cells] + [len(stage) for stage in EARLY]
    shapes = [(count, length, ROWS, LANES) for length in lengths]
    shapes.insert(1, (count, len(CORE), LANES))
    return pl.pallas_call(
        modes_kernel,
        out_shape=[jax.ShapeDtypeStruct(shape, jnp.float32) for shape in shapes],
        in_specs=[VMEM] * 3,
        out_specs=[VMEM] * len(shapes),
        scratch_shapes=[
            pltpu.VMEM((count, cells, LANES), jnp.float32),
            pltpu.VMEM((cells, ROWS, 2 * LANES), jnp.bfloat16),
            pltpu.VMEM((DEGREE, SUB, LANES), jnp.float32),
        ],
        compiler_params=pltpu.CompilerParams(vmem_limit_bytes=20 * 2**20),
        cost_estimate=pl.CostEstimate(flops=0, bytes_accessed=6 * 2**20, transcendentals=0),
        name="modes",
    )(own, across, modes)


def fields_kernel(beside, own_rows, *refs):
    stages, (below, above, low, high, modes, out) = refs[: DEGREE - 1], refs[DEGREE - 1 :][:6]
    rows, parts, back, hat, work_a, work_b, last, acc, tails = refs[DEGREE + 5 :]
    count = beside.shape[0]
    pitch = ROWS + 1
    for step, tail in enumerate(z_tails()):
        tails[step] = tail
    later = (below, above, low, high)
    firsts = all_rows(later, rows)
    offset = [0]
    for ref in later:
        offset.append(offset[-1] + spots_of(ref.shape[0]))

    def put(start, end, value):
        hat[start:end] = value

    def steps(place, half):
        part = pl.ds(half * SUB, SUB)

        def start(x, y):
            which, at = place_of(x, y)
            if which < 2:
                return beside[place, which * len(CORE) + at, part, :]
            return hat[offset[which - 2] + at, part, :]

        old = start
        for step in range(DEGREE):
            new = (work_a, work_b, work_a, None)[step]
            ready = EARLY[step] if step < DEGREE - 1 else {}

            def load(x, y, new=new, step=step, ready=ready):
                if (x, y) in ready:
                    return stages[step][place, ready[x, y], part, :]
                return new[x, y]

            def store(x, y, value, new=new):
                if new is None:
                    last[CORE.index((x, y)), part, :] = value
                else:
                    new[x, y] = value

            cells = {(x, y) for x in range(SIZE) for y in within(HALO - 1 - step)[x]}
            one_step(cells - set(ready), old, tails.at[step], start, store)
            old = load

    for place in range(count):
        densities(later, rows, firsts, place, parts, modes, put)
        for half in range(ROWS // SUB):
            steps(place, half)
        for at in range(len(CORE)):
            keep(back, at, last[at])
        result = turned(back, 0, len(CORE), modes)
        for at, (x, y) in enumerate(CORE):
            lanes = pl.ds((y - HALO) * pitch, ROWS)
            other = jnp.broadcast_to(own_rows[place, pl.ds(at, 1), :], (ROWS, LANES))
            value = result[at] * other
            acc[x - HALO, lanes, :] = acc[x - HALO, lanes, :] + value if place else value
    for x in range(EDGE):
        for group in range(ROWS):
            tile = acc[x, pl.ds(group, EDGE, stride=pitch), :]
            out[x, :, pl.ds(group * LANES, LANES)] = tile * (-power_coeffs()[-1])


def fields(halo, modes, count):
    own, across, *later = halo
    beside, own_rows, *stages = modes_of(own, across, modes, count)
    plane = pltpu.VMEM((SIZE, SIZE, SUB, LANES), jnp.float32)
    core = pltpu.VMEM((len(CORE), ROWS, LANES), jnp.float32)
    cells = sum(spots_of(array.shape[0]) for array in later)
    rows = ROWS * sum(array.shape[0] - spots_of(array.shape[0]) for array in later)
    return pl.pallas_call(
        fields_kernel,
        out_shape=jax.ShapeDtypeStruct((EDGE, EDGE, ROWS * LANES), jnp.float32),
        in_specs=[VMEM] * (7 + len(stages)),
        out_specs=VMEM,
        scratch_shapes=[
            pltpu.VMEM((count, rows, LANES), jnp.float32),
            pltpu.VMEM((cells, ROWS, 2 * LANES), jnp.bfloat16),
            pltpu.VMEM((len(CORE), ROWS, 2 * LANES), jnp.bfloat16),
            pltpu.VMEM((cells, ROWS, LANES), jnp.float32),
            plane,
            plane,
            core,
            pltpu.VMEM((EDGE, EDGE * (ROWS + 1), LANES), jnp.float32),
            pltpu.VMEM((DEGREE, SUB, LANES), jnp.float32),
        ],
        compiler_params=pltpu.CompilerParams(vmem_limit_bytes=24 * 2**20),
        name="fields",
    )(beside, own_rows, *stages, *later, modes)


def body(orbitals, src_owner, src_slot):
    packed, modes = messages(orbitals, src_owner, src_slot)
    return fields((packed[0], *exchange(*packed)), modes, src_slot.size)


def solution(mesh):
    in_specs = (P("sx", "sy", "orb"), P(), P())
    out_specs = P("sx", "sy", "orb")
    return jax.shard_map(body, mesh=mesh, in_specs=in_specs, out_specs=out_specs, check_vma=False)
```

```python
import functools
import math

import jax
import jax.numpy as jnp
from jax import lax
from jax.experimental import pallas as pl
from jax.experimental.pallas import tpu as pltpu
from jax.sharding import PartitionSpec as P

NZ = 32
LANES = 128
SUB = 8
ROWS = 16
DEGREE = 4
HALO = DEGREE
EDGE = 8

CHEB = (
    1.021021021021021,
    -1.7357357357357357,
    1.4753753753753753,
    -1.254069069069069,
    1.0659587087087088,
)


def power_coeffs():
    c0, c1, c2, c3, c4 = CHEB
    return (
        c0 - c2 + c4,
        -(c1 - 3.0 * c3) / 6.0,
        (2.0 * c2 - 8.0 * c4) / 36.0,
        -4.0 * c3 / 216.0,
        8.0 * c4 / 1296.0,
    )


CORNER_LOW = tuple(
    (x, y)
    for x in range(EDGE)
    for y in range(EDGE - HALO, EDGE)
    if min(x + 1, EDGE - x) + EDGE - y <= DEGREE
)
CORNER_HIGH = tuple((x, EDGE - 1 - y) for x, y in CORNER_LOW)
SPLIT = len(CORNER_LOW) // 2


def ring(axis, step):
    count = lax.axis_size(axis)
    return [(i, (i + step) % count) for i in range(count)]


def diagonal(step_x, step_y):
    count_x, count_y = lax.axis_size("sx"), lax.axis_size("sy")
    return [
        (i * count_y + j, (i + step_x) % count_x * count_y + (j + step_y) % count_y)
        for i in range(count_x)
        for j in range(count_y)
    ]


VMEM = pl.BlockSpec(memory_space=pltpu.VMEM)
SMALL = pltpu.CompilerParams(vmem_limit_bytes=8 * 2**20)


def spread_out(values):
    return lax.broadcast_in_dim(
        values, values.shape + (ROWS, LANES), tuple(range(values.ndim))
    )


def by_seat(entries):
    rounds, places, rows, lanes = entries.shape
    seat = lax.broadcasted_iota(jnp.int32, (rows, lanes), 1) // NZ
    value = entries[0, 0]
    for index in range(1, rounds * places):
        value = jnp.where(seat == index, entries[index // places, index % places], value)
    return value


def prepare_kernel(entries, orbitals, out, cells, scratch):
    per_tile = LANES // NZ
    slot = by_seat(entries[0])[:EDGE]
    lane = lax.broadcasted_iota(jnp.int32, (EDGE, LANES), 1)
    group, turn = slot // per_tile, (lane // NZ - slot % per_tile + per_tile) % per_tile
    asked = [pltpu.roll(group, LANES - step * NZ, 1) if step else group for step in range(per_tile)]
    found = [[jnp.zeros((EDGE, LANES), jnp.float32)] * EDGE for _ in range(per_tile)]
    for number in range(ROWS):
        lanes = pl.ds(number * LANES, LANES)
        tiles = [orbitals[row, :, lanes].astype(jnp.float32) for row in range(EDGE)]
        for step in range(per_tile):
            here = asked[step] == number
            found[step] = [jnp.where(here, tile, old) for tile, old in zip(tiles, found[step])]
    rows = []
    for row in range(EDGE):
        packed = found[0][row]
        for step in range(1, per_tile):
            packed = jnp.where(turn == step, pltpu.roll(found[step][row], step * NZ, 1), packed)
        rows.append(packed)
    for tile in range(EDGE // 2):
        out[tile] = jnp.concatenate(rows[2 * tile : 2 * tile + 2], axis=0).astype(jnp.bfloat16)
    for row in range(EDGE):
        for group in range(ROWS):
            tile = orbitals[row, :, pl.ds(group * LANES, LANES)].astype(jnp.float32)
            scratch[row, pl.ds(group, EDGE, stride=ROWS + 1), :] = tile
    for row in range(EDGE):
        for y in range(EDGE):
            tile = scratch[row, pl.ds(y * (ROWS + 1), ROWS), :]
            cells[row * EDGE + y] = tile.astype(jnp.bfloat16)


def prepare(entries, orbitals):
    lengths = (EDGE * EDGE // ROWS, EDGE * EDGE)
    return pl.pallas_call(
        prepare_kernel,
        out_shape=[jax.ShapeDtypeStruct((length, ROWS, LANES), jnp.bfloat16) for length in lengths],
        in_specs=[VMEM] * 2,
        out_specs=[VMEM] * 2,
        scratch_shapes=[pltpu.VMEM((EDGE, EDGE * (ROWS + 1), LANES), jnp.float32)],
        compiler_params=SMALL,
        name="prepare",
    )(entries, orbitals)


def chosen(entries, mine, others, bit):
    owner, me = by_seat(entries[1]), lax.axis_index("orb")
    count = lax.axis_size("orb")
    picked = []
    for tile in range(mine.shape[0]):
        value = mine[tile].astype(jnp.float32)
        for step, other in enumerate(others, 1):
            if bit is None:
                here = owner == lax.rem(me + count - step, count)
            else:
                here = (owner >> bit & 1) != (me >> bit & 1)
            value = jnp.where(here, other[tile].astype(jnp.float32), value)
        picked.append(value)
    return picked


def nearer_kernel(bit, entries, mine, other, out):
    for tile, value in enumerate(chosen(entries, mine, [other], bit)):
        out[tile] = value.astype(jnp.bfloat16)


def gathered(entries, mine):
    count = lax.axis_size("orb")
    if count & (count - 1):
        others = [lax.ppermute(mine, "orb", ring("orb", step)) for step in range(1, count)]
        return mine, others, None
    bits = count.bit_length() - 1
    for bit in range(bits):
        other = lax.ppermute(mine, "orb", [(i, i ^ 1 << bit) for i in range(count)])
        if bit == bits - 1:
            return mine, [other], bit
        mine = pl.pallas_call(
            functools.partial(nearer_kernel, bit),
            out_shape=jax.ShapeDtypeStruct(mine.shape, mine.dtype),
            in_specs=[VMEM] * 3,
            out_specs=VMEM,
            compiler_params=SMALL,
            name="nearer",
        )(entries, mine, other)
    return mine, [], None


def messages_kernel(bit, before, entries, cells, mine, *refs):
    others, (block, last, first, corner_low, corner_high) = refs[:-5], refs[-5:]
    picked = chosen(entries, mine, others, bit)

    def pack(ref, spots):
        for at, (x, y) in enumerate(spots):
            ref[at] = cells[x * EDGE + y]
        used = len(spots)
        runs = []
        for x, y in spots:
            if runs and runs[-1][0] == x and runs[-1][2] == y:
                runs[-1][2] = y + 1
            else:
                runs.append([x, y, y + 1])
        parts = [
            picked[x * EDGE // ROWS][x * EDGE % ROWS + low : x * EDGE % ROWS + high]
            for x, low, high in runs
        ]
        if used % ROWS:
            parts.append(jnp.zeros((ROWS - used % ROWS, LANES), jnp.float32))
        rows = jnp.concatenate(parts, axis=0).astype(jnp.bfloat16)
        for tile in range(rows.shape[0] // ROWS):
            ref[used + tile] = rows[tile * ROWS : (tile + 1) * ROWS]

    pack(block, [(x, y) for x in range(EDGE) for y in range(EDGE)])
    pack(last, [(x, y) for x in range(EDGE) for y in range(EDGE - HALO, EDGE)])
    pack(first, [(x, y) for x in range(EDGE) for y in range(HALO)])
    pack(corner_low, CORNER_LOW)
    pack(corner_high, CORNER_HIGH)


def tiles(spots):
    return spots + -(-spots // ROWS)


def spots_of(length):
    return length * ROWS // (ROWS + 1)


def messages(orbitals, src_owner, src_slot):
    entries = spread_out(jnp.stack([src_slot, src_owner]))
    mine, cells = prepare(entries, orbitals)
    mine, others, bit = gathered(entries, mine)
    lengths = [EDGE * EDGE] + [EDGE * HALO] * 2 + [len(CORNER_LOW)] * 2
    modes = sines(mine)
    packed = pl.pallas_call(
        functools.partial(messages_kernel, bit),
        out_shape=[
            jax.ShapeDtypeStruct((tiles(length), ROWS, LANES), jnp.bfloat16) for length in lengths
        ],
        in_specs=[pl.BlockSpec(memory_space=pl.ANY)] + [VMEM] * (3 + len(others)),
        out_specs=[VMEM] * 5,
        compiler_params=SMALL,
        name="messages",
    )(modes, entries, cells, mine, *others)
    return packed, modes


def exchange(block, last, first, corner_low, corner_high):
    both = ("sx", "sy")
    if lax.axis_size("sx") == 2:
        low = lax.ppermute(corner_low, both, diagonal(1, 1))
        high = lax.ppermute(corner_high, both, diagonal(1, -1))
        across = lax.ppermute(block, "sx", ring("sx", 1))
    else:
        def two_ways(cells, half, axes, down, up, merge):
            end = 2 * half
            back = lax.ppermute(jnp.concatenate([cells[:half], cells[end:]]), axes, down)
            ahead = lax.ppermute(jnp.concatenate([cells[half:end], cells[end:]]), axes, up)
            return jnp.concatenate([back[:half], ahead[:half], merge(back[half:], ahead[half:])])

        def halves(back, ahead):
            return jnp.concatenate([back[: back.shape[0] // 2], ahead[ahead.shape[0] // 2 :]])

        def rows(back, ahead):
            return jnp.concatenate([back[:, :SPLIT], ahead[:, SPLIT:]], axis=1)

        low = two_ways(corner_low, SPLIT, both, diagonal(-1, 1), diagonal(1, 1), rows)
        high = two_ways(corner_high, SPLIT, both, diagonal(-1, -1), diagonal(1, -1), rows)
        across = two_ways(block, EDGE * HALO, "sx", ring("sx", -1), ring("sx", 1), halves)
    below = lax.ppermute(last, "sy", ring("sy", 1))
    above = lax.ppermute(first, "sy", ring("sy", -1))
    return across, below, above, low, high


def place_of(x, y):
    row, core_x = (x - HALO) % EDGE, HALO <= x < HALO + EDGE
    if HALO <= y < HALO + EDGE:
        return (0 if core_x else 1), row * EDGE + y - HALO
    if y < HALO:
        return (2, row * HALO + y) if core_x else (4, CORNER_LOW.index((row, y + EDGE - HALO)))
    y = y - HALO - EDGE
    return (3, row * HALO + y) if core_x else (5, CORNER_HIGH.index((row, y)))


def reach(x, y):
    out_x = max(HALO - x, x - (HALO + EDGE - 1), 0)
    out_y = max(HALO - y, y - (HALO + EDGE - 1), 0)
    return out_x + out_y


def sines_kernel(after, out):
    shape = (LANES, LANES)
    row, col = (lax.broadcasted_iota(jnp.int32, shape, axis) for axis in range(2))
    product = ((row % NZ + 1) * (col % NZ + 1)).astype(jnp.float32)
    period = 2.0 * (NZ + 1)
    turn = product - period * jnp.floor((product + 0.5) / period)
    value = math.sqrt(2.0 / (NZ + 1)) * jnp.sin(turn * (math.pi / (NZ + 1)))
    value = jnp.where(row // NZ == col // NZ, value, 0.0)
    high = value.astype(jnp.bfloat16)
    low = (value - high.astype(jnp.float32)).astype(jnp.bfloat16)
    for first in (0, LANES):
        out[pl.ds(first, LANES), pl.ds(0, LANES)] = high
        out[pl.ds(first, LANES), pl.ds(LANES, LANES)] = low


def sines(after):
    return pl.pallas_call(
        sines_kernel,
        out_shape=jax.ShapeDtypeStruct((2 * LANES, 2 * LANES), jnp.bfloat16),
        in_specs=[pl.BlockSpec(memory_space=pl.ANY)],
        out_specs=VMEM,
        compiler_params=SMALL,
        cost_estimate=pl.CostEstimate(flops=0, bytes_accessed=2 * 2**20, transcendentals=0),
        name="sines",
    )(after)


def z_tails():
    lane = lax.broadcasted_iota(jnp.int32, (SUB, LANES), 1) % NZ
    value = 2.0 * jnp.cos((lane + 1).astype(jnp.float32) * (math.pi / (NZ + 1)))
    p0, p1, p2, p3, p4 = power_coeffs()
    a3, a2, a1, a0 = p3 / p4, p2 / p4, p1 / p4, p0 / p4
    return (
        4.0 * value + a3,
        (6.0 * value + 3.0 * a3) * value + a2,
        ((4.0 * value + 3.0 * a3) * value + 2.0 * a2) * value + a1,
        (((value + a3) * value + a2) * value + a1) * value + a0,
    )


SIZE = 2 * HALO + EDGE


def within(radius):
    return [[y for y in range(SIZE) if reach(x, y) <= radius] for x in range(SIZE)]


CORE = [(x, y) for x in range(HALO, HALO + EDGE) for y in range(HALO, HALO + EDGE)]


def source_rows(ref, out, first):
    shape = (LANES, LANES)
    lane = lax.broadcasted_iota(jnp.int32, shape, 1) % NZ
    line = lax.broadcasted_iota(jnp.int32, shape, 0)
    packed = ref[spots_of(ref.shape[0]) :].reshape(-1, LANES)
    for place in range(out.shape[0]):
        repeat = (line == lane + place * NZ).astype(jnp.bfloat16)
        out[place, pl.ds(first, packed.shape[0]), :] = jnp.dot(
            packed, repeat, preferred_element_type=jnp.float32
        )
    return first + packed.shape[0]


def keep(parts, at, value):
    high = value.astype(jnp.bfloat16)
    low = (value - high.astype(jnp.float32)).astype(jnp.bfloat16)
    parts[at, :, :LANES] = high
    parts[at, :, LANES:] = low


def turned(parts, first, end, modes):
    cells = end - first
    rows = parts[first:end].reshape(cells * ROWS, 2 * LANES)
    both = jnp.dot(rows, modes[...], preferred_element_type=jnp.float32)
    return (both[:, :LANES] + both[:, LANES:]).reshape(cells, ROWS, LANES)


def densities(refs, rows, parts, modes, hat):
    count = hat.shape[0]
    firsts = all_rows(refs, rows)
    cells = [
        (ref, at, first + at)
        for ref, first in zip(refs, firsts)
        for at in range(spots_of(ref.shape[0]))
    ]
    pieces = -(-len(cells) // 48)
    for piece in range(pieces):
        start, end = (len(cells) * at // pieces for at in (piece, piece + 1))
        for number in range(start, end):
            ref, at, row = cells[number]
            value = ref[at].astype(jnp.float32)
            for place in range(count):
                other = jnp.broadcast_to(rows[place, pl.ds(row, 1), :], (ROWS, LANES))
                keep(parts.at[place], number, value * other)
        for place in range(count):
            hat[place, start:end] = turned(parts.at[place], start, end, modes)


def all_rows(refs, rows):
    firsts = [0]
    for ref in refs:
        firsts.append(source_rows(ref, rows, firsts[-1]))
    return firsts


def early(step):
    cells = [
        (x, y)
        for x in range(1 + step, SIZE - 1 - step)
        for y in range(HALO + 1 + step, HALO + EDGE - 1 - step)
    ]
    return {cell: at for at, cell in enumerate(cells)}


EARLY = [early(step) for step in range(DEGREE - 1)]


def one_step(targets, old, tail, density, put):
    pairs = targets | {(x - 1, y - 1) for x, y in targets}
    wanted = {(x + 1, y) for x, y in pairs} | {(x, y + 1) for x, y in pairs}
    loaded, summed = {}, {}
    rows = sorted({x for x, _ in pairs})
    for x in rows:
        for cell in sorted(cell for cell in wanted if cell[0] in (x, x + 1)):
            if cell not in loaded:
                loaded[cell] = old(*cell)
        for y in range(SIZE):
            if (x, y) in pairs:
                summed[x, y] = loaded[x + 1, y] + loaded[x, y + 1]
            if (x, y) in targets:
                here = loaded.get((x, y)) if old is density else None
                here = density(x, y) if here is None else here
                put(x, y, summed[x, y] + summed[x - 1, y - 1] + tail[...] * here)


def modes_kernel(own, across, modes, hat, own_rows, *refs):
    stages, (rows, parts, tails) = refs[: DEGREE - 1], refs[DEGREE - 1 :]
    for step, tail in enumerate(z_tails()):
        tails[step] = tail
    densities((own, across), rows, parts, modes, hat)
    own_rows[...] = rows[:, : own_rows.shape[1], :] * (-power_coeffs()[-1])
    for place in range(hat.shape[0]):
        for half in range(ROWS // SUB):
            part = pl.ds(half * SUB, SUB)

            def start(x, y, place=place, part=part):
                which, at = place_of(x, y)
                return hat[place, which * len(CORE) + at, part, :]

            old = start
            for step, stage in enumerate(stages):

                def load(x, y, place=place, part=part, stage=stage, step=step):
                    return stage[place, EARLY[step][x, y], part, :]

                def store(x, y, value, place=place, part=part, stage=stage, step=step):
                    stage[place, EARLY[step][x, y], part, :] = value

                one_step(set(EARLY[step]), old, tails.at[step], start, store)
                old = load


def modes_of(own, across, modes, count):
    cells = 2 * len(CORE)
    lengths = [cells] + [len(stage) for stage in EARLY]
    shapes = [(count, length, ROWS, LANES) for length in lengths]
    shapes.insert(1, (count, len(CORE), LANES))
    return pl.pallas_call(
        modes_kernel,
        out_shape=[jax.ShapeDtypeStruct(shape, jnp.float32) for shape in shapes],
        in_specs=[VMEM] * 3,
        out_specs=[VMEM] * len(shapes),
        scratch_shapes=[
            pltpu.VMEM((count, cells, LANES), jnp.float32),
            pltpu.VMEM((count, cells, ROWS, 2 * LANES), jnp.bfloat16),
            pltpu.VMEM((DEGREE, SUB, LANES), jnp.float32),
        ],
        compiler_params=pltpu.CompilerParams(vmem_limit_bytes=20 * 2**20),
        cost_estimate=pl.CostEstimate(flops=0, bytes_accessed=6 * 2**20, transcendentals=0),
        name="modes",
    )(own, across, modes)


def fields_kernel(beside, own_rows, *refs):
    stages, (below, above, low, high, modes, out) = refs[: DEGREE - 1], refs[DEGREE - 1 :][:6]
    rows, parts, back, hat, work_a, work_b, last, acc, held, tails, sems = refs[DEGREE + 5 :]
    count = beside.shape[0]
    pitch = ROWS + 1
    for step, tail in enumerate(z_tails()):
        tails[step] = tail
    later = (below, above, low, high)
    offset = [0]
    for ref in later:
        offset.append(offset[-1] + spots_of(ref.shape[0]))
    densities(later, rows, parts, modes, hat)

    def steps(place, half):
        part = pl.ds(half * SUB, SUB)

        def start(x, y):
            which, at = place_of(x, y)
            if which < 2:
                return beside[place, which * len(CORE) + at, part, :]
            return hat[place, offset[which - 2] + at, part, :]

        old = start
        for step in range(DEGREE):
            new = (work_a, work_b, work_a, None)[step]
            ready = EARLY[step] if step < DEGREE - 1 else {}

            def load(x, y, new=new, step=step, ready=ready):
                if (x, y) in ready:
                    return stages[step][place, ready[x, y], part, :]
                return new[x, y]

            def store(x, y, value, new=new):
                if new is None:
                    last[place, CORE.index((x, y)), part, :] = value
                else:
                    new[x, y] = value

            cells = {(x, y) for x in range(SIZE) for y in within(HALO - 1 - step)[x]}
            one_step(cells - set(ready), old, tails.at[step], start, store)
            old = load

    for place in range(count):
        for half in range(ROWS // SUB):
            steps(place, half)
    copies = []
    for first in range(0, EDGE, 2):
        spots = range(first * EDGE, (first + 2) * EDGE)
        for place in range(count):
            for at, spot in enumerate(spots):
                keep(back, place * len(spots) + at, last[place, spot])
        result = turned(back, 0, count * len(spots), modes)
        for at, spot in enumerate(spots):
            total = None
            for place in range(count):
                other = jnp.broadcast_to(own_rows[place, pl.ds(spot, 1), :], (ROWS, LANES))
                value = result[place * len(spots) + at] * other
                total = value if total is None else total + value
            acc[spot // EDGE, pl.ds(spot % EDGE * pitch, ROWS), :] = total
        for x in range(first, first + 2):
            for group in range(ROWS):
                tile = acc[x, pl.ds(group, EDGE, stride=pitch), :]
                held[x, :, pl.ds(group * LANES, LANES)] = tile
        rows_x = pl.ds(first, 2)
        copies.append(
            pltpu.make_async_copy(held.at[rows_x], out.at[rows_x], sems.at[first // 2])
        )
        copies[-1].start()
    for copy in copies:
        copy.wait()


def fields(halo, modes, count):
    own, across, *later = halo
    beside, own_rows, *stages = modes_of(own, across, modes, count)
    plane = pltpu.VMEM((SIZE, SIZE, SUB, LANES), jnp.float32)
    cells = sum(spots_of(array.shape[0]) for array in later)
    rows = ROWS * sum(array.shape[0] - spots_of(array.shape[0]) for array in later)
    shape = (EDGE, EDGE, ROWS * LANES)
    return pl.pallas_call(
        fields_kernel,
        out_shape=jax.ShapeDtypeStruct(shape, jnp.float32),
        in_specs=[VMEM] * (7 + len(stages)),
        out_specs=pl.BlockSpec(memory_space=pl.ANY),
        scratch_shapes=[
            pltpu.VMEM((count, rows, LANES), jnp.float32),
            pltpu.VMEM((count, cells, ROWS, 2 * LANES), jnp.bfloat16),
            pltpu.VMEM((count * 2 * EDGE, ROWS, 2 * LANES), jnp.bfloat16),
            pltpu.VMEM((count, cells, ROWS, LANES), jnp.float32),
            plane,
            plane,
            pltpu.VMEM((count, len(CORE), ROWS, LANES), jnp.float32),
            pltpu.VMEM((EDGE, EDGE * (ROWS + 1), LANES), jnp.float32),
            pltpu.VMEM(shape, jnp.float32),
            pltpu.VMEM((DEGREE, SUB, LANES), jnp.float32),
            pltpu.SemaphoreType.DMA((EDGE // 2,)),
        ],
        compiler_params=pltpu.CompilerParams(vmem_limit_bytes=24 * 2**20),
        name="fields",
    )(beside, own_rows, *stages, *later, modes)


def body(orbitals, src_owner, src_slot):
    packed, modes = messages(orbitals, src_owner, src_slot)
    return fields((packed[0], *exchange(*packed)), modes, src_slot.size)


def solution(mesh):
    in_specs = (P("sx", "sy", "orb"), P(), P())
    out_specs = P("sx", "sy", "orb")
    return jax.shard_map(body, mesh=mesh, in_specs=in_specs, out_specs=out_specs, check_vma=False)
```

```python
import functools
import math

import jax
import jax.numpy as jnp
from jax import lax
from jax.experimental import pallas as pl
from jax.experimental.pallas import tpu as pltpu
from jax.sharding import PartitionSpec as P

NZ = 32
LANES = 128
SUB = 8
ROWS = 16
DEGREE = 4
HALO = DEGREE
EDGE = 8

CHEB = (
    1.021021021021021,
    -1.7357357357357357,
    1.4753753753753753,
    -1.254069069069069,
    1.0659587087087088,
)


def power_coeffs():
    c0, c1, c2, c3, c4 = CHEB
    return (
        c0 - c2 + c4,
        -(c1 - 3.0 * c3) / 6.0,
        (2.0 * c2 - 8.0 * c4) / 36.0,
        -4.0 * c3 / 216.0,
        8.0 * c4 / 1296.0,
    )


CORNER_LOW = tuple(
    (x, y)
    for x in range(EDGE)
    for y in range(EDGE - HALO, EDGE)
    if min(x + 1, EDGE - x) + EDGE - y <= DEGREE
)
CORNER_HIGH = tuple((x, EDGE - 1 - y) for x, y in CORNER_LOW)
SPLIT = len(CORNER_LOW) // 2


def ring(axis, step):
    count = lax.axis_size(axis)
    return [(i, (i + step) % count) for i in range(count)]


def diagonal(step_x, step_y):
    count_x, count_y = lax.axis_size("sx"), lax.axis_size("sy")
    return [
        (i * count_y + j, (i + step_x) % count_x * count_y + (j + step_y) % count_y)
        for i in range(count_x)
        for j in range(count_y)
    ]


VMEM = pl.BlockSpec(memory_space=pltpu.VMEM)
SMALL = pltpu.CompilerParams(vmem_limit_bytes=8 * 2**20)


def spread_out(values):
    return lax.broadcast_in_dim(
        values, values.shape + (ROWS, LANES), tuple(range(values.ndim))
    )


def by_seat(entries):
    rounds, places, rows, lanes = entries.shape
    seat = lax.broadcasted_iota(jnp.int32, (rows, lanes), 1) // NZ
    value = entries[0, 0]
    for index in range(1, rounds * places):
        value = jnp.where(seat == index, entries[index // places, index % places], value)
    return value


def prepare_kernel(entries, orbitals, out, cells, scratch):
    per_tile = LANES // NZ
    slot = by_seat(entries[0])[:EDGE]
    lane = lax.broadcasted_iota(jnp.int32, (EDGE, LANES), 1)
    group, turn = slot // per_tile, (lane // NZ - slot % per_tile + per_tile) % per_tile
    asked = [pltpu.roll(group, LANES - step * NZ, 1) if step else group for step in range(per_tile)]
    found = [[jnp.zeros((EDGE, LANES), jnp.float32)] * EDGE for _ in range(per_tile)]
    for number in range(ROWS):
        lanes = pl.ds(number * LANES, LANES)
        tiles = [orbitals[row, :, lanes].astype(jnp.float32) for row in range(EDGE)]
        for step in range(per_tile):
            here = asked[step] == number
            found[step] = [jnp.where(here, tile, old) for tile, old in zip(tiles, found[step])]
    rows = []
    for row in range(EDGE):
        packed = found[0][row]
        for step in range(1, per_tile):
            packed = jnp.where(turn == step, pltpu.roll(found[step][row], step * NZ, 1), packed)
        rows.append(packed)
    for tile in range(EDGE // 2):
        out[tile] = jnp.concatenate(rows[2 * tile : 2 * tile + 2], axis=0).astype(jnp.bfloat16)
    for row in range(EDGE):
        for group in range(ROWS):
            tile = orbitals[row, :, pl.ds(group * LANES, LANES)].astype(jnp.float32)
            scratch[row, pl.ds(group, EDGE, stride=ROWS + 1), :] = tile
    for row in range(EDGE):
        for y in range(EDGE):
            tile = scratch[row, pl.ds(y * (ROWS + 1), ROWS), :]
            cells[row * EDGE + y] = tile.astype(jnp.bfloat16)


def prepare(entries, orbitals):
    lengths = (EDGE * EDGE // ROWS, EDGE * EDGE)
    return pl.pallas_call(
        prepare_kernel,
        out_shape=[jax.ShapeDtypeStruct((length, ROWS, LANES), jnp.bfloat16) for length in lengths],
        in_specs=[VMEM] * 2,
        out_specs=[VMEM] * 2,
        scratch_shapes=[pltpu.VMEM((EDGE, EDGE * (ROWS + 1), LANES), jnp.float32)],
        compiler_params=SMALL,
        name="prepare",
    )(entries, orbitals)


def partners():
    count = lax.axis_size("orb")
    me = lax.axis_index("orb")
    if count & (count - 1):
        steps = range(1, count)
        return [(ring("orb", step), lax.rem(me + count - step, count)) for step in steps]
    steps = sorted(range(1, count), key=lambda step: step & -step, reverse=True)
    return [([(i, i ^ step) for i in range(count)], me ^ step) for step in steps]


def chosen(entries, mine, others):
    owner = by_seat(entries[1])
    holders = [holder for _, holder in partners()]
    picked = []
    for tile in range(mine.shape[0]):
        value = mine[tile].astype(jnp.float32)
        for holder, other in zip(holders, others):
            value = jnp.where(owner == holder, other[tile].astype(jnp.float32), value)
        picked.append(value)
    return picked


def messages_kernel(before, entries, cells, mine, *refs):
    others, (block, last, first, corner_low, corner_high) = refs[:-5], refs[-5:]
    picked = chosen(entries, mine, others)

    def pack(ref, spots):
        for at, (x, y) in enumerate(spots):
            ref[at] = cells[x * EDGE + y]
        used = len(spots)
        runs = []
        for x, y in spots:
            if runs and runs[-1][0] == x and runs[-1][2] == y:
                runs[-1][2] = y + 1
            else:
                runs.append([x, y, y + 1])
        parts = [
            picked[x * EDGE // ROWS][x * EDGE % ROWS + low : x * EDGE % ROWS + high]
            for x, low, high in runs
        ]
        if used % ROWS:
            parts.append(jnp.zeros((ROWS - used % ROWS, LANES), jnp.float32))
        rows = jnp.concatenate(parts, axis=0).astype(jnp.bfloat16)
        for tile in range(rows.shape[0] // ROWS):
            ref[used + tile] = rows[tile * ROWS : (tile + 1) * ROWS]

    pack(block, [(x, y) for x in range(EDGE) for y in range(EDGE)])
    pack(last, [(x, y) for x in range(EDGE) for y in range(EDGE - HALO, EDGE)])
    pack(first, [(x, y) for x in range(EDGE) for y in range(HALO)])
    pack(corner_low, CORNER_LOW)
    pack(corner_high, CORNER_HIGH)


def tiles(spots):
    return spots + -(-spots // ROWS)


def spots_of(length):
    return length * ROWS // (ROWS + 1)


def messages(orbitals, src_owner, src_slot):
    entries = spread_out(jnp.stack([src_slot, src_owner]))
    mine, cells = prepare(entries, orbitals)
    others = [lax.ppermute(mine, "orb", pairs) for pairs, _ in partners()]
    lengths = [EDGE * EDGE] + [EDGE * HALO] * 2 + [len(CORNER_LOW)] * 2
    modes = sines(mine)
    packed = pl.pallas_call(
        messages_kernel,
        out_shape=[
            jax.ShapeDtypeStruct((tiles(length), ROWS, LANES), jnp.bfloat16) for length in lengths
        ],
        in_specs=[pl.BlockSpec(memory_space=pl.ANY)] + [VMEM] * (3 + len(others)),
        out_specs=[VMEM] * 5,
        compiler_params=SMALL,
        name="messages",
    )(modes, entries, cells, mine, *others)
    return packed, modes


def exchange(block, last, first, corner_low, corner_high):
    both = ("sx", "sy")
    if lax.axis_size("sx") == 2:
        low = lax.ppermute(corner_low, both, diagonal(1, 1))
        high = lax.ppermute(corner_high, both, diagonal(1, -1))
        across = lax.ppermute(block, "sx", ring("sx", 1))
    else:
        def two_ways(cells, half, axes, down, up, merge):
            end = 2 * half
            back = lax.ppermute(jnp.concatenate([cells[:half], cells[end:]]), axes, down)
            ahead = lax.ppermute(jnp.concatenate([cells[half:end], cells[end:]]), axes, up)
            return jnp.concatenate([back[:half], ahead[:half], merge(back[half:], ahead[half:])])

        def halves(back, ahead):
            return jnp.concatenate([back[: back.shape[0] // 2], ahead[ahead.shape[0] // 2 :]])

        def rows(back, ahead):
            return jnp.concatenate([back[:, :SPLIT], ahead[:, SPLIT:]], axis=1)

        low = two_ways(corner_low, SPLIT, both, diagonal(-1, 1), diagonal(1, 1), rows)
        high = two_ways(corner_high, SPLIT, both, diagonal(-1, -1), diagonal(1, -1), rows)
        across = two_ways(block, EDGE * HALO, "sx", ring("sx", -1), ring("sx", 1), halves)
    below = lax.ppermute(last, "sy", ring("sy", 1))
    above = lax.ppermute(first, "sy", ring("sy", -1))
    return across, below, above, low, high


def place_of(x, y):
    row, core_x = (x - HALO) % EDGE, HALO <= x < HALO + EDGE
    if HALO <= y < HALO + EDGE:
        return (0 if core_x else 1), row * EDGE + y - HALO
    if y < HALO:
        return (2, row * HALO + y) if core_x else (4, CORNER_LOW.index((row, y + EDGE - HALO)))
    y = y - HALO - EDGE
    return (3, row * HALO + y) if core_x else (5, CORNER_HIGH.index((row, y)))


def reach(x, y):
    out_x = max(HALO - x, x - (HALO + EDGE - 1), 0)
    out_y = max(HALO - y, y - (HALO + EDGE - 1), 0)
    return out_x + out_y


def sines_kernel(after, out):
    shape = (LANES, LANES)
    row, col = (lax.broadcasted_iota(jnp.int32, shape, axis) for axis in range(2))
    product = ((row % NZ + 1) * (col % NZ + 1)).astype(jnp.float32)
    period = 2.0 * (NZ + 1)
    turn = product - period * jnp.floor((product + 0.5) / period)
    value = math.sqrt(2.0 / (NZ + 1)) * jnp.sin(turn * (math.pi / (NZ + 1)))
    value = jnp.where(row // NZ == col // NZ, value, 0.0)
    high = value.astype(jnp.bfloat16)
    low = (value - high.astype(jnp.float32)).astype(jnp.bfloat16)
    for first in (0, LANES):
        out[pl.ds(first, LANES), pl.ds(0, LANES)] = high
        out[pl.ds(first, LANES), pl.ds(LANES, LANES)] = low


def sines(after):
    return pl.pallas_call(
        sines_kernel,
        out_shape=jax.ShapeDtypeStruct((2 * LANES, 2 * LANES), jnp.bfloat16),
        in_specs=[pl.BlockSpec(memory_space=pl.ANY)],
        out_specs=VMEM,
        compiler_params=SMALL,
        cost_estimate=pl.CostEstimate(flops=0, bytes_accessed=2 * 2**20, transcendentals=0),
        name="sines",
    )(after)


def z_tails():
    lane = lax.broadcasted_iota(jnp.int32, (SUB, LANES), 1) % NZ
    value = 2.0 * jnp.cos((lane + 1).astype(jnp.float32) * (math.pi / (NZ + 1)))
    p0, p1, p2, p3, p4 = power_coeffs()
    a3, a2, a1, a0 = p3 / p4, p2 / p4, p1 / p4, p0 / p4
    return (
        4.0 * value + a3,
        (6.0 * value + 3.0 * a3) * value + a2,
        ((4.0 * value + 3.0 * a3) * value + 2.0 * a2) * value + a1,
        (((value + a3) * value + a2) * value + a1) * value + a0,
    )


SIZE = 2 * HALO + EDGE


def within(radius):
    return [[y for y in range(SIZE) if reach(x, y) <= radius] for x in range(SIZE)]


CORE = [(x, y) for x in range(HALO, HALO + EDGE) for y in range(HALO, HALO + EDGE)]


def source_rows(ref, out, first):
    shape = (LANES, LANES)
    lane = lax.broadcasted_iota(jnp.int32, shape, 1) % NZ
    line = lax.broadcasted_iota(jnp.int32, shape, 0)
    packed = ref[spots_of(ref.shape[0]) :].reshape(-1, LANES)
    for place in range(out.shape[0]):
        repeat = (line == lane + place * NZ).astype(jnp.bfloat16)
        out[place, pl.ds(first, packed.shape[0]), :] = jnp.dot(
            packed, repeat, preferred_element_type=jnp.float32
        )
    return first + packed.shape[0]


def keep(parts, at, value):
    high = value.astype(jnp.bfloat16)
    low = (value - high.astype(jnp.float32)).astype(jnp.bfloat16)
    parts[at, :, :LANES] = high
    parts[at, :, LANES:] = low


def turned(parts, first, end, modes):
    cells = end - first
    rows = parts[first:end].reshape(cells * ROWS, 2 * LANES)
    both = jnp.dot(rows, modes[...], preferred_element_type=jnp.float32)
    return (both[:, :LANES] + both[:, LANES:]).reshape(cells, ROWS, LANES)


def densities(refs, rows, parts, modes, hat):
    count = hat.shape[0]
    firsts = all_rows(refs, rows)
    cells = [
        (ref, at, first + at)
        for ref, first in zip(refs, firsts)
        for at in range(spots_of(ref.shape[0]))
    ]
    pieces = -(-len(cells) // 48)
    for piece in range(pieces):
        start, end = (len(cells) * at // pieces for at in (piece, piece + 1))
        for number in range(start, end):
            ref, at, row = cells[number]
            value = ref[at].astype(jnp.float32)
            for place in range(count):
                other = jnp.broadcast_to(rows[place, pl.ds(row, 1), :], (ROWS, LANES))
                keep(parts.at[place], number, value * other)
        for place in range(count):
            hat[place, start:end] = turned(parts.at[place], start, end, modes)


def all_rows(refs, rows):
    firsts = [0]
    for ref in refs:
        firsts.append(source_rows(ref, rows, firsts[-1]))
    return firsts


def early(step):
    cells = [
        (x, y)
        for x in range(1 + step, SIZE - 1 - step)
        for y in range(HALO + 1 + step, HALO + EDGE - 1 - step)
    ]
    return {cell: at for at, cell in enumerate(cells)}


EARLY = [early(step) for step in range(DEGREE - 1)]


def one_step(targets, old, tail, density, put):
    pairs = targets | {(x - 1, y - 1) for x, y in targets}
    wanted = {(x + 1, y) for x, y in pairs} | {(x, y + 1) for x, y in pairs}
    loaded, summed = {}, {}
    rows = sorted({x for x, _ in pairs})
    for x in rows:
        for cell in sorted(cell for cell in wanted if cell[0] in (x, x + 1)):
            if cell not in loaded:
                loaded[cell] = old(*cell)
        for y in range(SIZE):
            if (x, y) in pairs:
                summed[x, y] = loaded[x + 1, y] + loaded[x, y + 1]
            if (x, y) in targets:
                here = loaded.get((x, y)) if old is density else None
                here = density(x, y) if here is None else here
                put(x, y, summed[x, y] + summed[x - 1, y - 1] + tail[...] * here)


def modes_kernel(own, across, modes, hat, own_rows, *refs):
    stages, (rows, parts, tails) = refs[: DEGREE - 1], refs[DEGREE - 1 :]
    for step, tail in enumerate(z_tails()):
        tails[step] = tail
    densities((own, across), rows, parts, modes, hat)
    own_rows[...] = rows[:, : own_rows.shape[1], :] * (-power_coeffs()[-1])
    for place in range(hat.shape[0]):
        for half in range(ROWS // SUB):
            part = pl.ds(half * SUB, SUB)

            def start(x, y, place=place, part=part):
                which, at = place_of(x, y)
                return hat[place, which * len(CORE) + at, part, :]

            old = start
            for step, stage in enumerate(stages):

                def load(x, y, place=place, part=part, stage=stage, step=step):
                    return stage[place, EARLY[step][x, y], part, :]

                def store(x, y, value, place=place, part=part, stage=stage, step=step):
                    stage[place, EARLY[step][x, y], part, :] = value

                one_step(set(EARLY[step]), old, tails.at[step], start, store)
                old = load


def modes_of(own, across, modes, count):
    cells = 2 * len(CORE)
    lengths = [cells] + [len(stage) for stage in EARLY]
    shapes = [(count, length, ROWS, LANES) for length in lengths]
    shapes.insert(1, (count, len(CORE), LANES))
    return pl.pallas_call(
        modes_kernel,
        out_shape=[jax.ShapeDtypeStruct(shape, jnp.float32) for shape in shapes],
        in_specs=[VMEM] * 3,
        out_specs=[VMEM] * len(shapes),
        scratch_shapes=[
            pltpu.VMEM((count, cells, LANES), jnp.float32),
            pltpu.VMEM((count, cells, ROWS, 2 * LANES), jnp.bfloat16),
            pltpu.VMEM((DEGREE, SUB, LANES), jnp.float32),
        ],
        compiler_params=pltpu.CompilerParams(vmem_limit_bytes=20 * 2**20),
        cost_estimate=pl.CostEstimate(flops=0, bytes_accessed=6 * 2**20, transcendentals=0),
        name="modes",
    )(own, across, modes)


def fields_kernel(beside, own_rows, *refs):
    stages, (below, above, low, high, modes, out) = refs[: DEGREE - 1], refs[DEGREE - 1 :][:6]
    rows, parts, back, hat, work_a, work_b, last, acc, held, tails, sems = refs[DEGREE + 5 :]
    count = beside.shape[0]
    pitch = ROWS + 1
    for step, tail in enumerate(z_tails()):
        tails[step] = tail
    later = (below, above, low, high)
    offset = [0]
    for ref in later:
        offset.append(offset[-1] + spots_of(ref.shape[0]))
    densities(later, rows, parts, modes, hat)

    def steps(place, half):
        part = pl.ds(half * SUB, SUB)

        def start(x, y):
            which, at = place_of(x, y)
            if which < 2:
                return beside[place, which * len(CORE) + at, part, :]
            return hat[place, offset[which - 2] + at, part, :]

        old = start
        for step in range(DEGREE):
            new = (work_a, work_b, work_a, None)[step]
            ready = EARLY[step] if step < DEGREE - 1 else {}

            def load(x, y, new=new, step=step, ready=ready):
                if (x, y) in ready:
                    return stages[step][place, ready[x, y], part, :]
                return new[x, y]

            def store(x, y, value, new=new):
                if new is None:
                    last[place, CORE.index((x, y)), part, :] = value
                else:
                    new[x, y] = value

            cells = {(x, y) for x in range(SIZE) for y in within(HALO - 1 - step)[x]}
            one_step(cells - set(ready), old, tails.at[step], start, store)
            old = load

    for place in range(count):
        for half in range(ROWS // SUB):
            steps(place, half)
    copies = []
    for first in range(0, EDGE, 2):
        spots = range(first * EDGE, (first + 2) * EDGE)
        for place in range(count):
            for at, spot in enumerate(spots):
                keep(back, place * len(spots) + at, last[place, spot])
        result = turned(back, 0, count * len(spots), modes)
        for at, spot in enumerate(spots):
            total = None
            for place in range(count):
                other = jnp.broadcast_to(own_rows[place, pl.ds(spot, 1), :], (ROWS, LANES))
                value = result[place * len(spots) + at] * other
                total = value if total is None else total + value
            acc[spot // EDGE, pl.ds(spot % EDGE * pitch, ROWS), :] = total
        for x in range(first, first + 2):
            for group in range(ROWS):
                tile = acc[x, pl.ds(group, EDGE, stride=pitch), :]
                held[x, :, pl.ds(group * LANES, LANES)] = tile
        rows_x = pl.ds(first, 2)
        copies.append(
            pltpu.make_async_copy(held.at[rows_x], out.at[rows_x], sems.at[first // 2])
        )
        copies[-1].start()
    for copy in copies:
        copy.wait()


def fields(halo, modes, count):
    own, across, *later = halo
    beside, own_rows, *stages = modes_of(own, across, modes, count)
    plane = pltpu.VMEM((SIZE, SIZE, SUB, LANES), jnp.float32)
    cells = sum(spots_of(array.shape[0]) for array in later)
    rows = ROWS * sum(array.shape[0] - spots_of(array.shape[0]) for array in later)
    shape = (EDGE, EDGE, ROWS * LANES)
    return pl.pallas_call(
        fields_kernel,
        out_shape=jax.ShapeDtypeStruct(shape, jnp.float32),
        in_specs=[VMEM] * (7 + len(stages)),
        out_specs=pl.BlockSpec(memory_space=pl.ANY),
        scratch_shapes=[
            pltpu.VMEM((count, rows, LANES), jnp.float32),
            pltpu.VMEM((count, cells, ROWS, 2 * LANES), jnp.bfloat16),
            pltpu.VMEM((count * 2 * EDGE, ROWS, 2 * LANES), jnp.bfloat16),
            pltpu.VMEM((count, cells, ROWS, LANES), jnp.float32),
            plane,
            plane,
            pltpu.VMEM((count, len(CORE), ROWS, LANES), jnp.float32),
            pltpu.VMEM((EDGE, EDGE * (ROWS + 1), LANES), jnp.float32),
            pltpu.VMEM(shape, jnp.float32),
            pltpu.VMEM((DEGREE, SUB, LANES), jnp.float32),
            pltpu.SemaphoreType.DMA((EDGE // 2,)),
        ],
        compiler_params=pltpu.CompilerParams(vmem_limit_bytes=24 * 2**20),
        name="fields",
    )(beside, own_rows, *stages, *later, modes)


def body(orbitals, src_owner, src_slot):
    packed, modes = messages(orbitals, src_owner, src_slot)
    return fields((packed[0], *exchange(*packed)), modes, src_slot.size)


def solution(mesh):
    in_specs = (P("sx", "sy", "orb"), P(), P())
    out_specs = P("sx", "sy", "orb")
    return jax.shard_map(body, mesh=mesh, in_specs=in_specs, out_specs=out_specs, check_vma=False)
```

```python
import functools
import math

import jax
import jax.numpy as jnp
from jax import lax
from jax.experimental import pallas as pl
from jax.experimental.pallas import tpu as pltpu
from jax.sharding import PartitionSpec as P

NZ = 32
LANES = 128
SUB = 8
ROWS = 16
DEGREE = 4
HALO = DEGREE
EDGE = 8

CHEB = (
    1.021021021021021,
    -1.7357357357357357,
    1.4753753753753753,
    -1.254069069069069,
    1.0659587087087088,
)


def power_coeffs():
    c0, c1, c2, c3, c4 = CHEB
    return (
        c0 - c2 + c4,
        -(c1 - 3.0 * c3) / 6.0,
        (2.0 * c2 - 8.0 * c4) / 36.0,
        -4.0 * c3 / 216.0,
        8.0 * c4 / 1296.0,
    )


CORNER_LOW = tuple(
    (x, y)
    for x in range(EDGE)
    for y in range(EDGE - HALO, EDGE)
    if min(x + 1, EDGE - x) + EDGE - y <= DEGREE
)
CORNER_HIGH = tuple((x, EDGE - 1 - y) for x, y in CORNER_LOW)
SPLIT = len(CORNER_LOW) // 2


def ring(axis, step):
    count = lax.axis_size(axis)
    return [(i, (i + step) % count) for i in range(count)]


def diagonal(step_x, step_y):
    count_x, count_y = lax.axis_size("sx"), lax.axis_size("sy")
    return [
        (i * count_y + j, (i + step_x) % count_x * count_y + (j + step_y) % count_y)
        for i in range(count_x)
        for j in range(count_y)
    ]


VMEM = pl.BlockSpec(memory_space=pltpu.VMEM)
SMALL = pltpu.CompilerParams(vmem_limit_bytes=8 * 2**20)


def spread_out(values):
    return lax.broadcast_in_dim(
        values, values.shape + (ROWS, LANES), tuple(range(values.ndim))
    )


def by_seat(entries):
    rounds, places, rows, lanes = entries.shape
    seat = lax.broadcasted_iota(jnp.int32, (rows, lanes), 1) // NZ
    value = entries[0, 0]
    for index in range(1, rounds * places):
        value = jnp.where(seat == index, entries[index // places, index % places], value)
    return value


def prepare_kernel(entries, orbitals, out, cells, scratch):
    per_tile = LANES // NZ
    slot = by_seat(entries[0])[:EDGE]
    lane = lax.broadcasted_iota(jnp.int32, (EDGE, LANES), 1)
    group, turn = slot // per_tile, (lane // NZ - slot % per_tile + per_tile) % per_tile
    asked = [pltpu.roll(group, LANES - step * NZ, 1) if step else group for step in range(per_tile)]
    found = [[jnp.zeros((EDGE, LANES), jnp.float32)] * EDGE for _ in range(per_tile)]
    for number in range(ROWS):
        lanes = pl.ds(number * LANES, LANES)
        tiles = [orbitals[row, :, lanes].astype(jnp.float32) for row in range(EDGE)]
        for step in range(per_tile):
            here = asked[step] == number
            found[step] = [jnp.where(here, tile, old) for tile, old in zip(tiles, found[step])]
    rows = []
    for row in range(EDGE):
        packed = found[0][row]
        for step in range(1, per_tile):
            packed = jnp.where(turn == step, pltpu.roll(found[step][row], step * NZ, 1), packed)
        rows.append(packed)
    for tile in range(EDGE // 2):
        out[tile] = jnp.concatenate(rows[2 * tile : 2 * tile + 2], axis=0).astype(jnp.bfloat16)
    for row in range(EDGE):
        for group in range(ROWS):
            tile = orbitals[row, :, pl.ds(group * LANES, LANES)].astype(jnp.float32)
            scratch[row, pl.ds(group, EDGE, stride=ROWS + 1), :] = tile
    for row in range(EDGE):
        for y in range(EDGE):
            tile = scratch[row, pl.ds(y * (ROWS + 1), ROWS), :]
            cells[row * EDGE + y] = tile.astype(jnp.bfloat16)


def prepare(entries, orbitals):
    lengths = (EDGE * EDGE // ROWS, EDGE * EDGE)
    return pl.pallas_call(
        prepare_kernel,
        out_shape=[jax.ShapeDtypeStruct((length, ROWS, LANES), jnp.bfloat16) for length in lengths],
        in_specs=[VMEM] * 2,
        out_specs=[VMEM] * 2,
        scratch_shapes=[pltpu.VMEM((EDGE, EDGE * (ROWS + 1), LANES), jnp.float32)],
        compiler_params=SMALL,
        name="prepare",
    )(entries, orbitals)


def chosen(entries, mine, others, bit):
    owner, me = by_seat(entries[1]), lax.axis_index("orb")
    count = lax.axis_size("orb")
    picked = []
    for tile in range(mine.shape[0]):
        value = mine[tile].astype(jnp.float32)
        for step, other in enumerate(others, 1):
            if bit is None:
                here = owner == lax.rem(me + count - step, count)
            else:
                here = (owner >> bit & 1) != (me >> bit & 1)
            value = jnp.where(here, other[tile].astype(jnp.float32), value)
        picked.append(value)
    return picked


def nearer_kernel(bit, entries, mine, other, out):
    for tile, value in enumerate(chosen(entries, mine, [other], bit)):
        out[tile] = value.astype(jnp.bfloat16)


def gathered(entries, mine):
    count = lax.axis_size("orb")
    if count & (count - 1):
        others = [lax.ppermute(mine, "orb", ring("orb", step)) for step in range(1, count)]
        return mine, others, None
    bits = count.bit_length() - 1
    for bit in range(bits):
        other = lax.ppermute(mine, "orb", [(i, i ^ 1 << bit) for i in range(count)])
        if bit == bits - 1:
            return mine, [other], bit
        mine = pl.pallas_call(
            functools.partial(nearer_kernel, bit),
            out_shape=jax.ShapeDtypeStruct(mine.shape, mine.dtype),
            in_specs=[VMEM] * 3,
            out_specs=VMEM,
            compiler_params=SMALL,
            name="nearer",
        )(entries, mine, other)
    return mine, [], None


def messages_kernel(bit, before, entries, cells, mine, *refs):
    others, (block, last, first, corner_low, corner_high) = refs[:-5], refs[-5:]
    picked = chosen(entries, mine, others, bit)

    def pack(ref, spots):
        for at, (x, y) in enumerate(spots):
            ref[at] = cells[x * EDGE + y]
        used = len(spots)
        runs = []
        for x, y in spots:
            if runs and runs[-1][0] == x and runs[-1][2] == y:
                runs[-1][2] = y + 1
            else:
                runs.append([x, y, y + 1])
        parts = [
            picked[x * EDGE // ROWS][x * EDGE % ROWS + low : x * EDGE % ROWS + high]
            for x, low, high in runs
        ]
        if used % ROWS:
            parts.append(jnp.zeros((ROWS - used % ROWS, LANES), jnp.float32))
        rows = jnp.concatenate(parts, axis=0).astype(jnp.bfloat16)
        for tile in range(rows.shape[0] // ROWS):
            ref[used + tile] = rows[tile * ROWS : (tile + 1) * ROWS]

    pack(block, [(x, y) for x in range(EDGE) for y in range(EDGE)])
    pack(last, [(x, y) for x in range(EDGE) for y in range(EDGE - HALO, EDGE)])
    pack(first, [(x, y) for x in range(EDGE) for y in range(HALO)])
    pack(corner_low, CORNER_LOW)
    pack(corner_high, CORNER_HIGH)


def tiles(spots):
    return spots + -(-spots // ROWS)


def spots_of(length):
    return length * ROWS // (ROWS + 1)


def messages(orbitals, src_owner, src_slot):
    entries = spread_out(jnp.stack([src_slot, src_owner]))
    mine, cells = prepare(entries, orbitals)
    mine, others, bit = gathered(entries, mine)
    lengths = [EDGE * EDGE] + [EDGE * HALO] * 2 + [len(CORNER_LOW)] * 2
    modes, tails = sines(mine)
    packed = pl.pallas_call(
        functools.partial(messages_kernel, bit),
        out_shape=[
            jax.ShapeDtypeStruct((tiles(length), ROWS, LANES), jnp.bfloat16) for length in lengths
        ],
        in_specs=[pl.BlockSpec(memory_space=pl.ANY)] + [VMEM] * (3 + len(others)),
        out_specs=[VMEM] * 5,
        compiler_params=SMALL,
        name="messages",
    )(modes, entries, cells, mine, *others)
    return packed, modes, tails


def exchange(block, last, first, corner_low, corner_high):
    both = ("sx", "sy")
    if lax.axis_size("sx") == 2:
        low = lax.ppermute(corner_low, both, diagonal(1, 1))
        high = lax.ppermute(corner_high, both, diagonal(1, -1))
        across = lax.ppermute(block, "sx", ring("sx", 1))
    else:
        def two_ways(cells, half, axes, down, up, merge):
            end = 2 * half
            back = lax.ppermute(jnp.concatenate([cells[:half], cells[end:]]), axes, down)
            ahead = lax.ppermute(jnp.concatenate([cells[half:end], cells[end:]]), axes, up)
            return jnp.concatenate([back[:half], ahead[:half], merge(back[half:], ahead[half:])])

        def halves(back, ahead):
            return jnp.concatenate([back[: back.shape[0] // 2], ahead[ahead.shape[0] // 2 :]])

        def rows(back, ahead):
            return jnp.concatenate([back[:, :SPLIT], ahead[:, SPLIT:]], axis=1)

        low = two_ways(corner_low, SPLIT, both, diagonal(-1, 1), diagonal(1, 1), rows)
        high = two_ways(corner_high, SPLIT, both, diagonal(-1, -1), diagonal(1, -1), rows)
        across = two_ways(block, EDGE * HALO, "sx", ring("sx", -1), ring("sx", 1), halves)
    below = lax.ppermute(last, "sy", ring("sy", 1))
    above = lax.ppermute(first, "sy", ring("sy", -1))
    return across, below, above, low, high


def place_of(x, y):
    row, core_x = (x - HALO) % EDGE, HALO <= x < HALO + EDGE
    if HALO <= y < HALO + EDGE:
        return (0 if core_x else 1), row * EDGE + y - HALO
    if y < HALO:
        return (2, row * HALO + y) if core_x else (4, CORNER_LOW.index((row, y + EDGE - HALO)))
    y = y - HALO - EDGE
    return (3, row * HALO + y) if core_x else (5, CORNER_HIGH.index((row, y)))


def reach(x, y):
    out_x = max(HALO - x, x - (HALO + EDGE - 1), 0)
    out_y = max(HALO - y, y - (HALO + EDGE - 1), 0)
    return out_x + out_y


def sines_kernel(after, out, tails):
    shape = (LANES, LANES)
    row, col = (lax.broadcasted_iota(jnp.int32, shape, axis) for axis in range(2))
    product = ((row % NZ + 1) * (col % NZ + 1)).astype(jnp.float32)
    period = 2.0 * (NZ + 1)
    turn = product - period * jnp.floor((product + 0.5) / period)
    value = math.sqrt(2.0 / (NZ + 1)) * jnp.sin(turn * (math.pi / (NZ + 1)))
    value = jnp.where(row // NZ == col // NZ, value, 0.0)
    high = value.astype(jnp.bfloat16)
    low = (value - high.astype(jnp.float32)).astype(jnp.bfloat16)
    for first in (0, LANES):
        out[pl.ds(first, LANES), pl.ds(0, LANES)] = high
        out[pl.ds(first, LANES), pl.ds(LANES, LANES)] = low
    for step, tail in enumerate(z_tails()):
        tails[step] = tail


def sines(after):
    return pl.pallas_call(
        sines_kernel,
        out_shape=[
            jax.ShapeDtypeStruct((2 * LANES, 2 * LANES), jnp.bfloat16),
            jax.ShapeDtypeStruct((DEGREE, SUB, LANES), jnp.float32),
        ],
        in_specs=[pl.BlockSpec(memory_space=pl.ANY)],
        out_specs=[VMEM] * 2,
        compiler_params=SMALL,
        cost_estimate=pl.CostEstimate(flops=0, bytes_accessed=2 * 2**20, transcendentals=0),
        name="sines",
    )(after)


def z_tails():
    lane = lax.broadcasted_iota(jnp.int32, (SUB, LANES), 1) % NZ
    value = 2.0 * jnp.cos((lane + 1).astype(jnp.float32) * (math.pi / (NZ + 1)))
    p0, p1, p2, p3, p4 = power_coeffs()
    a3, a2, a1, a0 = p3 / p4, p2 / p4, p1 / p4, p0 / p4
    return (
        4.0 * value + a3,
        (6.0 * value + 3.0 * a3) * value + a2,
        ((4.0 * value + 3.0 * a3) * value + 2.0 * a2) * value + a1,
        (((value + a3) * value + a2) * value + a1) * value + a0,
    )


SIZE = 2 * HALO + EDGE


def within(radius):
    return [[y for y in range(SIZE) if reach(x, y) <= radius] for x in range(SIZE)]


CORE = [(x, y) for x in range(HALO, HALO + EDGE) for y in range(HALO, HALO + EDGE)]


def all_rows(refs, rows):
    count = rows.shape[0]
    shape = (LANES, count * LANES)
    lane = lax.broadcasted_iota(jnp.int32, shape, 1)
    line = lax.broadcasted_iota(jnp.int32, shape, 0)
    repeat = (line == lane // LANES * NZ + lane % NZ).astype(jnp.bfloat16)
    packed = [ref[spots_of(ref.shape[0]) :].reshape(-1, LANES) for ref in refs]
    firsts = [sum(part.shape[0] for part in packed[:at]) for at in range(len(packed))]
    packed = jnp.concatenate(packed, axis=0)
    spread = jnp.dot(packed, repeat, preferred_element_type=jnp.float32)
    for place in range(count):
        rows[place, : packed.shape[0], :] = spread[:, place * LANES : (place + 1) * LANES]
    return firsts


def keep(parts, at, value):
    high = value.astype(jnp.bfloat16)
    low = (value - high.astype(jnp.float32)).astype(jnp.bfloat16)
    parts[at, :, :LANES] = high
    parts[at, :, LANES:] = low


def turned(parts, first, end, modes):
    cells = end - first
    rows = parts[first:end].reshape(cells * ROWS, 2 * LANES)
    both = jnp.dot(rows, modes[...], preferred_element_type=jnp.float32)
    return (both[:, :LANES] + both[:, LANES:]).reshape(cells, ROWS, LANES)


def densities(refs, rows, parts, modes, hat):
    count = hat.shape[0]
    firsts = all_rows(refs, rows)
    cells = [
        (ref, at, first + at)
        for ref, first in zip(refs, firsts)
        for at in range(spots_of(ref.shape[0]))
    ]
    pieces = -(-len(cells) // 48)
    for piece in range(pieces):
        start, end = (len(cells) * at // pieces for at in (piece, piece + 1))
        for number in range(start, end):
            ref, at, row = cells[number]
            value = ref[at].astype(jnp.float32)
            for place in range(count):
                other = jnp.broadcast_to(rows[place, pl.ds(row, 1), :], (ROWS, LANES))
                keep(parts.at[place], number, value * other)
        for place in range(count):
            hat[place, start:end] = turned(parts.at[place], start, end, modes)


def early(step):
    cells = [
        (x, y)
        for x in range(1 + step, SIZE - 1 - step)
        for y in range(HALO + 1 + step, HALO + EDGE - 1 - step)
    ]
    return {cell: at for at, cell in enumerate(cells)}


EARLY = [early(step) for step in range(DEGREE - 1)]


def one_step(targets, old, tail, density, put):
    pairs = targets | {(x - 1, y - 1) for x, y in targets}
    wanted = {(x + 1, y) for x, y in pairs} | {(x, y + 1) for x, y in pairs}
    loaded, summed = {}, {}
    rows = sorted({x for x, _ in pairs})
    for x in rows:
        for cell in sorted(cell for cell in wanted if cell[0] in (x, x + 1)):
            if cell not in loaded:
                loaded[cell] = old(*cell)
        for y in range(SIZE):
            if (x, y) in pairs:
                summed[x, y] = loaded[x + 1, y] + loaded[x, y + 1]
            if (x, y) in targets:
                here = loaded.get((x, y)) if old is density else None
                here = density(x, y) if here is None else here
                put(x, y, summed[x, y] + summed[x - 1, y - 1] + tail[...] * here)


def modes_kernel(own, across, modes, tails, hat, own_rows, *refs):
    stages, (rows, parts) = refs[: DEGREE - 1], refs[DEGREE - 1 :]
    densities((own, across), rows, parts, modes, hat)
    own_rows[...] = rows[:, : own_rows.shape[1], :] * (-power_coeffs()[-1])
    for place in range(hat.shape[0]):
        for half in range(ROWS // SUB):
            part = pl.ds(half * SUB, SUB)

            def start(x, y, place=place, part=part):
                which, at = place_of(x, y)
                return hat[place, which * len(CORE) + at, part, :]

            old = start
            for step, stage in enumerate(stages):

                def load(x, y, place=place, part=part, stage=stage, step=step):
                    return stage[place, EARLY[step][x, y], part, :]

                def store(x, y, value, place=place, part=part, stage=stage, step=step):
                    stage[place, EARLY[step][x, y], part, :] = value

                one_step(set(EARLY[step]), old, tails.at[step], start, store)
                old = load


def modes_of(own, across, modes, tails, count):
    cells = 2 * len(CORE)
    lengths = [cells] + [len(stage) for stage in EARLY]
    shapes = [(count, length, ROWS, LANES) for length in lengths]
    shapes.insert(1, (count, len(CORE), LANES))
    return pl.pallas_call(
        modes_kernel,
        out_shape=[jax.ShapeDtypeStruct(shape, jnp.float32) for shape in shapes],
        in_specs=[VMEM] * 4,
        out_specs=[VMEM] * len(shapes),
        scratch_shapes=[
            pltpu.VMEM((count, cells, LANES), jnp.float32),
            pltpu.VMEM((count, cells, ROWS, 2 * LANES), jnp.bfloat16),
        ],
        compiler_params=pltpu.CompilerParams(vmem_limit_bytes=20 * 2**20),
        cost_estimate=pl.CostEstimate(flops=0, bytes_accessed=6 * 2**20, transcendentals=0),
        name="modes",
    )(own, across, modes, tails)


def fields_kernel(beside, own_rows, *refs):
    stages, (below, above, low, high, modes, tails, out) = (
        refs[: DEGREE - 1],
        refs[DEGREE - 1 :][:7],
    )
    rows, parts, back, hat, work_a, work_b, last, acc, held, sems = refs[DEGREE + 6 :]
    count = beside.shape[0]
    pitch = ROWS + 1
    later = (below, above, low, high)
    offset = [0]
    for ref in later:
        offset.append(offset[-1] + spots_of(ref.shape[0]))
    densities(later, rows, parts, modes, hat)

    def steps(place, half):
        part = pl.ds(half * SUB, SUB)

        def start(x, y):
            which, at = place_of(x, y)
            if which < 2:
                return beside[place, which * len(CORE) + at, part, :]
            return hat[place, offset[which - 2] + at, part, :]

        old = start
        for step in range(DEGREE):
            new = (work_a, work_b, work_a, None)[step]
            ready = EARLY[step] if step < DEGREE - 1 else {}

            def load(x, y, new=new, step=step, ready=ready):
                if (x, y) in ready:
                    return stages[step][place, ready[x, y], part, :]
                return new[x, y]

            def store(x, y, value, new=new):
                if new is None:
                    last[place, CORE.index((x, y)), part, :] = value
                else:
                    new[x, y] = value

            cells = {(x, y) for x in range(SIZE) for y in within(HALO - 1 - step)[x]}
            one_step(cells - set(ready), old, tails.at[step], start, store)
            old = load

    for place in range(count):
        for half in range(ROWS // SUB):
            steps(place, half)
    copies = []
    for first in range(0, EDGE, 2):
        spots = range(first * EDGE, (first + 2) * EDGE)
        for place in range(count):
            for at, spot in enumerate(spots):
                keep(back, place * len(spots) + at, last[place, spot])
        result = turned(back, 0, count * len(spots), modes)
        for at, spot in enumerate(spots):
            total = None
            for place in range(count):
                other = jnp.broadcast_to(own_rows[place, pl.ds(spot, 1), :], (ROWS, LANES))
                value = result[place * len(spots) + at] * other
                total = value if total is None else total + value
            acc[spot // EDGE, pl.ds(spot % EDGE * pitch, ROWS), :] = total
        for x in range(first, first + 2):
            for group in range(ROWS):
                tile = acc[x, pl.ds(group, EDGE, stride=pitch), :]
                held[x, :, pl.ds(group * LANES, LANES)] = tile
        rows_x = pl.ds(first, 2)
        copies.append(
            pltpu.make_async_copy(held.at[rows_x], out.at[rows_x], sems.at[first // 2])
        )
        copies[-1].start()
    for copy in copies:
        copy.wait()


def fields(halo, modes, tails, count):
    own, across, *later = halo
    beside, own_rows, *stages = modes_of(own, across, modes, tails, count)
    plane = pltpu.VMEM((SIZE, SIZE, SUB, LANES), jnp.float32)
    cells = sum(spots_of(array.shape[0]) for array in later)
    rows = ROWS * sum(array.shape[0] - spots_of(array.shape[0]) for array in later)
    shape = (EDGE, EDGE, ROWS * LANES)
    return pl.pallas_call(
        fields_kernel,
        out_shape=jax.ShapeDtypeStruct(shape, jnp.float32),
        in_specs=[VMEM] * (8 + len(stages)),
        out_specs=pl.BlockSpec(memory_space=pl.ANY),
        scratch_shapes=[
            pltpu.VMEM((count, rows, LANES), jnp.float32),
            pltpu.VMEM((count, cells, ROWS, 2 * LANES), jnp.bfloat16),
            pltpu.VMEM((count * 2 * EDGE, ROWS, 2 * LANES), jnp.bfloat16),
            pltpu.VMEM((count, cells, ROWS, LANES), jnp.float32),
            plane,
            plane,
            pltpu.VMEM((count, len(CORE), ROWS, LANES), jnp.float32),
            pltpu.VMEM((EDGE, EDGE * (ROWS + 1), LANES), jnp.float32),
            pltpu.VMEM(shape, jnp.float32),
            pltpu.SemaphoreType.DMA((EDGE // 2,)),
        ],
        compiler_params=pltpu.CompilerParams(vmem_limit_bytes=24 * 2**20),
        name="fields",
    )(beside, own_rows, *stages, *later, modes, tails)


def body(orbitals, src_owner, src_slot):
    packed, modes, tails = messages(orbitals, src_owner, src_slot)
    return fields((packed[0], *exchange(*packed)), modes, tails, src_slot.size)


def solution(mesh):
    in_specs = (P("sx", "sy", "orb"), P(), P())
    out_specs = P("sx", "sy", "orb")
    return jax.shard_map(body, mesh=mesh, in_specs=in_specs, out_specs=out_specs, check_vma=False)
```

```python
import functools
import math

import jax
import jax.numpy as jnp
from jax import lax
from jax.experimental import pallas as pl
from jax.experimental.pallas import tpu as pltpu
from jax.sharding import PartitionSpec as P

NZ = 32
LANES = 128
SUB = 8
ROWS = 16
DEGREE = 4
HALO = DEGREE
EDGE = 8

CHEB = (
    1.021021021021021,
    -1.7357357357357357,
    1.4753753753753753,
    -1.254069069069069,
    1.0659587087087088,
)


def power_coeffs():
    c0, c1, c2, c3, c4 = CHEB
    return (
        c0 - c2 + c4,
        -(c1 - 3.0 * c3) / 6.0,
        (2.0 * c2 - 8.0 * c4) / 36.0,
        -4.0 * c3 / 216.0,
        8.0 * c4 / 1296.0,
    )


CORNER_LOW = tuple(
    (x, y)
    for x in range(EDGE)
    for y in range(EDGE - HALO, EDGE)
    if min(x + 1, EDGE - x) + EDGE - y <= DEGREE
)
CORNER_HIGH = tuple((x, EDGE - 1 - y) for x, y in CORNER_LOW)
SPLIT = len(CORNER_LOW) // 2


def ring(axis, step):
    count = lax.axis_size(axis)
    return [(i, (i + step) % count) for i in range(count)]


def diagonal(step_x, step_y):
    count_x, count_y = lax.axis_size("sx"), lax.axis_size("sy")
    return [
        (i * count_y + j, (i + step_x) % count_x * count_y + (j + step_y) % count_y)
        for i in range(count_x)
        for j in range(count_y)
    ]


VMEM = pl.BlockSpec(memory_space=pltpu.VMEM)
SMALL = pltpu.CompilerParams(vmem_limit_bytes=8 * 2**20)


def spread_out(values):
    return lax.broadcast_in_dim(
        values, values.shape + (ROWS, LANES), tuple(range(values.ndim))
    )


def by_seat(entries):
    rounds, places, rows, lanes = entries.shape
    seat = lax.broadcasted_iota(jnp.int32, (rows, lanes), 1) // NZ
    value = entries[0, 0]
    for index in range(1, rounds * places):
        value = jnp.where(seat == index, entries[index // places, index % places], value)
    return value


def prepare_kernel(entries, orbitals, out, cells, scratch):
    per_tile = LANES // NZ
    slot = by_seat(entries[0])[:EDGE]
    lane = lax.broadcasted_iota(jnp.int32, (EDGE, LANES), 1)
    group, turn = slot // per_tile, (lane // NZ - slot % per_tile + per_tile) % per_tile
    asked = [pltpu.roll(group, LANES - step * NZ, 1) if step else group for step in range(per_tile)]
    found = [[jnp.zeros((EDGE, LANES), jnp.float32)] * EDGE for _ in range(per_tile)]
    for number in range(ROWS):
        lanes = pl.ds(number * LANES, LANES)
        tiles = [orbitals[row, :, lanes].astype(jnp.float32) for row in range(EDGE)]
        for step in range(per_tile):
            here = asked[step] == number
            found[step] = [jnp.where(here, tile, old) for tile, old in zip(tiles, found[step])]
    rows = []
    for row in range(EDGE):
        packed = found[0][row]
        for step in range(1, per_tile):
            packed = jnp.where(turn == step, pltpu.roll(found[step][row], step * NZ, 1), packed)
        rows.append(packed)
    for tile in range(EDGE // 2):
        out[tile] = jnp.concatenate(rows[2 * tile : 2 * tile + 2], axis=0).astype(jnp.bfloat16)
    for row in range(EDGE):
        for group in range(ROWS):
            tile = orbitals[row, :, pl.ds(group * LANES, LANES)].astype(jnp.float32)
            scratch[row, pl.ds(group, EDGE, stride=ROWS + 1), :] = tile
    for row in range(EDGE):
        for y in range(EDGE):
            tile = scratch[row, pl.ds(y * (ROWS + 1), ROWS), :]
            cells[row * EDGE + y] = tile.astype(jnp.bfloat16)


def prepare(entries, orbitals):
    lengths = (EDGE * EDGE // ROWS, EDGE * EDGE)
    return pl.pallas_call(
        prepare_kernel,
        out_shape=[jax.ShapeDtypeStruct((length, ROWS, LANES), jnp.bfloat16) for length in lengths],
        in_specs=[VMEM] * 2,
        out_specs=[VMEM] * 2,
        scratch_shapes=[pltpu.VMEM((EDGE, EDGE * (ROWS + 1), LANES), jnp.float32)],
        compiler_params=SMALL,
        name="prepare",
    )(entries, orbitals)


def chosen(entries, mine, others, bit):
    owner, me = by_seat(entries[1]), lax.axis_index("orb")
    count = lax.axis_size("orb")
    picked = []
    for tile in range(mine.shape[0]):
        value = mine[tile].astype(jnp.float32)
        for step, other in enumerate(others, 1):
            if bit is None:
                here = owner == lax.rem(me + count - step, count)
            else:
                here = (owner >> bit & 1) != (me >> bit & 1)
            value = jnp.where(here, other[tile].astype(jnp.float32), value)
        picked.append(value)
    return picked


def nearer_kernel(bit, entries, mine, other, out):
    for tile, value in enumerate(chosen(entries, mine, [other], bit)):
        out[tile] = value.astype(jnp.bfloat16)


def gathered(entries, mine):
    count = lax.axis_size("orb")
    if count & (count - 1):
        others = [lax.ppermute(mine, "orb", ring("orb", step)) for step in range(1, count)]
        return mine, others, None
    bits = count.bit_length() - 1
    for bit in range(bits):
        other = lax.ppermute(mine, "orb", [(i, i ^ 1 << bit) for i in range(count)])
        if bit == bits - 1:
            return mine, [other], bit
        mine = pl.pallas_call(
            functools.partial(nearer_kernel, bit),
            out_shape=jax.ShapeDtypeStruct(mine.shape, mine.dtype),
            in_specs=[VMEM] * 3,
            out_specs=VMEM,
            compiler_params=SMALL,
            name="nearer",
        )(entries, mine, other)
    return mine, [], None


def messages_kernel(bit, before, entries, cells, mine, *refs):
    others, (block, last, first, corner_low, corner_high) = refs[:-5], refs[-5:]
    picked = chosen(entries, mine, others, bit)

    def pack(ref, spots):
        for at, (x, y) in enumerate(spots):
            ref[at] = cells[x * EDGE + y]
        used = len(spots)
        runs = []
        for x, y in spots:
            if runs and runs[-1][0] == x and runs[-1][2] == y:
                runs[-1][2] = y + 1
            else:
                runs.append([x, y, y + 1])
        parts = [
            picked[x * EDGE // ROWS][x * EDGE % ROWS + low : x * EDGE % ROWS + high]
            for x, low, high in runs
        ]
        if used % ROWS:
            parts.append(jnp.zeros((ROWS - used % ROWS, LANES), jnp.float32))
        rows = jnp.concatenate(parts, axis=0).astype(jnp.bfloat16)
        for tile in range(rows.shape[0] // ROWS):
            ref[used + tile] = rows[tile * ROWS : (tile + 1) * ROWS]

    for tile in range(block.shape[0]):
        rows = picked[tile] if tile < len(picked) else jnp.zeros((ROWS, LANES), jnp.float32)
        block[tile] = rows.astype(jnp.bfloat16)
    pack(last, [(x, y) for x in range(EDGE) for y in range(EDGE - HALO, EDGE)])
    pack(first, [(x, y) for x in range(EDGE) for y in range(HALO)])
    pack(corner_low, CORNER_LOW)
    pack(corner_high, CORNER_HIGH)


def tiles(spots):
    return spots + -(-spots // ROWS)


def spots_of(length):
    return length * ROWS // (ROWS + 1)


def messages(orbitals, src_owner, src_slot):
    entries = spread_out(jnp.stack([src_slot, src_owner]))
    mine, cells = prepare(entries, orbitals)
    mine, others, bit = gathered(entries, mine)
    lengths = [EDGE * HALO] * 2 + [len(CORNER_LOW)] * 2
    modes, tails = sines(mine)
    packed = pl.pallas_call(
        functools.partial(messages_kernel, bit),
        out_shape=[
            jax.ShapeDtypeStruct((length, ROWS, LANES), jnp.bfloat16)
            for length in [tiles(len(CORNER_LOW)) + 1] + [tiles(length) for length in lengths]
        ],
        in_specs=[pl.BlockSpec(memory_space=pl.ANY)] + [VMEM] * (3 + len(others)),
        out_specs=[VMEM] * 5,
        compiler_params=SMALL,
        name="messages",
    )(modes, entries, cells, mine, *others)
    return cells, packed, modes, tails


def across_x(tiles, used):
    if lax.axis_size("sx") == 2:
        return lax.ppermute(tiles, "sx", ring("sx", 1))
    half = used // 2
    low = lax.ppermute(tiles[:half], "sx", ring("sx", -1))
    return jnp.concatenate([low, lax.ppermute(tiles[half:used], "sx", ring("sx", 1))], axis=0)


def across_corner(cells, step_y):
    both = ("sx", "sy")
    if lax.axis_size("sx") == 2:
        return lax.ppermute(cells, both, diagonal(1, step_y))
    end = 2 * SPLIT
    back, ahead = (
        lax.ppermute(jnp.concatenate([part, cells[end:]]), both, diagonal(step_x, step_y))
        for part, step_x in ((cells[:SPLIT], -1), (cells[SPLIT:end], 1))
    )
    rows = jnp.concatenate([back[SPLIT:, :SPLIT], ahead[SPLIT:, SPLIT:]], axis=1)
    return jnp.concatenate([back[:SPLIT], ahead[:SPLIT], rows], axis=0)


def exchange(cells, sources, last, first, corner_low, corner_high):
    beside = (cells, across_x(cells, cells.shape[0]))
    rows = (sources, across_x(sources, EDGE * EDGE // ROWS))
    below = lax.ppermute(last, "sy", ring("sy", 1))
    above = lax.ppermute(first, "sy", ring("sy", -1))
    low, high = across_corner(corner_low, 1), across_corner(corner_high, -1)
    return beside, rows, (below, above, low, high)


def place_of(x, y):
    row, core_x = (x - HALO) % EDGE, HALO <= x < HALO + EDGE
    if HALO <= y < HALO + EDGE:
        return (0 if core_x else 1), row * EDGE + y - HALO
    if y < HALO:
        return (2, row * HALO + y) if core_x else (4, CORNER_LOW.index((row, y + EDGE - HALO)))
    y = y - HALO - EDGE
    return (3, row * HALO + y) if core_x else (5, CORNER_HIGH.index((row, y)))


def reach(x, y):
    out_x = max(HALO - x, x - (HALO + EDGE - 1), 0)
    out_y = max(HALO - y, y - (HALO + EDGE - 1), 0)
    return out_x + out_y


def sines_kernel(after, out, tails):
    shape = (LANES, LANES)
    row, col = (lax.broadcasted_iota(jnp.int32, shape, axis) for axis in range(2))
    product = ((row % NZ + 1) * (col % NZ + 1)).astype(jnp.float32)
    period = 2.0 * (NZ + 1)
    turn = product - period * jnp.floor((product + 0.5) / period)
    value = math.sqrt(2.0 / (NZ + 1)) * jnp.sin(turn * (math.pi / (NZ + 1)))
    value = jnp.where(row // NZ == col // NZ, value, 0.0)
    high = value.astype(jnp.bfloat16)
    low = (value - high.astype(jnp.float32)).astype(jnp.bfloat16)
    for first in (0, LANES):
        out[pl.ds(first, LANES), pl.ds(0, LANES)] = high
        out[pl.ds(first, LANES), pl.ds(LANES, LANES)] = low
    for step, tail in enumerate(z_tails()):
        tails[step] = tail


def sines(after):
    return pl.pallas_call(
        sines_kernel,
        out_shape=[
            jax.ShapeDtypeStruct((2 * LANES, 2 * LANES), jnp.bfloat16),
            jax.ShapeDtypeStruct((DEGREE, SUB, LANES), jnp.float32),
        ],
        in_specs=[pl.BlockSpec(memory_space=pl.ANY)],
        out_specs=[VMEM] * 2,
        compiler_params=SMALL,
        cost_estimate=pl.CostEstimate(flops=0, bytes_accessed=2 * 2**20, transcendentals=0),
        name="sines",
    )(after)


def z_tails():
    lane = lax.broadcasted_iota(jnp.int32, (SUB, LANES), 1) % NZ
    value = 2.0 * jnp.cos((lane + 1).astype(jnp.float32) * (math.pi / (NZ + 1)))
    p0, p1, p2, p3, p4 = power_coeffs()
    a3, a2, a1, a0 = p3 / p4, p2 / p4, p1 / p4, p0 / p4
    return (
        4.0 * value + a3,
        (6.0 * value + 3.0 * a3) * value + a2,
        ((4.0 * value + 3.0 * a3) * value + 2.0 * a2) * value + a1,
        (((value + a3) * value + a2) * value + a1) * value + a0,
    )


SIZE = 2 * HALO + EDGE


def within(radius):
    return [[y for y in range(SIZE) if reach(x, y) <= radius] for x in range(SIZE)]


CORE = [(x, y) for x in range(HALO, HALO + EDGE) for y in range(HALO, HALO + EDGE)]


def all_rows(refs, rows):
    count = rows.shape[0]
    shape = (LANES, count * LANES)
    lane = lax.broadcasted_iota(jnp.int32, shape, 1)
    line = lax.broadcasted_iota(jnp.int32, shape, 0)
    repeat = (line == lane // LANES * NZ + lane % NZ).astype(jnp.bfloat16)
    packed = [ref[...].reshape(-1, LANES) for ref in refs]
    firsts = [sum(part.shape[0] for part in packed[:at]) for at in range(len(packed))]
    packed = jnp.concatenate(packed, axis=0)
    spread = jnp.dot(packed, repeat, preferred_element_type=jnp.float32)
    for place in range(count):
        rows[place, : packed.shape[0], :] = spread[:, place * LANES : (place + 1) * LANES]
    return firsts


def keep(parts, at, value):
    high = value.astype(jnp.bfloat16)
    low = (value - high.astype(jnp.float32)).astype(jnp.bfloat16)
    parts[at, :, :LANES] = high
    parts[at, :, LANES:] = low


def turned(parts, first, end, modes):
    cells = end - first
    rows = parts[first:end].reshape(cells * ROWS, 2 * LANES)
    both = jnp.dot(rows, modes[...], preferred_element_type=jnp.float32)
    return (both[:, :LANES] + both[:, LANES:]).reshape(cells, ROWS, LANES)


def densities(refs, sources, rows, parts, modes, hat):
    count = hat.shape[0]
    firsts = all_rows(sources, rows)
    cells = [
        (ref, at, first + at)
        for ref, first in zip(refs, firsts)
        for at in range(ref.shape[0])
    ]
    pieces = -(-len(cells) // 48)
    for piece in range(pieces):
        start, end = (len(cells) * at // pieces for at in (piece, piece + 1))
        for number in range(start, end):
            ref, at, row = cells[number]
            value = ref[at].astype(jnp.float32)
            for place in range(count):
                other = jnp.broadcast_to(rows[place, pl.ds(row, 1), :], (ROWS, LANES))
                keep(parts.at[place], number, value * other)
        for place in range(count):
            hat[place, start:end] = turned(parts.at[place], start, end, modes)


def early(step):
    cells = [
        (x, y)
        for x in range(1 + step, SIZE - 1 - step)
        for y in range(HALO + 1 + step, HALO + EDGE - 1 - step)
    ]
    return {cell: at for at, cell in enumerate(cells)}


EARLY = [early(step) for step in range(DEGREE - 1)]


def one_step(targets, old, tail, density, put):
    pairs = targets | {(x - 1, y - 1) for x, y in targets}
    wanted = {(x + 1, y) for x, y in pairs} | {(x, y + 1) for x, y in pairs}
    loaded, summed = {}, {}
    rows = sorted({x for x, _ in pairs})
    for x in rows:
        for cell in sorted(cell for cell in wanted if cell[0] in (x, x + 1)):
            if cell not in loaded:
                loaded[cell] = old(*cell)
        for y in range(SIZE):
            if (x, y) in pairs:
                summed[x, y] = loaded[x + 1, y] + loaded[x, y + 1]
            if (x, y) in targets:
                here = loaded.get((x, y)) if old is density else None
                here = density(x, y) if here is None else here
                put(x, y, summed[x, y] + summed[x - 1, y - 1] + tail[...] * here)


def modes_kernel(own, across, own_sources, sources, modes, tails, hat, own_rows, *refs):
    stages, (rows, parts) = refs[: DEGREE - 1], refs[DEGREE - 1 :]
    used = pl.ds(0, EDGE * EDGE // ROWS)
    sources = (own_sources.at[used], sources.at[used])
    densities((own, across), sources, rows, parts, modes, hat)
    own_rows[...] = rows[:, : own_rows.shape[1], :] * (-power_coeffs()[-1])
    for place in range(hat.shape[0]):
        for half in range(ROWS // SUB):
            part = pl.ds(half * SUB, SUB)

            def start(x, y, place=place, part=part):
                which, at = place_of(x, y)
                return hat[place, which * len(CORE) + at, part, :]

            old = start
            for step, stage in enumerate(stages):

                def load(x, y, place=place, part=part, stage=stage, step=step):
                    return stage[place, EARLY[step][x, y], part, :]

                def store(x, y, value, place=place, part=part, stage=stage, step=step):
                    stage[place, EARLY[step][x, y], part, :] = value

                one_step(set(EARLY[step]), old, tails.at[step], start, store)
                old = load


def modes_of(beside, sources, modes, tails, count):
    cells = 2 * len(CORE)
    lengths = [cells] + [len(stage) for stage in EARLY]
    shapes = [(count, length, ROWS, LANES) for length in lengths]
    shapes.insert(1, (count, len(CORE), LANES))
    return pl.pallas_call(
        modes_kernel,
        out_shape=[jax.ShapeDtypeStruct(shape, jnp.float32) for shape in shapes],
        in_specs=[VMEM] * 6,
        out_specs=[VMEM] * len(shapes),
        scratch_shapes=[
            pltpu.VMEM((count, cells, LANES), jnp.float32),
            pltpu.VMEM((count, cells, ROWS, 2 * LANES), jnp.bfloat16),
        ],
        compiler_params=pltpu.CompilerParams(vmem_limit_bytes=20 * 2**20),
        cost_estimate=pl.CostEstimate(flops=0, bytes_accessed=6 * 2**20, transcendentals=0),
        name="modes",
    )(*beside, *sources, modes, tails)


def fields_kernel(beside, own_rows, *refs):
    stages, (below, above, low, high, modes, tails, out) = (
        refs[: DEGREE - 1],
        refs[DEGREE - 1 :][:7],
    )
    rows, parts, back, hat, work_a, work_b, last, acc, held, sems = refs[DEGREE + 6 :]
    count = beside.shape[0]
    pitch = ROWS + 1
    later = (below, above, low, high)
    offset = [0]
    for ref in later:
        offset.append(offset[-1] + spots_of(ref.shape[0]))
    cells = [ref.at[pl.ds(0, spots_of(ref.shape[0]))] for ref in later]
    sources = [
        ref.at[pl.ds(spots_of(ref.shape[0]), ref.shape[0] - spots_of(ref.shape[0]))] for ref in later
    ]
    densities(cells, sources, rows, parts, modes, hat)

    def steps(place, half):
        part = pl.ds(half * SUB, SUB)

        def start(x, y):
            which, at = place_of(x, y)
            if which < 2:
                return beside[place, which * len(CORE) + at, part, :]
            return hat[place, offset[which - 2] + at, part, :]

        old = start
        for step in range(DEGREE):
            new = (work_a, work_b, work_a, None)[step]
            ready = EARLY[step] if step < DEGREE - 1 else {}

            def load(x, y, new=new, step=step, ready=ready):
                if (x, y) in ready:
                    return stages[step][place, ready[x, y], part, :]
                return new[x, y]

            def store(x, y, value, new=new):
                if new is None:
                    last[place, CORE.index((x, y)), part, :] = value
                else:
                    new[x, y] = value

            cells = {(x, y) for x in range(SIZE) for y in within(HALO - 1 - step)[x]}
            one_step(cells - set(ready), old, tails.at[step], start, store)
            old = load

    for place in range(count):
        for half in range(ROWS // SUB):
            steps(place, half)
    copies = []
    for first in range(0, EDGE, 2):
        spots = range(first * EDGE, (first + 2) * EDGE)
        for place in range(count):
            for at, spot in enumerate(spots):
                keep(back, place * len(spots) + at, last[place, spot])
        result = turned(back, 0, count * len(spots), modes)
        for at, spot in enumerate(spots):
            total = None
            for place in range(count):
                other = jnp.broadcast_to(own_rows[place, pl.ds(spot, 1), :], (ROWS, LANES))
                value = result[place * len(spots) + at] * other
                total = value if total is None else total + value
            acc[spot // EDGE, pl.ds(spot % EDGE * pitch, ROWS), :] = total
        for x in range(first, first + 2):
            for group in range(ROWS):
                tile = acc[x, pl.ds(group, EDGE, stride=pitch), :]
                held[x, :, pl.ds(group * LANES, LANES)] = tile
        rows_x = pl.ds(first, 2)
        copies.append(
            pltpu.make_async_copy(held.at[rows_x], out.at[rows_x], sems.at[first // 2])
        )
        copies[-1].start()
    for copy in copies:
        copy.wait()


def fields(beside, sources, later, modes, tails, count):
    beside, own_rows, *stages = modes_of(beside, sources, modes, tails, count)
    plane = pltpu.VMEM((SIZE, SIZE, SUB, LANES), jnp.float32)
    cells = sum(spots_of(array.shape[0]) for array in later)
    rows = ROWS * sum(array.shape[0] - spots_of(array.shape[0]) for array in later)
    shape = (EDGE, EDGE, ROWS * LANES)
    return pl.pallas_call(
        fields_kernel,
        out_shape=jax.ShapeDtypeStruct(shape, jnp.float32),
        in_specs=[VMEM] * (8 + len(stages)),
        out_specs=pl.BlockSpec(memory_space=pl.ANY),
        scratch_shapes=[
            pltpu.VMEM((count, rows, LANES), jnp.float32),
            pltpu.VMEM((count, cells, ROWS, 2 * LANES), jnp.bfloat16),
            pltpu.VMEM((count * 2 * EDGE, ROWS, 2 * LANES), jnp.bfloat16),
            pltpu.VMEM((count, cells, ROWS, LANES), jnp.float32),
            plane,
            plane,
            pltpu.VMEM((count, len(CORE), ROWS, LANES), jnp.float32),
            pltpu.VMEM((EDGE, EDGE * (ROWS + 1), LANES), jnp.float32),
            pltpu.VMEM(shape, jnp.float32),
            pltpu.SemaphoreType.DMA((EDGE // 2,)),
        ],
        compiler_params=pltpu.CompilerParams(vmem_limit_bytes=24 * 2**20),
        name="fields",
    )(beside, own_rows, *stages, *later, modes, tails)


def body(orbitals, src_owner, src_slot):
    cells, packed, modes, tails = messages(orbitals, src_owner, src_slot)
    return fields(*exchange(cells, *packed), modes, tails, src_slot.size)


def solution(mesh):
    in_specs = (P("sx", "sy", "orb"), P(), P())
    out_specs = P("sx", "sy", "orb")
    return jax.shard_map(body, mesh=mesh, in_specs=in_specs, out_specs=out_specs, check_vma=False)
```

```python
import functools
import math

import jax
import jax.numpy as jnp
from jax import lax
from jax.experimental import pallas as pl
from jax.experimental.pallas import tpu as pltpu
from jax.sharding import PartitionSpec as P

NZ = 32
LANES = 128
SUB = 8
ROWS = 16
DEGREE = 4
HALO = DEGREE
EDGE = 8

CHEB = (
    1.021021021021021,
    -1.7357357357357357,
    1.4753753753753753,
    -1.254069069069069,
    1.0659587087087088,
)


def power_coeffs():
    c0, c1, c2, c3, c4 = CHEB
    return (
        c0 - c2 + c4,
        -(c1 - 3.0 * c3) / 6.0,
        (2.0 * c2 - 8.0 * c4) / 36.0,
        -4.0 * c3 / 216.0,
        8.0 * c4 / 1296.0,
    )


CORNER_LOW = tuple(
    (x, y)
    for x in range(EDGE)
    for y in range(EDGE - HALO, EDGE)
    if min(x + 1, EDGE - x) + EDGE - y <= DEGREE
)
CORNER_HIGH = tuple((x, EDGE - 1 - y) for x, y in CORNER_LOW)
SPLIT = len(CORNER_LOW) // 2


def ring(axis, step):
    count = lax.axis_size(axis)
    return [(i, (i + step) % count) for i in range(count)]


def diagonal(step_x, step_y):
    count_x, count_y = lax.axis_size("sx"), lax.axis_size("sy")
    return [
        (i * count_y + j, (i + step_x) % count_x * count_y + (j + step_y) % count_y)
        for i in range(count_x)
        for j in range(count_y)
    ]


VMEM = pl.BlockSpec(memory_space=pltpu.VMEM)
SMALL = pltpu.CompilerParams(vmem_limit_bytes=8 * 2**20)


def spread_out(values):
    return lax.broadcast_in_dim(
        values, values.shape + (ROWS, LANES), tuple(range(values.ndim))
    )


def by_seat(entries):
    rounds, places, rows, lanes = entries.shape
    seat = lax.broadcasted_iota(jnp.int32, (rows, lanes), 1) // NZ
    value = entries[0, 0]
    for index in range(1, rounds * places):
        value = jnp.where(seat == index, entries[index // places, index % places], value)
    return value


def prepare_kernel(entries, orbitals, out, cells, scratch):
    per_tile = LANES // NZ
    slot = by_seat(entries[0])[:EDGE]
    lane = lax.broadcasted_iota(jnp.int32, (EDGE, LANES), 1)
    group, turn = slot // per_tile, (lane // NZ - slot % per_tile + per_tile) % per_tile
    asked = [pltpu.roll(group, LANES - step * NZ, 1) if step else group for step in range(per_tile)]
    found = [[jnp.zeros((EDGE, LANES), jnp.float32)] * EDGE for _ in range(per_tile)]
    for number in range(ROWS):
        lanes = pl.ds(number * LANES, LANES)
        tiles = [orbitals[row, :, lanes].astype(jnp.float32) for row in range(EDGE)]
        for step in range(per_tile):
            here = asked[step] == number
            found[step] = [jnp.where(here, tile, old) for tile, old in zip(tiles, found[step])]
    rows = []
    for row in range(EDGE):
        packed = found[0][row]
        for step in range(1, per_tile):
            packed = jnp.where(turn == step, pltpu.roll(found[step][row], step * NZ, 1), packed)
        rows.append(packed)
    for tile in range(EDGE // 2):
        out[tile] = jnp.concatenate(rows[2 * tile : 2 * tile + 2], axis=0).astype(jnp.bfloat16)
    for row in range(EDGE):
        for group in range(ROWS):
            tile = orbitals[row, :, pl.ds(group * LANES, LANES)].astype(jnp.float32)
            scratch[row, pl.ds(group, EDGE, stride=ROWS + 1), :] = tile
    for row in range(EDGE):
        for y in range(EDGE):
            tile = scratch[row, pl.ds(y * (ROWS + 1), ROWS), :]
            cells[row * EDGE + y] = tile.astype(jnp.bfloat16)


def prepare(entries, orbitals):
    lengths = (EDGE * EDGE // ROWS, EDGE * EDGE)
    return pl.pallas_call(
        prepare_kernel,
        out_shape=[jax.ShapeDtypeStruct((length, ROWS, LANES), jnp.bfloat16) for length in lengths],
        in_specs=[VMEM] * 2,
        out_specs=[VMEM] * 2,
        scratch_shapes=[pltpu.VMEM((EDGE, EDGE * (ROWS + 1), LANES), jnp.float32)],
        compiler_params=SMALL,
        name="prepare",
    )(entries, orbitals)


def chosen(entries, mine, others, bit):
    owner, me = by_seat(entries[1]), lax.axis_index("orb")
    count = lax.axis_size("orb")
    picked = []
    for tile in range(mine.shape[0]):
        value = mine[tile].astype(jnp.float32)
        for step, other in enumerate(others, 1):
            if bit is None:
                here = owner == lax.rem(me + count - step, count)
            else:
                here = (owner >> bit & 1) != (me >> bit & 1)
            value = jnp.where(here, other[tile].astype(jnp.float32), value)
        picked.append(value)
    return picked


def nearer_kernel(bit, entries, mine, other, out):
    for tile, value in enumerate(chosen(entries, mine, [other], bit)):
        out[tile] = value.astype(jnp.bfloat16)


def gathered(entries, mine):
    count = lax.axis_size("orb")
    if count & (count - 1):
        others = [lax.ppermute(mine, "orb", ring("orb", step)) for step in range(1, count)]
        return mine, others, None
    bits = count.bit_length() - 1
    for bit in range(bits):
        other = lax.ppermute(mine, "orb", [(i, i ^ 1 << bit) for i in range(count)])
        if bit == bits - 1:
            return mine, [other], bit
        mine = pl.pallas_call(
            functools.partial(nearer_kernel, bit),
            out_shape=jax.ShapeDtypeStruct(mine.shape, mine.dtype),
            in_specs=[VMEM] * 3,
            out_specs=VMEM,
            compiler_params=SMALL,
            name="nearer",
        )(entries, mine, other)
    return mine, [], None


def pack(ref, spots, cells, picked):
    runs = []
    for at, (x, y) in enumerate(spots):
        ref[at] = cells[x * EDGE + y]
        if runs and runs[-1][0] == x and runs[-1][2] == y:
            runs[-1][2] = y + 1
        else:
            runs.append([x, y, y + 1])
    parts = [
        picked[x * EDGE // ROWS][x * EDGE % ROWS + low : x * EDGE % ROWS + high]
        for x, low, high in runs
    ]
    used = len(spots)
    if used % ROWS:
        parts.append(jnp.zeros((ROWS - used % ROWS, LANES), jnp.float32))
    rows = jnp.concatenate(parts, axis=0).astype(jnp.bfloat16)
    for tile in range(rows.shape[0] // ROWS):
        ref[used + tile] = rows[tile * ROWS : (tile + 1) * ROWS]


def messages_kernel(bit, before, entries, cells, mine, *refs):
    others, (sources, last, first, corner) = refs[:-4], refs[-4:]
    picked = chosen(entries, mine, others, bit)
    for tile in range(sources.shape[0]):
        rows = picked[tile] if tile < len(picked) else jnp.zeros((ROWS, LANES), jnp.float32)
        sources[tile] = rows.astype(jnp.bfloat16)
    pack(last, [(x, y) for x in range(EDGE) for y in range(EDGE - HALO, EDGE)], cells, picked)
    pack(first, [(x, y) for x in range(EDGE) for y in range(HALO)], cells, picked)
    pack(corner, CORNER_LOW, cells, picked)


def corner_kernel(before, cells, sources, corner):
    picked = [sources[tile].astype(jnp.float32) for tile in range(EDGE * EDGE // ROWS)]
    pack(corner, CORNER_HIGH, cells, picked)


def tiles(spots):
    return spots + -(-spots // ROWS)


def spots_of(length):
    return length * ROWS // (ROWS + 1)


def messages(orbitals, src_owner, src_slot):
    entries = spread_out(jnp.stack([src_slot, src_owner]))
    mine, cells = prepare(entries, orbitals)
    mine, others, bit = gathered(entries, mine)
    modes, tails = sines(mine)
    lengths = [tiles(len(CORNER_LOW)) + 1] + [tiles(EDGE * HALO)] * 2 + [tiles(len(CORNER_LOW))]
    any_space = pl.BlockSpec(memory_space=pl.ANY)
    sources, last, first, low = pl.pallas_call(
        functools.partial(messages_kernel, bit),
        out_shape=[jax.ShapeDtypeStruct((length, ROWS, LANES), jnp.bfloat16) for length in lengths],
        in_specs=[any_space] + [VMEM] * (3 + len(others)),
        out_specs=[VMEM] * 4,
        compiler_params=SMALL,
        name="messages",
    )(modes, entries, cells, mine, *others)
    beside = (cells, across_x(cells, cells.shape[0]))
    high = pl.pallas_call(
        corner_kernel,
        out_shape=jax.ShapeDtypeStruct((tiles(len(CORNER_HIGH)), ROWS, LANES), jnp.bfloat16),
        in_specs=[any_space] + [VMEM] * 2,
        out_specs=VMEM,
        compiler_params=SMALL,
        name="corner",
    )(beside[1], cells, sources)
    return beside, (sources, last, first, low, high), modes, tails


def across_x(tiles, used):
    if lax.axis_size("sx") == 2:
        return lax.ppermute(tiles, "sx", ring("sx", 1))
    half = used // 2
    low = lax.ppermute(tiles[:half], "sx", ring("sx", -1))
    return jnp.concatenate([low, lax.ppermute(tiles[half:used], "sx", ring("sx", 1))], axis=0)


def across_corner(cells, step_y):
    both = ("sx", "sy")
    if lax.axis_size("sx") == 2:
        return lax.ppermute(cells, both, diagonal(1, step_y))
    end = 2 * SPLIT
    back, ahead = (
        lax.ppermute(jnp.concatenate([part, cells[end:]]), both, diagonal(step_x, step_y))
        for part, step_x in ((cells[:SPLIT], -1), (cells[SPLIT:end], 1))
    )
    rows = jnp.concatenate([back[SPLIT:, :SPLIT], ahead[SPLIT:, SPLIT:]], axis=1)
    return jnp.concatenate([back[:SPLIT], ahead[:SPLIT], rows], axis=0)


def exchange(sources, last, first, corner_low, corner_high):
    rows = (sources, across_x(sources, EDGE * EDGE // ROWS))
    below = lax.ppermute(last, "sy", ring("sy", 1))
    above = lax.ppermute(first, "sy", ring("sy", -1))
    low, high = across_corner(corner_low, 1), across_corner(corner_high, -1)
    return rows, (below, above, low, high)


def place_of(x, y):
    row, core_x = (x - HALO) % EDGE, HALO <= x < HALO + EDGE
    if HALO <= y < HALO + EDGE:
        return (0 if core_x else 1), row * EDGE + y - HALO
    if y < HALO:
        return (2, row * HALO + y) if core_x else (4, CORNER_LOW.index((row, y + EDGE - HALO)))
    y = y - HALO - EDGE
    return (3, row * HALO + y) if core_x else (5, CORNER_HIGH.index((row, y)))


def reach(x, y):
    out_x = max(HALO - x, x - (HALO + EDGE - 1), 0)
    out_y = max(HALO - y, y - (HALO + EDGE - 1), 0)
    return out_x + out_y


def sines_kernel(after, out, tails):
    shape = (LANES, LANES)
    row, col = (lax.broadcasted_iota(jnp.int32, shape, axis) for axis in range(2))
    product = ((row % NZ + 1) * (col % NZ + 1)).astype(jnp.float32)
    period = 2.0 * (NZ + 1)
    turn = product - period * jnp.floor((product + 0.5) / period)
    value = math.sqrt(2.0 / (NZ + 1)) * jnp.sin(turn * (math.pi / (NZ + 1)))
    value = jnp.where(row // NZ == col // NZ, value, 0.0)
    high = value.astype(jnp.bfloat16)
    low = (value - high.astype(jnp.float32)).astype(jnp.bfloat16)
    for first in (0, LANES):
        out[pl.ds(first, LANES), pl.ds(0, LANES)] = high
        out[pl.ds(first, LANES), pl.ds(LANES, LANES)] = low
    for step, tail in enumerate(z_tails()):
        tails[step] = tail


def sines(after):
    return pl.pallas_call(
        sines_kernel,
        out_shape=[
            jax.ShapeDtypeStruct((2 * LANES, 2 * LANES), jnp.bfloat16),
            jax.ShapeDtypeStruct((DEGREE, SUB, LANES), jnp.float32),
        ],
        in_specs=[pl.BlockSpec(memory_space=pl.ANY)],
        out_specs=[VMEM] * 2,
        compiler_params=SMALL,
        cost_estimate=pl.CostEstimate(flops=0, bytes_accessed=2 * 2**20, transcendentals=0),
        name="sines",
    )(after)


def z_tails():
    lane = lax.broadcasted_iota(jnp.int32, (SUB, LANES), 1) % NZ
    value = 2.0 * jnp.cos((lane + 1).astype(jnp.float32) * (math.pi / (NZ + 1)))
    p0, p1, p2, p3, p4 = power_coeffs()
    a3, a2, a1, a0 = p3 / p4, p2 / p4, p1 / p4, p0 / p4
    return (
        4.0 * value + a3,
        (6.0 * value + 3.0 * a3) * value + a2,
        ((4.0 * value + 3.0 * a3) * value + 2.0 * a2) * value + a1,
        (((value + a3) * value + a2) * value + a1) * value + a0,
    )


SIZE = 2 * HALO + EDGE


def within(radius):
    return [[y for y in range(SIZE) if reach(x, y) <= radius] for x in range(SIZE)]


CORE = [(x, y) for x in range(HALO, HALO + EDGE) for y in range(HALO, HALO + EDGE)]


def all_rows(refs, rows):
    count = rows.shape[0]
    shape = (LANES, count * LANES)
    lane = lax.broadcasted_iota(jnp.int32, shape, 1)
    line = lax.broadcasted_iota(jnp.int32, shape, 0)
    repeat = (line == lane // LANES * NZ + lane % NZ).astype(jnp.bfloat16)
    packed = [ref[...].reshape(-1, LANES) for ref in refs]
    firsts = [sum(part.shape[0] for part in packed[:at]) for at in range(len(packed))]
    packed = jnp.concatenate(packed, axis=0)
    spread = jnp.dot(packed, repeat, preferred_element_type=jnp.float32)
    for place in range(count):
        rows[place, : packed.shape[0], :] = spread[:, place * LANES : (place + 1) * LANES]
    return firsts


def keep(parts, at, value):
    high = value.astype(jnp.bfloat16)
    low = (value - high.astype(jnp.float32)).astype(jnp.bfloat16)
    parts[at, :, :LANES] = high
    parts[at, :, LANES:] = low


def turned(parts, first, end, modes):
    cells = end - first
    rows = parts[first:end].reshape(cells * ROWS, 2 * LANES)
    both = jnp.dot(rows, modes[...], preferred_element_type=jnp.float32)
    return (both[:, :LANES] + both[:, LANES:]).reshape(cells, ROWS, LANES)


def densities(refs, sources, rows, parts, modes, hat):
    count = hat.shape[0]
    firsts = all_rows(sources, rows)
    cells = [
        (ref, at, first + at)
        for ref, first in zip(refs, firsts)
        for at in range(ref.shape[0])
    ]
    pieces = -(-len(cells) // 48)
    for piece in range(pieces):
        start, end = (len(cells) * at // pieces for at in (piece, piece + 1))
        for number in range(start, end):
            ref, at, row = cells[number]
            value = ref[at].astype(jnp.float32)
            for place in range(count):
                other = jnp.broadcast_to(rows[place, pl.ds(row, 1), :], (ROWS, LANES))
                keep(parts.at[place], number, value * other)
        for place in range(count):
            hat[place, start:end] = turned(parts.at[place], start, end, modes)


def early(step):
    cells = [
        (x, y)
        for x in range(1 + step, SIZE - 1 - step)
        for y in range(HALO + 1 + step, HALO + EDGE - 1 - step)
    ]
    return {cell: at for at, cell in enumerate(cells)}


EARLY = [early(step) for step in range(DEGREE - 1)]


def one_step(targets, old, tail, density, put):
    pairs = targets | {(x - 1, y - 1) for x, y in targets}
    wanted = {(x + 1, y) for x, y in pairs} | {(x, y + 1) for x, y in pairs}
    loaded, summed = {}, {}
    rows = sorted({x for x, _ in pairs})
    for x in rows:
        for cell in sorted(cell for cell in wanted if cell[0] in (x, x + 1)):
            if cell not in loaded:
                loaded[cell] = old(*cell)
        for y in range(SIZE):
            if (x, y) in pairs:
                summed[x, y] = loaded[x + 1, y] + loaded[x, y + 1]
            if (x, y) in targets:
                here = loaded.get((x, y)) if old is density else None
                here = density(x, y) if here is None else here
                put(x, y, summed[x, y] + summed[x - 1, y - 1] + tail[...] * here)


def modes_kernel(own, across, own_sources, sources, modes, tails, hat, own_rows, *refs):
    stages, (rows, parts) = refs[: DEGREE - 1], refs[DEGREE - 1 :]
    used = pl.ds(0, EDGE * EDGE // ROWS)
    sources = (own_sources.at[used], sources.at[used])
    densities((own, across), sources, rows, parts, modes, hat)
    own_rows[...] = rows[:, : own_rows.shape[1], :] * (-power_coeffs()[-1])
    for place in range(hat.shape[0]):
        for half in range(ROWS // SUB):
            part = pl.ds(half * SUB, SUB)

            def start(x, y, place=place, part=part):
                which, at = place_of(x, y)
                return hat[place, which * len(CORE) + at, part, :]

            old = start
            for step, stage in enumerate(stages):

                def load(x, y, place=place, part=part, stage=stage, step=step):
                    return stage[place, EARLY[step][x, y], part, :]

                def store(x, y, value, place=place, part=part, stage=stage, step=step):
                    stage[place, EARLY[step][x, y], part, :] = value

                one_step(set(EARLY[step]), old, tails.at[step], start, store)
                old = load


def modes_of(beside, sources, modes, tails, count):
    cells = 2 * len(CORE)
    lengths = [cells] + [len(stage) for stage in EARLY]
    shapes = [(count, length, ROWS, LANES) for length in lengths]
    shapes.insert(1, (count, len(CORE), LANES))
    return pl.pallas_call(
        modes_kernel,
        out_shape=[jax.ShapeDtypeStruct(shape, jnp.float32) for shape in shapes],
        in_specs=[VMEM] * 6,
        out_specs=[VMEM] * len(shapes),
        scratch_shapes=[
            pltpu.VMEM((count, cells, LANES), jnp.float32),
            pltpu.VMEM((count, cells, ROWS, 2 * LANES), jnp.bfloat16),
        ],
        compiler_params=pltpu.CompilerParams(vmem_limit_bytes=20 * 2**20),
        cost_estimate=pl.CostEstimate(flops=0, bytes_accessed=6 * 2**20, transcendentals=0),
        name="modes",
    )(*beside, *sources, modes, tails)


def fields_kernel(beside, own_rows, *refs):
    stages, (below, above, low, high, modes, tails, out) = (
        refs[: DEGREE - 1],
        refs[DEGREE - 1 :][:7],
    )
    rows, parts, back, hat, work_a, work_b, last, acc, held, sems = refs[DEGREE + 6 :]
    count = beside.shape[0]
    pitch = ROWS + 1
    later = (below, above, low, high)
    offset = [0]
    for ref in later:
        offset.append(offset[-1] + spots_of(ref.shape[0]))
    cells = [ref.at[pl.ds(0, spots_of(ref.shape[0]))] for ref in later]
    sources = [
        ref.at[pl.ds(spots_of(ref.shape[0]), ref.shape[0] - spots_of(ref.shape[0]))] for ref in later
    ]
    densities(cells, sources, rows, parts, modes, hat)

    def steps(place, half):
        part = pl.ds(half * SUB, SUB)

        def start(x, y):
            which, at = place_of(x, y)
            if which < 2:
                return beside[place, which * len(CORE) + at, part, :]
            return hat[place, offset[which - 2] + at, part, :]

        old = start
        for step in range(DEGREE):
            new = (work_a, work_b, work_a, None)[step]
            ready = EARLY[step] if step < DEGREE - 1 else {}

            def load(x, y, new=new, step=step, ready=ready):
                if (x, y) in ready:
                    return stages[step][place, ready[x, y], part, :]
                return new[x, y]

            def store(x, y, value, new=new):
                if new is None:
                    last[place, CORE.index((x, y)), part, :] = value
                else:
                    new[x, y] = value

            cells = {(x, y) for x in range(SIZE) for y in within(HALO - 1 - step)[x]}
            one_step(cells - set(ready), old, tails.at[step], start, store)
            old = load

    for place in range(count):
        for half in range(ROWS // SUB):
            steps(place, half)
    copies = []
    for first in range(0, EDGE, 2):
        spots = range(first * EDGE, (first + 2) * EDGE)
        for place in range(count):
            for at, spot in enumerate(spots):
                keep(back, place * len(spots) + at, last[place, spot])
        result = turned(back, 0, count * len(spots), modes)
        for at, spot in enumerate(spots):
            total = None
            for place in range(count):
                other = jnp.broadcast_to(own_rows[place, pl.ds(spot, 1), :], (ROWS, LANES))
                value = result[place * len(spots) + at] * other
                total = value if total is None else total + value
            acc[spot // EDGE, pl.ds(spot % EDGE * pitch, ROWS), :] = total
        for x in range(first, first + 2):
            for group in range(ROWS):
                tile = acc[x, pl.ds(group, EDGE, stride=pitch), :]
                held[x, :, pl.ds(group * LANES, LANES)] = tile
        rows_x = pl.ds(first, 2)
        copies.append(
            pltpu.make_async_copy(held.at[rows_x], out.at[rows_x], sems.at[first // 2])
        )
        copies[-1].start()
    for copy in copies:
        copy.wait()


def fields(beside, sources, later, modes, tails, count):
    beside, own_rows, *stages = modes_of(beside, sources, modes, tails, count)
    plane = pltpu.VMEM((SIZE, SIZE, SUB, LANES), jnp.float32)
    cells = sum(spots_of(array.shape[0]) for array in later)
    rows = ROWS * sum(array.shape[0] - spots_of(array.shape[0]) for array in later)
    shape = (EDGE, EDGE, ROWS * LANES)
    return pl.pallas_call(
        fields_kernel,
        out_shape=jax.ShapeDtypeStruct(shape, jnp.float32),
        in_specs=[VMEM] * (8 + len(stages)),
        out_specs=pl.BlockSpec(memory_space=pl.ANY),
        scratch_shapes=[
            pltpu.VMEM((count, rows, LANES), jnp.float32),
            pltpu.VMEM((count, cells, ROWS, 2 * LANES), jnp.bfloat16),
            pltpu.VMEM((count * 2 * EDGE, ROWS, 2 * LANES), jnp.bfloat16),
            pltpu.VMEM((count, cells, ROWS, LANES), jnp.float32),
            plane,
            plane,
            pltpu.VMEM((count, len(CORE), ROWS, LANES), jnp.float32),
            pltpu.VMEM((EDGE, EDGE * (ROWS + 1), LANES), jnp.float32),
            pltpu.VMEM(shape, jnp.float32),
            pltpu.SemaphoreType.DMA((EDGE // 2,)),
        ],
        compiler_params=pltpu.CompilerParams(vmem_limit_bytes=24 * 2**20),
        name="fields",
    )(beside, own_rows, *stages, *later, modes, tails)


def body(orbitals, src_owner, src_slot):
    beside, packed, modes, tails = messages(orbitals, src_owner, src_slot)
    return fields(beside, *exchange(*packed), modes, tails, src_slot.size)


def solution(mesh):
    in_specs = (P("sx", "sy", "orb"), P(), P())
    out_specs = P("sx", "sy", "orb")
    return jax.shard_map(body, mesh=mesh, in_specs=in_specs, out_specs=out_specs, check_vma=False)
```
